256 devices in a mesh: seq: 64 (over z, y, core), tp: 4 (over x).
Axes of the slice: x: 4, y: 4, z: 8, core: 2. Of those that a mesh axis runs over, the one named last changes fastest.
Arguments:
- query: bfloat16 [53248, 2048], P('seq', 'tp'), may hold values from -200 to 200
- d_attended: bfloat16 [53248, 2048], P('seq', 'tp'), may hold values from -6 to 6
- encoded: bfloat16 [1024, 128, 896], P('seq', 'tp'), may hold values from -6 to 6
- key_weight: bfloat16 [896, 2048], replicated, may hold values from -0.1875 to 0.1875
- value_weight: bfloat16 [896, 2048], replicated, may hold values from -0.1875 to 0.1875
- nbr_shard: int32 [832, 2], P('seq'), may hold values from 0 to 63, all different within a row; in each aligned block of 13 rows (0 to 12, 13 to 25, ...) at most 2 rows name the same one
- nbr_row: int32 [832, 2], P('seq'), may hold values from 0 to 15
Outputs:
- attended: bfloat16 [53248, 2048], P('seq', 'tp')
- d_query: bfloat16 [53248, 2048], P('seq', 'tp')
- d_encoded: bfloat16 [1024, 128, 896], P('seq', 'tp')
The draws below stay inside these ranges and needn't reach their ends.
Inputs may be any that keep to these rules, and one draw needn't show every extreme that they name: `nbr_shard`: a span's 2 neighbours lie on different indices; among the 13 spans of one sequence no index is named more than 2 times, a bound that some block reaches.
All inputs are finite; a program needn't handle non-finite values.
Results may differ from the reference program's by a relative error of at most 0.017.
The reference program's roundings to bfloat16 on the way count: a program that leaves them out, or rounds other values in their place, can miss the bound.
Values may be sent and summed in bfloat16 or wider, within the bound.
No kernel may reach another device: no remote copies, remote signals or barrier semaphores. Data moves between devices by JAX's collectives and lax.ppermute only.
A program may use at most 192 MiB of HBM per device.

```python
import math
import jax
import jax.numpy as jnp
import numpy as np
from jax import lax

HEADS = 16
HD = 128
E_DIM = 896
SPAN = 64
NBR_LEN = 128
NBRS = 2
CH_DEV = 13
ENC_DEV = 16
TOK_DEV = 832
CAP = 2
TOKENS = 53248
SPANS = 832
ENC_ROWS = 1024
N_SEQ = 64


def draw_query(key, part):
    key = jax.random.fold_in(key, 11)
    first = jax.random.fold_in(key, 0)
    shape = (TOKENS, HEADS * HD)
    values = jnp.clip(jax.random.normal(first, shape, jnp.float32), -6.0, 6.0)
    return values.astype(jnp.bfloat16)


def draw_d_attended(key, part):
    key = jax.random.fold_in(key, 12)
    first = jax.random.fold_in(key, 0)
    shape = (TOKENS, HEADS * HD)
    values = jnp.clip(jax.random.normal(first, shape, jnp.float32), -6.0, 6.0)
    return values.astype(jnp.bfloat16)


def plant(values, rng, least, high):
    shape = values.shape
    spot = [jax.random.randint(jax.random.fold_in(rng, axis), (), 0, shape[axis]) for axis in range(len(shape))]
    values = values.at[tuple(spot)].set(least)
    longest = shape.index(max(shape))
    spot[longest] = (spot[longest] + 1) % shape[longest]
    return values.at[tuple(spot)].set(high)


def block_levels(own_key, shape, shards, low, high):
    gain, own = 1.0, jax.random.fold_in(own_key, 6)
    for position, shards_of in shards:
        heights = jnp.exp(jax.random.uniform(jax.random.fold_in(own, position), (shards_of,), jnp.float32, low / len(shards), high / len(shards)))
        gain = gain * jnp.repeat(heights, shape[position] // shards_of).reshape([-1 if axis == position else 1 for axis in range(len(shape))])
    return gain


def assign_block(rng, own, number, rows, amount, top, bound, slope):
    sequence = jax.random.permutation(rng, amount)
    heavy_load, ordinary = load_shares(amount, rows * top, bound, slope, True), load_shares(amount, rows * top, bound, slope, False)
    places = jnp.arange(amount)

    def named(sizes, offset_by):
        used = int((sizes > 0).sum())
        fixed = max(1, used // 4)
        moved = fixed + (places - fixed + offset_by * (used - fixed)) % max(1, amount - fixed)
        return jnp.zeros((amount,), jnp.int32).at[sequence[jnp.where(places < fixed, places, moved)]].set(jnp.asarray(sizes, jnp.int32))

    sizes = jnp.where(number % 4 == 0, named(heavy_load, number // 4), named(ordinary, number - number // 4 - 1))
    mixed = jax.random.permutation(jax.random.fold_in(own, 3), amount)
    donor, taker = mixed[0:amount // 2 * 2:2], mixed[1:amount // 2 * 2:2]
    room = jnp.minimum(sizes[donor] - 1, bound - sizes[taker]) // 2
    room = jnp.where((donor == sequence[0]) | (taker == sequence[0]) | (sizes[taker] == 0), 0, jnp.maximum(room, 0))
    moved = jax.random.randint(jax.random.fold_in(own, 4), (amount // 2,), 0, 1 << 20) % (room + 1)
    sizes = sizes.at[donor].add(-moved).at[taker].add(moved)
    members = jnp.searchsorted(jnp.cumsum(sizes), jnp.arange(rows * top), side="right").astype(jnp.int32)
    grid = members.reshape(top, rows).T
    grid = grid[jax.random.permutation(jax.random.fold_in(own, 1), rows)]
    offset_by = jax.random.randint(jax.random.fold_in(own, 2), (rows, 1), 0, top)
    return jnp.take_along_axis(grid, (jnp.arange(top)[None, :] + offset_by) % top, axis=1)


def load_shares(amount, total, limit, slope, full):
    portions = [(1 << 20) // math.isqrt(rank ** slope) + 1 for rank in range(1, amount + 1)]
    largest = limit if full else min(limit, max(-(-total // amount), total * portions[0] // sum(portions)))
    least = 1 if total - largest >= amount - 1 else 0
    given, spare = [largest] + [least] * (amount - 1), total - largest - least * (amount - 1)
    while spare > 0:
        free = [i for i in range(1, amount) if given[i] < largest] or [i for i in range(1, amount) if given[i] < limit]
        pool, budget = sum([portions[i] for i in free]), spare
        for i in free:
            more = min(limit - given[i], max(1, budget * portions[i] // pool), spare)
            given[i] = given[i] + more
            spare = spare - more
    return np.array(given)


def noise(key, dims, deviation, limit, shards=(), kind=jnp.bfloat16):
    values = jax.random.normal(key, dims, jnp.float32) * deviation
    if len(shards) > 0:
        values = block_levels(key, dims, shards, -0.22, 0.18) * values
    return jnp.clip(values, min=-limit, max=limit).astype(kind)


def setup_inputs(seed: int = 0) -> dict:
    splits = jax.random.split(jax.random.key(seed), 8)
    query = draw_query(jax.random.fold_in(splits[7], 71), 0)
    d_attended = draw_d_attended(jax.random.fold_in(splits[7], 71), 0)
    encoded = noise(splits[2], (ENC_ROWS, NBR_LEN, E_DIM), 1.0, 6.0, ((0, 64), (1, 4)))
    key_weight = noise(splits[3], (E_DIM, HEADS * HD), E_DIM ** -0.5, 0.1875)
    value_weight = noise(splits[4], (E_DIM, HEADS * HD), E_DIM ** -0.5, 0.1875)
    nbr_shard_keys = jax.random.split(jax.random.fold_in(splits[5], 1), SPANS // CH_DEV)
    nbr_shard_turns = jax.random.permutation(jax.random.fold_in(splits[5], 3), SPANS // CH_DEV)
    nbr_shard = jax.vmap(lambda own, number: assign_block(jax.random.fold_in(splits[5], 2), own, number, CH_DEV, N_SEQ, NBRS, CAP, 2))(nbr_shard_keys, nbr_shard_turns).reshape((SPANS, NBRS))
    nbr_row = plant(jax.random.randint(splits[6], (SPANS, NBRS), 0, ENC_DEV), jax.random.fold_in(splits[6], 1), 0, ENC_DEV - 1).astype(jnp.int32)
    return {"query": query, "d_attended": d_attended, "encoded": encoded, "key_weight": key_weight, "value_weight": value_weight, "nbr_shard": nbr_shard, "nbr_row": nbr_row}


def shift_rows(tokens_in):
    padding = jnp.zeros((SPAN - 1, tokens_in.shape[1]), tokens_in.dtype)
    return jnp.concatenate([tokens_in[SPAN - 1:], padding], 0)


def unshift_rows(tokens_in):
    padding = jnp.zeros((SPAN - 1, tokens_in.shape[1]), tokens_in.dtype)
    return jnp.concatenate([padding, tokens_in[:tokens_in.shape[0] - SPAN + 1]], 0)


def attend(shifted, grad_shift, key_rows, value_rows):
    factor = HD ** -0.5
    f32 = jnp.float32
    scores = jnp.einsum("cqhd,ckhd->chqk", shifted.astype(f32), key_rows.astype(f32)) * factor
    row_max = jnp.max(scores, axis=-1, keepdims=True)
    weights = jnp.exp(scores - row_max)
    probs = weights / jnp.sum(weights, axis=-1, keepdims=True)
    probs_b = probs.astype(jnp.bfloat16)
    blended = jnp.einsum("chqk,ckhd->cqhd", probs_b.astype(f32), value_rows.astype(f32))
    grad_probs = jnp.einsum("cqhd,ckhd->chqk", grad_shift.astype(f32), value_rows.astype(f32))
    inner = jnp.sum(probs * grad_probs, axis=-1, keepdims=True)
    grad_scores = (probs * (grad_probs - inner) * factor).astype(jnp.bfloat16)
    grad_shifted = jnp.einsum("chqk,ckhd->cqhd", grad_scores.astype(f32), key_rows.astype(f32))
    grad_keys = jnp.einsum("chqk,cqhd->ckhd", grad_scores.astype(f32), shifted.astype(f32)).astype(jnp.bfloat16)
    grad_values = jnp.einsum("chqk,cqhd->ckhd", probs_b.astype(f32), grad_shift.astype(f32)).astype(jnp.bfloat16)
    return blended, grad_shifted, grad_keys, grad_values


def reference(query, d_attended, encoded, key_weight, value_weight, nbr_shard, nbr_row):
    width = HEADS * HD
    picks = (nbr_shard * ENC_DEV + nbr_row).astype(jnp.int32)
    query_seq = query.reshape(N_SEQ, TOK_DEV, width)
    grad_seq = d_attended.reshape(N_SEQ, TOK_DEV, width)
    picks_seq = picks.reshape(N_SEQ, CH_DEV * NBRS)

    def one_sequence(store_grad, items):
        query_rows, grad_rows, chosen = items
        fetched = jnp.take(encoded, chosen, axis=0).reshape(CH_DEV * NBRS * NBR_LEN, E_DIM)
        key_rows = jnp.dot(fetched, key_weight, preferred_element_type=jnp.float32).astype(jnp.bfloat16)
        value_rows = jnp.dot(fetched, value_weight, preferred_element_type=jnp.float32).astype(jnp.bfloat16)
        key_rows = key_rows.reshape(CH_DEV, NBRS * NBR_LEN, HEADS, HD)
        value_rows = value_rows.reshape(CH_DEV, NBRS * NBR_LEN, HEADS, HD)
        shifted = shift_rows(query_rows).reshape(CH_DEV, SPAN, HEADS, HD)
        grad_shift = shift_rows(grad_rows).reshape(CH_DEV, SPAN, HEADS, HD)
        blended, grad_shifted, grad_keys, grad_values = attend(shifted, grad_shift, key_rows, value_rows)
        attended = unshift_rows(blended.reshape(TOK_DEV, width)).astype(jnp.bfloat16)
        d_query = unshift_rows(grad_shifted.reshape(TOK_DEV, width)).astype(jnp.bfloat16)
        grad_keys = grad_keys.reshape(CH_DEV * NBRS * NBR_LEN, width)
        grad_values = grad_values.reshape(CH_DEV * NBRS * NBR_LEN, width)
        d_nbr = (jnp.dot(grad_keys, key_weight.T, preferred_element_type=jnp.float32)
                 + jnp.dot(grad_values, value_weight.T, preferred_element_type=jnp.float32)).astype(jnp.bfloat16)
        d_nbr = d_nbr.reshape(CH_DEV * NBRS, NBR_LEN, E_DIM).astype(jnp.float32)
        store_grad = store_grad.at[chosen].add(d_nbr)
        return store_grad, (attended, d_query)

    start_grad = jnp.zeros((ENC_ROWS, NBR_LEN, E_DIM), jnp.float32)
    store_grad, outputs = lax.scan(one_sequence, start_grad, (query_seq, grad_seq, picks_seq))
    attended = outputs[0].reshape(TOKENS, width)
    d_query = outputs[1].reshape(TOKENS, width)
    return attended, d_query, store_grad.astype(jnp.bfloat16)
```

```python
import jax
import jax.numpy as jnp
from jax import lax
from jax.experimental import pallas as pl
from jax.experimental.pallas import tpu as pltpu
from jax.sharding import Mesh, PartitionSpec as P

HD = 128
SPAN = 64
LANES = 8
PIECE = 4
WIDTHS = (256, 256, 384)
BF = jnp.bfloat16
F32 = jnp.float32
VMEM_BYTES = 48 * 1024 * 1024


def matmul(left, right, left_dim=1, right_dim=0):
    return lax.dot_general(
        left, right, (((left_dim,), (right_dim,)), ((), ())), preferred_element_type=F32
    )


def bounds(widths):
    starts = [0]
    for width in widths:
        starts.append(starts[-1] + width)
    return list(zip(starts[:-1], starts[1:]))


def reorder_matrix(size, stored, quarter):
    to = lax.broadcasted_iota(jnp.int32, (size, size), 0)
    source = lax.broadcasted_iota(jnp.int32, (size, size), 1)
    lane = to // (stored * PIECE)
    row = (to // PIECE) % stored
    token = to % PIECE
    return (source == row * quarter + lane * PIECE + token).astype(F32).astype(BF)


def split_pieces(encoded):
    stored, quarter, features = encoded.shape
    size = stored * quarter

    def kernel(enc_ref, *outs):
        order = reorder_matrix(size, stored, quarter)
        for out, (start, end) in zip(outs, bounds(WIDTHS)):
            out[...] = matmul(order, enc_ref[:, start:end]).astype(BF)

    return pl.pallas_call(
        kernel,
        out_shape=[jax.ShapeDtypeStruct((size, width), BF) for width in WIDTHS],
        compiler_params=pltpu.CompilerParams(vmem_limit_bytes=VMEM_BYTES),
        cost_estimate=pl.CostEstimate(
            flops=2 * size * size * features, bytes_accessed=4 * size * features, transcendentals=0
        ),
        name="split_pieces",
    )(encoded.reshape(size, features))


def join_pieces(parts, stored, quarter, features):
    size = stored * quarter

    def kernel(*refs):
        out_ref = refs[-1]
        order = reorder_matrix(size, stored, quarter)
        for part, (start, end) in zip(refs[:-1], bounds(WIDTHS)):
            out_ref[:, start:end] = matmul(order, part[...], 0, 0).astype(BF)

    joined = pl.pallas_call(
        kernel,
        out_shape=jax.ShapeDtypeStruct((size, features), BF),
        compiler_params=pltpu.CompilerParams(vmem_limit_bytes=VMEM_BYTES),
        cost_estimate=pl.CostEstimate(
            flops=2 * size * size * features, bytes_accessed=4 * size * features, transcendentals=0
        ),
        name="join_pieces",
    )(*parts)
    return joined.reshape(stored, quarter, features)


def pick_rows(store, target):
    planes, rows, width = store.shape
    picks = target.shape[0]

    def kernel(target_ref, store_ref, out_ref, total):
        step = pl.program_id(0)
        row = lax.broadcasted_iota(jnp.int32, (picks, rows), 1) + step * rows
        one_hot = (row == target_ref[...]).astype(F32).astype(BF)
        term = matmul(one_hot, store_ref[0])

        @pl.when(step == 0)
        def _():
            total[...] = term

        @pl.when(step > 0)
        def _():
            total[...] += term

        @pl.when(step == planes - 1)
        def _():
            out_ref[...] = total[...].astype(BF)

    return pl.pallas_call(
        kernel,
        grid=(planes,),
        in_specs=[
            pl.BlockSpec((picks, 1), lambda i: (0, 0)),
            pl.BlockSpec((1, rows, width), lambda i: (i, 0, 0)),
        ],
        out_specs=pl.BlockSpec((picks, width), lambda i: (0, 0)),
        out_shape=jax.ShapeDtypeStruct((picks, width), BF),
        scratch_shapes=[pltpu.VMEM((picks, width), F32)],
        compiler_params=pltpu.CompilerParams(vmem_limit_bytes=VMEM_BYTES),
        cost_estimate=pl.CostEstimate(
            flops=2 * picks * planes * rows * width,
            bytes_accessed=2 * (picks + planes * rows) * width,
            transcendentals=0,
        ),
        name="pick_rows",
    )(target, store)


def sum_rows(terms, target, planes, rows):
    picks, width = terms.shape

    def kernel(target_ref, terms_ref, out_ref):
        step = pl.program_id(0)
        row = lax.broadcasted_iota(jnp.int32, (rows, picks), 0) + step * rows
        one_hot = (row == target_ref[...]).astype(F32).astype(BF)
        out_ref[0] = matmul(one_hot, terms_ref[...]).astype(BF)

    return pl.pallas_call(
        kernel,
        grid=(planes,),
        in_specs=[
            pl.BlockSpec((1, picks), lambda i: (0, 0)),
            pl.BlockSpec((picks, width), lambda i: (0, 0)),
        ],
        out_specs=pl.BlockSpec((1, rows, width), lambda i: (i, 0, 0)),
        out_shape=jax.ShapeDtypeStruct((planes, rows, width), BF),
        compiler_params=pltpu.CompilerParams(vmem_limit_bytes=VMEM_BYTES),
        cost_estimate=pl.CostEstimate(
            flops=2 * picks * planes * rows * width,
            bytes_accessed=2 * (picks + planes * rows) * width,
            transcendentals=0,
        ),
        name="sum_rows",
    )(target, terms)


def attend_spans(member, fetched, key_weight, value_weight, query, d_attended):
    groups, spans, piece_rows, _ = fetched[0].shape
    keys = groups * piece_rows
    features = key_weight.shape[0]
    tokens, width = query.shape
    heads = width // HD
    factor = HD ** (-0.5)
    chunks = len(WIDTHS)

    def kernel(member_ref, *refs):
        parts = refs[:chunks]
        wk_ref, wv_ref, q0_ref, q1_ref, g0_ref, g1_ref = refs[chunks : chunks + 6]
        att_ref, dq_ref = refs[chunks + 6 : chunks + 8]
        outs = refs[chunks + 8 : 2 * chunks + 8]
        last_att, last_dq = refs[2 * chunks + 8 :]
        span = pl.program_id(0)

        @pl.when(span == 0)
        def _():
            last_att[...] = jnp.zeros_like(last_att)
            last_dq[...] = jnp.zeros_like(last_dq)

        rows = jnp.concatenate(
            [part[:, 0].astype(F32).reshape(keys, part.shape[3]).astype(BF) for part in parts], 1
        )
        wk = wk_ref[...]
        wv = wv_ref[...]
        key_rows = matmul(rows, wk).astype(BF)
        value_rows = matmul(rows, wv).astype(BF)

        to = lax.broadcasted_iota(jnp.int32, (SPAN, 2 * SPAN), 0)
        source = lax.broadcasted_iota(jnp.int32, (SPAN, 2 * SPAN), 1)
        inside = (source < SPAN) | (span < spans - 1)
        ahead = ((source == to + SPAN - 1) & inside).astype(F32).astype(BF)
        back = (source == to + 1).astype(F32).astype(BF)
        shifted = matmul(ahead, jnp.concatenate([q0_ref[...], q1_ref[...]], 0)).astype(BF)
        grad_shift = matmul(ahead, jnp.concatenate([g0_ref[...], g1_ref[...]], 0)).astype(BF)

        blended, grad_shifted, grad_keys, grad_values = [], [], [], []
        for head in range(heads):
            cols = slice(head * HD, (head + 1) * HD)
            q, g, k, v = shifted[:, cols], grad_shift[:, cols], key_rows[:, cols], value_rows[:, cols]
            scores = matmul(q, k, 1, 1) * factor
            weights = jnp.exp(scores - jnp.max(scores, axis=1, keepdims=True))
            probs = weights / jnp.sum(weights, axis=1, keepdims=True)
            probs_b = probs.astype(BF)
            blended.append(matmul(probs_b, v))
            grad_probs = matmul(g, v, 1, 1)
            inner = jnp.sum(probs * grad_probs, axis=1, keepdims=True)
            grad_scores = (probs * (grad_probs - inner) * factor).astype(BF)
            grad_shifted.append(matmul(grad_scores, k))
            grad_keys.append(matmul(grad_scores, q, 0, 0))
            grad_values.append(matmul(probs_b, g, 0, 0))
        now_att = jnp.concatenate(blended, 1).astype(BF)
        now_dq = jnp.concatenate(grad_shifted, 1).astype(BF)
        att_ref[...] = matmul(back, jnp.concatenate([last_att[...], now_att], 0)).astype(BF)
        dq_ref[...] = matmul(back, jnp.concatenate([last_dq[...], now_dq], 0)).astype(BF)
        last_att[...] = now_att
        last_dq[...] = now_dq
        gk = jnp.concatenate(grad_keys, 1).astype(BF)
        gv = jnp.concatenate(grad_values, 1).astype(BF)
        for out, (start, end) in zip(outs, bounds(WIDTHS)):
            term = matmul(gk, wk[start:end], 1, 1) + matmul(gv, wv[start:end], 1, 1)
            out[...] = term.reshape(groups, 1, piece_rows, end - start).astype(BF)

    def this(i, m):
        return (i, 0)

    def following(i, m):
        return (jnp.minimum(i + 1, spans - 1), 0)

    block = (SPAN, width)
    part_specs = [
        pl.BlockSpec((groups, 1, piece_rows, w), lambda i, m: (0, i, 0, 0)) for w in WIDTHS
    ]
    weight_spec = pl.BlockSpec((features, width), lambda i, m: (0, m[0]))
    return pl.pallas_call(
        kernel,
        grid_spec=pltpu.PrefetchScalarGridSpec(
            num_scalar_prefetch=1,
            grid=(spans,),
            in_specs=part_specs
            + [
                weight_spec,
                weight_spec,
                pl.BlockSpec(block, this),
                pl.BlockSpec(block, following),
                pl.BlockSpec(block, this),
                pl.BlockSpec(block, following),
            ],
            out_specs=[pl.BlockSpec(block, this), pl.BlockSpec(block, this)] + part_specs,
            scratch_shapes=[pltpu.VMEM(block, BF), pltpu.VMEM(block, BF)],
        ),
        out_shape=[jax.ShapeDtypeStruct((tokens, width), BF)] * 2
        + [jax.ShapeDtypeStruct((groups, spans, piece_rows, w), BF) for w in WIDTHS],
        compiler_params=pltpu.CompilerParams(vmem_limit_bytes=VMEM_BYTES),
        cost_estimate=pl.CostEstimate(
            flops=spans * (8 * keys * features * width + 14 * SPAN * keys * width),
            bytes_accessed=4 * spans * keys * features + 8 * tokens * width,
            transcendentals=spans * heads * SPAN * keys,
        ),
        name="attend_spans",
    )(member, *fetched, key_weight, value_weight, query, query, d_attended, d_attended)


def shards(query, d_attended, encoded, key_weight, value_weight, nbr_shard, nbr_row):
    plane = ("y", "c")
    planes = lax.axis_size("z")
    groups = lax.axis_size("x")
    member = lax.axis_index("x").astype(jnp.int32).reshape(1)
    spans, neighbours = nbr_shard.shape
    stored, quarter, features = encoded.shape
    rows = LANES * stored * PIECE
    requested = spans * neighbours * PIECE

    picks = (nbr_shard * stored + nbr_row).reshape(spans * neighbours)
    all_picks = lax.all_gather(picks, plane, tiled=True)
    target = (all_picks[:, None] * PIECE + jnp.arange(PIECE, dtype=jnp.int32)[None, :]).reshape(-1)

    fetched = []
    for piece in split_pieces(encoded):
        piece = lax.all_to_all(piece, plane, 0, 0, tiled=True)
        store = lax.all_gather(piece, "z", axis=0, tiled=False)
        picked = pick_rows(store, target.reshape(-1, 1))
        mine = lax.all_to_all(picked, plane, 0, 0, tiled=True)
        every = lax.all_gather(mine, "x", axis=0, tiled=False)
        fetched.append(every.reshape(groups * LANES, spans, neighbours * PIECE, -1))

    attended, d_query, *terms = attend_spans(
        member, fetched, key_weight, value_weight, query, d_attended
    )

    returned = []
    for term in terms:
        width = term.shape[-1]
        swapped = lax.all_to_all(
            term.reshape(groups, LANES * requested, width), "x", 0, 0, tiled=True
        )
        d_nbr = jnp.sum(swapped.astype(F32), axis=0).astype(BF)
        home = lax.all_to_all(d_nbr, plane, 0, 0, tiled=True)
        sums = sum_rows(home, target.reshape(1, -1), planes, rows)
        reduced = lax.psum_scatter(sums, "z", scatter_dimension=0, tiled=True)
        reduced = reduced.reshape(rows, width)
        returned.append(lax.all_to_all(reduced, plane, 0, 0, tiled=True))
    d_encoded = join_pieces(returned, stored, quarter, features)
    return (attended, d_query, d_encoded)


def solution(mesh):
    groups = mesh.devices.shape[1]
    fine = Mesh(mesh.devices.reshape(-1, LANES // 2, 2, groups), ("z", "y", "c", "x"))
    seq = ("z", "y", "c")
    placed = (
        P(seq, "x"),
        P(seq, "x"),
        P(seq, "x", None),
        P(),
        P(),
        P(seq, None),
        P(seq, None),
    )
    return jax.shard_map(
        shards,
        mesh=fine,
        in_specs=placed,
        out_specs=(P(seq, "x"), P(seq, "x"), P(seq, "x", None)),
        check_vma=False,
    )
```

```python
import jax
import jax.numpy as jnp
from jax import lax
from jax.experimental import pallas as pl
from jax.experimental.pallas import tpu as pltpu
from jax.sharding import Mesh, PartitionSpec as P

HD = 128
SPAN = 64
LANES = 8
PIECE = 4
WIDTHS = (512, 384)
BF = jnp.bfloat16
F32 = jnp.float32
I32 = jnp.int32
PARAMS = pltpu.CompilerParams(vmem_limit_bytes=48 * 1024 * 1024)


def matmul(left, right, left_dim=1, right_dim=0):
    return lax.dot_general(
        left, right, (((left_dim,), (right_dim,)), ((), ())), preferred_element_type=F32
    )


def bounds(widths):
    starts = [0]
    for width in widths:
        starts.append(starts[-1] + width)
    return list(zip(starts[:-1], starts[1:]))


def cost(flops, bytes_accessed, transcendentals=0):
    return pl.CostEstimate(
        flops=int(flops), bytes_accessed=int(bytes_accessed), transcendentals=int(transcendentals)
    )


def send_ring(array, axis, step):
    size = lax.axis_size(axis)
    if step % size == 0:
        return array
    return lax.ppermute(array, axis, [(i, (i + step) % size) for i in range(size)])


def piece_matrix(plane_ref, away, stored, quarter):
    plane = (plane_ref[0] + away) % LANES
    shape = (stored * PIECE, stored * quarter)
    to = lax.broadcasted_iota(I32, shape, 0)
    source = lax.broadcasted_iota(I32, shape, 1)
    token = (to // PIECE) * quarter + to % PIECE + plane * PIECE
    return (source == token).astype(F32).astype(BF)


def split_pieces(encoded, plane):
    stored, quarter, features = encoded.shape
    size = stored * quarter

    def kernel(plane_ref, enc_ref, *outs):
        order = jnp.concatenate(
            [piece_matrix(plane_ref, away, stored, quarter) for away in range(LANES)], 0
        )
        step = stored * PIECE
        for chunk, (start, end) in enumerate(bounds(WIDTHS)):
            pieces = matmul(order, enc_ref[:, start:end]).astype(BF)
            for away in range(LANES):
                outs[chunk * LANES + away][...] = pieces[away * step : (away + 1) * step]

    outs = pl.pallas_call(
        kernel,
        in_specs=[pl.BlockSpec(memory_space=pltpu.SMEM), pl.BlockSpec(memory_space=pltpu.VMEM)],
        out_shape=[
            jax.ShapeDtypeStruct((stored * PIECE, width), BF)
            for width in WIDTHS
            for _ in range(LANES)
        ],
        compiler_params=PARAMS,
        cost_estimate=cost(2 * size * size * features, 4 * size * features),
        name="split_pieces",
    )(plane, encoded.reshape(size, features))
    return [outs[i * LANES : (i + 1) * LANES] for i in range(len(WIDTHS))]


def join_pieces(parts, plane, stored, quarter, features):
    size = stored * quarter

    def kernel(plane_ref, *refs):
        out_ref = refs[-1]
        order = jnp.concatenate(
            [piece_matrix(plane_ref, away, stored, quarter) for away in range(LANES)], 0
        )
        for chunk, (start, end) in enumerate(bounds(WIDTHS)):
            pieces = [ref[...] for ref in refs[chunk * LANES : (chunk + 1) * LANES]]
            out_ref[:, start:end] = matmul(order, jnp.concatenate(pieces, 0), 0, 0).astype(BF)

    joined = pl.pallas_call(
        kernel,
        in_specs=[pl.BlockSpec(memory_space=pltpu.SMEM)]
        + [pl.BlockSpec(memory_space=pltpu.VMEM)] * (LANES * len(WIDTHS)),
        out_shape=jax.ShapeDtypeStruct((size, features), BF),
        compiler_params=PARAMS,
        cost_estimate=cost(2 * size * size * features, 4 * size * features),
        name="join_pieces",
    )(plane, *[piece for part in parts for piece in part])
    return joined.reshape(stored, quarter, features)


def pick_rows(stores, target, other=None):
    rows, width = stores[0].shape
    blocks = len(stores)
    picks = target.shape[0]
    parts = 1 if other is None else LANES
    each = picks // parts
    extra = [] if other is None else [other]

    def kernel(target_ref, *refs):
        total = None if other is None else refs[blocks][...].astype(F32)
        outs = refs[blocks + len(extra) :]
        column = lax.broadcasted_iota(I32, (picks, rows), 1)
        for block in range(blocks):
            one_hot = (column == target_ref[...] - block * rows).astype(F32).astype(BF)
            term = matmul(one_hot, refs[block][...])
            total = term if total is None else total + term
        for part in range(parts):
            outs[part][...] = total[part * each : (part + 1) * each].astype(BF)

    return pl.pallas_call(
        kernel,
        out_shape=[jax.ShapeDtypeStruct((each, width), BF)] * parts,
        compiler_params=PARAMS,
        cost_estimate=cost(
            2 * picks * blocks * rows * width, 2 * (picks + blocks * rows) * width
        ),
        name="pick_rows",
    )(target, *stores, *extra)


def sum_rows(terms, target, blocks, rows):
    width = terms[0].shape[1]
    picks = target.shape[1]
    count = len(terms)

    def kernel(target_ref, *refs):
        joined = jnp.concatenate([ref[...] for ref in refs[:count]], 0)
        row = lax.broadcasted_iota(I32, (rows, picks), 0)
        for block in range(blocks):
            one_hot = (row == target_ref[...] - block * rows).astype(F32).astype(BF)
            refs[count + block][...] = matmul(one_hot, joined).astype(BF)

    return pl.pallas_call(
        kernel,
        out_shape=[jax.ShapeDtypeStruct((rows, width), BF)] * blocks,
        compiler_params=PARAMS,
        cost_estimate=cost(
            2 * picks * blocks * rows * width, 2 * (picks + blocks * rows) * width
        ),
        name="sum_rows",
    )(target, *terms)


def add_and_cut(terms, parts):
    rows, width = terms[0].shape
    each = rows // parts
    count = len(terms)

    def kernel(*refs):
        total = refs[0][...].astype(F32)
        for ref in refs[1:count]:
            total = total + ref[...].astype(F32)
        for part in range(parts):
            refs[count + part][...] = total[part * each : (part + 1) * each].astype(BF)

    return pl.pallas_call(
        kernel,
        out_shape=[jax.ShapeDtypeStruct((each, width), BF)] * parts,
        compiler_params=PARAMS,
        cost_estimate=cost(count * rows * width, 2 * (count + 1) * rows * width),
        name="add_and_cut",
    )(*terms)


def attend_spans(member, fetched, key_weight, value_weight, query, d_attended):
    groups = len(fetched[0])
    spans, piece_rows = fetched[0][0].shape[1:3]
    here = LANES * piece_rows
    keys = groups * here
    features = key_weight.shape[0]
    tokens, width = query.shape
    heads = width // HD
    factor = HD ** (-0.5)
    count = len(WIDTHS) * groups

    def kernel(member_ref, *refs):
        parts = refs[:count]
        wk_ref, wv_ref, q0_ref, q1_ref, g0_ref, g1_ref = refs[count : count + 6]
        att_ref, dq_ref = refs[count + 6 : count + 8]
        outs = refs[count + 8 : 2 * count + 8]
        last_att, last_dq = refs[2 * count + 8 :]
        span = pl.program_id(0)

        @pl.when(span == 0)
        def _():
            last_att[...] = jnp.zeros_like(last_att)
            last_dq[...] = jnp.zeros_like(last_dq)

        def chunk_rows(chunk):
            pieces = [
                part[:, 0].astype(F32).reshape(here, part.shape[3])
                for part in parts[chunk * groups : (chunk + 1) * groups]
            ]
            return jnp.concatenate(pieces, 0).astype(BF)

        rows = jnp.concatenate([chunk_rows(chunk) for chunk in range(len(WIDTHS))], 1)
        wk = wk_ref[...]
        wv = wv_ref[...]
        key_rows = matmul(rows, wk).astype(BF)
        value_rows = matmul(rows, wv).astype(BF)

        to = lax.broadcasted_iota(I32, (SPAN, 2 * SPAN), 0)
        source = lax.broadcasted_iota(I32, (SPAN, 2 * SPAN), 1)
        inside = (source < SPAN) | (span < spans - 1)
        ahead = ((source == to + SPAN - 1) & inside).astype(F32).astype(BF)
        back = (source == to + 1).astype(F32).astype(BF)
        shifted = matmul(ahead, jnp.concatenate([q0_ref[...], q1_ref[...]], 0)).astype(BF)
        grad_shift = matmul(ahead, jnp.concatenate([g0_ref[...], g1_ref[...]], 0)).astype(BF)

        cols = [slice(head * HD, (head + 1) * HD) for head in range(heads)]
        scores = [matmul(shifted[:, c], key_rows[:, c], 1, 1) * factor for c in cols]
        grad_probs = [matmul(grad_shift[:, c], value_rows[:, c], 1, 1) for c in cols]
        probs_b, grad_scores = [], []
        for score, grad in zip(scores, grad_probs):
            weights = jnp.exp(score - jnp.max(score, axis=1, keepdims=True))
            probs = weights / jnp.sum(weights, axis=1, keepdims=True)
            inner = jnp.sum(probs * grad, axis=1, keepdims=True)
            probs_b.append(probs.astype(BF))
            grad_scores.append((probs * (grad - inner) * factor).astype(BF))
        blended = [matmul(p, value_rows[:, c]) for p, c in zip(probs_b, cols)]
        grad_shifted = [matmul(s, key_rows[:, c]) for s, c in zip(grad_scores, cols)]
        grad_keys = [matmul(s, shifted[:, c], 0, 0) for s, c in zip(grad_scores, cols)]
        grad_values = [matmul(p, grad_shift[:, c], 0, 0) for p, c in zip(probs_b, cols)]
        now_att = jnp.concatenate(blended, 1).astype(BF)
        now_dq = jnp.concatenate(grad_shifted, 1).astype(BF)
        att_ref[...] = matmul(back, jnp.concatenate([last_att[...], now_att], 0)).astype(BF)
        dq_ref[...] = matmul(back, jnp.concatenate([last_dq[...], now_dq], 0)).astype(BF)
        last_att[...] = now_att
        last_dq[...] = now_dq
        gk = jnp.concatenate(grad_keys, 1).astype(BF)
        gv = jnp.concatenate(grad_values, 1).astype(BF)
        for chunk, (start, end) in enumerate(bounds(WIDTHS)):
            term = matmul(gk, wk[start:end], 1, 1) + matmul(gv, wv[start:end], 1, 1)
            for group in range(groups):
                piece = term[group * here : (group + 1) * here]
                outs[chunk * groups + group][...] = piece.reshape(
                    LANES, 1, piece_rows, end - start
                ).astype(BF)

    def this(i, m):
        return (i, 0)

    def following(i, m):
        return (jnp.minimum(i + 1, spans - 1), 0)

    block = (SPAN, width)
    part_specs = [
        pl.BlockSpec((LANES, 1, piece_rows, w), lambda i, m: (0, i, 0, 0))
        for w in WIDTHS
        for _ in range(groups)
    ]
    weight_spec = pl.BlockSpec((features, width), lambda i, m: (0, m[0]))
    outs = pl.pallas_call(
        kernel,
        grid_spec=pltpu.PrefetchScalarGridSpec(
            num_scalar_prefetch=1,
            grid=(spans,),
            in_specs=part_specs
            + [
                weight_spec,
                weight_spec,
                pl.BlockSpec(block, this),
                pl.BlockSpec(block, following),
                pl.BlockSpec(block, this),
                pl.BlockSpec(block, following),
            ],
            out_specs=[pl.BlockSpec(block, this), pl.BlockSpec(block, this)] + part_specs,
            scratch_shapes=[pltpu.VMEM(block, BF), pltpu.VMEM(block, BF)],
        ),
        out_shape=[jax.ShapeDtypeStruct((tokens, width), BF)] * 2
        + [
            jax.ShapeDtypeStruct((LANES, spans, piece_rows, w), BF)
            for w in WIDTHS
            for _ in range(groups)
        ],
        compiler_params=PARAMS,
        cost_estimate=cost(
            spans * (8 * keys * features * width + 14 * SPAN * keys * width),
            4 * spans * keys * features + 8 * tokens * width,
            spans * heads * SPAN * keys,
        ),
        name="attend_spans",
    )(
        member,
        *[part for parts in fetched for part in parts],
        key_weight,
        value_weight,
        query,
        query,
        d_attended,
        d_attended,
    )
    terms = [outs[2 + i * groups : 2 + (i + 1) * groups] for i in range(len(WIDTHS))]
    return outs[0], outs[1], terms


def shards(query, d_attended, encoded, key_weight, value_weight, nbr_shard, nbr_row):
    planes = lax.axis_size("z")
    groups = lax.axis_size("x")
    columns = lax.axis_size("y")
    z, y, c, x = [lax.axis_index(axis).astype(I32) for axis in ("z", "y", "c", "x")]
    spans, neighbours = nbr_shard.shape
    stored, quarter, features = encoded.shape
    rows = planes * stored * PIECE
    plane = z.reshape(1)

    own = []
    for pieces in split_pieces(encoded, plane):
        own.append(
            jnp.concatenate([send_ring(piece, "z", k) for k, piece in enumerate(pieces)], 0)
        )

    picks = (nbr_shard * stored + nbr_row).reshape(spans * neighbours)
    picks, own[0] = lax.optimization_barrier((picks, own[0]))
    picks = lax.all_gather(picks, ("z", "c"), tiled=True).reshape(planes, 2, -1)
    picks = jnp.roll(jnp.roll(picks, -z, 0), -c, 1).transpose(1, 0, 2)
    store = picks // stored
    away_y = (y - store // 2 % columns) % columns
    away_z = (z - store // (2 * columns)) % planes
    first = away_y * rows + away_z * (stored * PIECE) + picks % stored * PIECE
    first = jnp.where(store % 2 == c, first, -columns * rows)
    target = (first[..., None] + jnp.arange(PIECE, dtype=I32)).reshape(2, -1)

    fetched = []
    for chunk, width in enumerate(WIDTHS):
        gathered = [send_ring(own[chunk], "y", a) for a in range(columns)]
        (theirs,) = pick_rows(gathered, target[1].reshape(-1, 1))
        picked = pick_rows(gathered, target[0].reshape(-1, 1), send_ring(theirs, "c", 1))
        mine = jnp.concatenate([send_ring(part, "z", r) for r, part in enumerate(picked)], 0)
        fetched.append(
            [
                send_ring(mine, "x", away).reshape(LANES, spans, neighbours * PIECE, width)
                for away in range(groups)
            ]
        )

    attended, d_query, terms = attend_spans(
        x.reshape(1), fetched, key_weight, value_weight, query, d_attended
    )

    returned = []
    for chunk, parts in enumerate(terms):
        width = WIDTHS[chunk]
        arrived = [
            send_ring(part.reshape(-1, width), "x", -away) for away, part in enumerate(parts)
        ]
        d_nbr = add_and_cut(arrived, planes)
        home = jnp.concatenate([send_ring(part, "z", -r) for r, part in enumerate(d_nbr)], 0)
        sums = sum_rows([home, send_ring(home, "c", 1)], target.reshape(1, -1), columns, rows)
        whole = add_and_cut([send_ring(part, "y", -a) for a, part in enumerate(sums)], planes)
        returned.append([send_ring(part, "z", -k) for k, part in enumerate(whole)])
    d_encoded = join_pieces(returned, plane, stored, quarter, features)
    return (attended, d_query, d_encoded)


def solution(mesh):
    groups = mesh.devices.shape[1]
    fine = Mesh(mesh.devices.reshape(-1, LANES // 2, 2, groups), ("z", "y", "c", "x"))
    seq = ("z", "y", "c")
    placed = (
        P(seq, "x"),
        P(seq, "x"),
        P(seq, "x", None),
        P(),
        P(),
        P(seq, None),
        P(seq, None),
    )
    return jax.shard_map(
        shards,
        mesh=fine,
        in_specs=placed,
        out_specs=(P(seq, "x"), P(seq, "x"), P(seq, "x", None)),
        check_vma=False,
    )
```

```python
import jax
import jax.numpy as jnp
from jax import lax
from jax.experimental import pallas as pl
from jax.experimental.pallas import tpu as pltpu
from jax.sharding import Mesh, PartitionSpec as P

HD = 128
SPAN = 64
LANES = 8
PIECE = 4
WIDTHS = (512, 384)
BF = jnp.bfloat16
F32 = jnp.float32
I32 = jnp.int32
PARAMS = pltpu.CompilerParams(vmem_limit_bytes=48 * 1024 * 1024)


def matmul(left, right, left_dim=1, right_dim=0):
    return lax.dot_general(
        left, right, (((left_dim,), (right_dim,)), ((), ())), preferred_element_type=F32
    )


def bounds(widths):
    starts = [0]
    for width in widths:
        starts.append(starts[-1] + width)
    return list(zip(starts[:-1], starts[1:]))


def cost(flops, bytes_accessed, transcendentals=0):
    return pl.CostEstimate(
        flops=int(flops), bytes_accessed=int(bytes_accessed), transcendentals=int(transcendentals)
    )


def send_ring(array, axis, step):
    size = lax.axis_size(axis)
    if step % size == 0:
        return array
    return lax.ppermute(array, axis, [(i, (i + step) % size) for i in range(size)])


def piece_matrix(plane_ref, away, stored, quarter):
    plane = (plane_ref[0] + away) % LANES
    shape = (stored * PIECE, stored * quarter)
    to = lax.broadcasted_iota(I32, shape, 0)
    source = lax.broadcasted_iota(I32, shape, 1)
    token = (to // PIECE) * quarter + to % PIECE + plane * PIECE
    return (source == token).astype(F32).astype(BF)


def split_pieces(encoded, plane):
    stored, quarter, features = encoded.shape
    size = stored * quarter

    def kernel(plane_ref, enc_ref, *outs):
        order = jnp.concatenate(
            [piece_matrix(plane_ref, away, stored, quarter) for away in range(LANES)], 0
        )
        step = stored * PIECE
        for chunk, (start, end) in enumerate(bounds(WIDTHS)):
            pieces = matmul(order, enc_ref[:, start:end]).astype(BF)
            for away in range(LANES):
                outs[chunk * LANES + away][...] = pieces[away * step : (away + 1) * step]

    outs = pl.pallas_call(
        kernel,
        in_specs=[pl.BlockSpec(memory_space=pltpu.SMEM), pl.BlockSpec(memory_space=pltpu.VMEM)],
        out_shape=[
            jax.ShapeDtypeStruct((stored * PIECE, width), BF)
            for width in WIDTHS
            for _ in range(LANES)
        ],
        compiler_params=PARAMS,
        cost_estimate=cost(2 * size * size * features, 4 * size * features),
        name="split_pieces",
    )(plane, encoded.reshape(size, features))
    return [outs[i * LANES : (i + 1) * LANES] for i in range(len(WIDTHS))]


def join_pieces(parts, plane, stored, quarter, features):
    size = stored * quarter

    def kernel(plane_ref, *refs):
        out_ref = refs[-1]
        order = jnp.concatenate(
            [piece_matrix(plane_ref, away, stored, quarter) for away in range(LANES)], 0
        )
        for chunk, (start, end) in enumerate(bounds(WIDTHS)):
            pieces = [ref[...] for ref in refs[chunk * LANES : (chunk + 1) * LANES]]
            out_ref[:, start:end] = matmul(order, jnp.concatenate(pieces, 0), 0, 0).astype(BF)

    joined = pl.pallas_call(
        kernel,
        in_specs=[pl.BlockSpec(memory_space=pltpu.SMEM)]
        + [pl.BlockSpec(memory_space=pltpu.VMEM)] * (LANES * len(WIDTHS)),
        out_shape=jax.ShapeDtypeStruct((size, features), BF),
        compiler_params=PARAMS,
        cost_estimate=cost(2 * size * size * features, 4 * size * features),
        name="join_pieces",
    )(plane, *[piece for part in parts for piece in part])
    return joined.reshape(stored, quarter, features)


def pick_rows(stores, target, other=None):
    rows, width = stores[0].shape
    blocks = len(stores)
    picks = target.shape[0]
    parts = 1 if other is None else LANES
    each = picks // parts
    extra = [] if other is None else [other]

    def kernel(target_ref, *refs):
        total = None if other is None else refs[blocks][...].astype(F32)
        outs = refs[blocks + len(extra) :]
        column = lax.broadcasted_iota(I32, (picks, rows), 1)
        for block in range(blocks):
            one_hot = (column == target_ref[...] - block * rows).astype(F32).astype(BF)
            term = matmul(one_hot, refs[block][...])
            total = term if total is None else total + term
        for part in range(parts):
            outs[part][...] = total[part * each : (part + 1) * each].astype(BF)

    return pl.pallas_call(
        kernel,
        out_shape=[jax.ShapeDtypeStruct((each, width), BF)] * parts,
        compiler_params=PARAMS,
        cost_estimate=cost(
            2 * picks * blocks * rows * width, 2 * (picks + blocks * rows) * width
        ),
        name="pick_rows",
    )(target, *stores, *extra)


def sum_rows(terms, target, blocks, rows):
    width = terms[0].shape[1]
    picks = target.shape[1]
    count = len(terms)

    def kernel(target_ref, *refs):
        joined = jnp.concatenate([ref[...] for ref in refs[:count]], 0)
        row = lax.broadcasted_iota(I32, (rows, picks), 0)
        for block in range(blocks):
            one_hot = (row == target_ref[...] - block * rows).astype(F32).astype(BF)
            refs[count + block][...] = matmul(one_hot, joined).astype(BF)

    return pl.pallas_call(
        kernel,
        out_shape=[jax.ShapeDtypeStruct((rows, width), BF)] * blocks,
        compiler_params=PARAMS,
        cost_estimate=cost(
            2 * picks * blocks * rows * width, 2 * (picks + blocks * rows) * width
        ),
        name="sum_rows",
    )(target, *terms)


def add_and_cut(terms, parts):
    rows, width = terms[0].shape
    each = rows // parts
    count = len(terms)

    def kernel(*refs):
        total = refs[0][...].astype(F32)
        for ref in refs[1:count]:
            total = total + ref[...].astype(F32)
        for part in range(parts):
            refs[count + part][...] = total[part * each : (part + 1) * each].astype(BF)

    return pl.pallas_call(
        kernel,
        out_shape=[jax.ShapeDtypeStruct((each, width), BF)] * parts,
        compiler_params=PARAMS,
        cost_estimate=cost(count * rows * width, 2 * (count + 1) * rows * width),
        name="add_and_cut",
    )(*terms)


def move_tokens(arrays, forward):
    tokens, width = arrays[0].shape
    spans = tokens // SPAN
    count = len(arrays)

    def kernel(*refs):
        to = lax.broadcasted_iota(I32, (SPAN, 2 * SPAN), 0)
        source = lax.broadcasted_iota(I32, (SPAN, 2 * SPAN), 1)
        step = SPAN - 1 if forward else 1
        order = (source == to + step).astype(F32).astype(BF)
        blank = jnp.zeros((SPAN, width), BF)
        for ref, out in zip(refs[:count], refs[count:]):
            for span in range(spans):
                low = span if forward else span - 1
                pair = [
                    ref[u * SPAN : (u + 1) * SPAN] if 0 <= u < spans else blank
                    for u in (low, low + 1)
                ]
                moved = matmul(order, jnp.concatenate(pair, 0))
                out[span * SPAN : (span + 1) * SPAN] = moved.astype(BF)

    return pl.pallas_call(
        kernel,
        out_shape=[jax.ShapeDtypeStruct((tokens, width), BF)] * count,
        compiler_params=PARAMS,
        cost_estimate=cost(4 * count * tokens * SPAN * width, 4 * count * tokens * width),
        name="move_tokens",
    )(*arrays)


def two_heads(pair):
    column = lax.broadcasted_iota(I32, (2 * SPAN, 2 * HD), 1)
    row = lax.broadcasted_iota(I32, (2 * SPAN, 2 * HD), 0)
    mask = ((column < HD) == (row < SPAN)).astype(F32).astype(BF)
    return jnp.concatenate([pair, pair], 0) * mask


def score_spans(fetched, key_weight, value_weight, shifted, grad_shift):
    count = len(fetched[0])
    chunks = len(fetched)
    features, all_width = key_weight.shape
    groups, tokens, width = shifted.shape
    spans = tokens // SPAN
    piece_rows = fetched[0][0].shape[0] // spans
    keys = count * piece_rows
    pairs = all_width // (2 * HD)
    per_group = pairs // groups
    factor = HD ** (-0.5)

    def kernel(*refs):
        wk_ref, wv_ref, q_ref, g_ref = refs[count * chunks : count * chunks + 4]
        k_ref, v_ref, w_ref, gp_ref, stat_ref, rows_ref = refs[count * chunks + 4 :]

        @pl.when(pl.program_id(0) == 0)
        def _():
            for chunk, (start, end) in enumerate(bounds(WIDTHS)):
                parts = [ref[...] for ref in refs[chunk * count : (chunk + 1) * count]]
                rows_ref[:, start:end] = jnp.concatenate(parts, 0)

        rows = rows_ref[...]

        def project(weight):
            out = matmul(rows, weight).reshape(count, spans, piece_rows, 2 * HD)
            return out.transpose(1, 0, 2, 3).reshape(spans, keys, 2 * HD).astype(BF)

        k_ref[...] = project(wk_ref[...])
        v_ref[...] = project(wv_ref[...])
        for span in range(spans):
            tok = pl.ds(span * SPAN, SPAN)
            scores = matmul(k_ref[span], two_heads(q_ref[0, tok, :]), 1, 1) * factor
            grad = matmul(v_ref[span], two_heads(g_ref[0, tok, :]), 1, 1)
            top = jnp.max(scores, axis=0, keepdims=True)
            weights = jnp.exp(scores - top)
            w_ref[0, span] = weights
            gp_ref[0, span] = grad
            stat_ref[0, 0, pl.ds(span, 1), :] = top
            stat_ref[0, 1, pl.ds(span, 1), :] = jnp.sum(weights, axis=0, keepdims=True)
            stat_ref[0, 2, pl.ds(span, 1), :] = jnp.sum(weights * grad, axis=0, keepdims=True)

    whole = [
        pl.BlockSpec((spans * piece_rows, w), lambda i: (0, 0)) for w in WIDTHS for _ in range(count)
    ]
    weight_spec = pl.BlockSpec((features, 2 * HD), lambda i: (0, i))
    token_spec = pl.BlockSpec((1, tokens, 2 * HD), lambda i: (i // per_group, 0, i % per_group))
    kv_spec = pl.BlockSpec((spans, keys, 2 * HD), lambda i: (0, 0, i))
    score_spec = pl.BlockSpec((1, spans, keys, 2 * SPAN), lambda i: (i, 0, 0, 0))
    return pl.pallas_call(
        kernel,
        grid=(pairs,),
        in_specs=whole + [weight_spec, weight_spec, token_spec, token_spec],
        out_specs=[
            kv_spec,
            kv_spec,
            score_spec,
            score_spec,
            pl.BlockSpec((1, 3, spans, 2 * SPAN), lambda i: (i, 0, 0, 0)),
        ],
        out_shape=[
            jax.ShapeDtypeStruct((spans, keys, all_width), BF),
            jax.ShapeDtypeStruct((spans, keys, all_width), BF),
            jax.ShapeDtypeStruct((pairs, spans, keys, 2 * SPAN), F32),
            jax.ShapeDtypeStruct((pairs, spans, keys, 2 * SPAN), F32),
            jax.ShapeDtypeStruct((pairs, 3, spans, 2 * SPAN), F32),
        ],
        scratch_shapes=[pltpu.VMEM((count * spans * piece_rows, features), BF)],
        compiler_params=PARAMS,
        cost_estimate=cost(
            4 * spans * keys * (features + SPAN) * all_width,
            8 * spans * keys * all_width,
            spans * keys * SPAN * 2 * pairs,
        ),
        name="score_spans",
    )(*[part for parts in fetched for part in parts], key_weight, value_weight, shifted, grad_shift)


def blend_spans(
    key_rows, value_rows, weights, grad_probs, stats, key_weight, value_weight, shifted, grad_shift
):
    features, all_width = key_weight.shape
    groups, tokens, width = shifted.shape
    spans, keys, _ = key_rows.shape
    count = LANES
    chunks = len(WIDTHS)
    piece_rows = keys // count
    pairs = all_width // (2 * HD)
    per_group = pairs // groups
    factor = HD ** (-0.5)
    devices = len(stats)

    def kernel(k_ref, v_ref, w_ref, gp_ref, *refs):
        stat_refs = refs[:devices]
        wk_ref, wv_ref, q_ref, g_ref, att_ref, dq_ref = refs[devices : devices + 6]
        outs = refs[devices + 6 : devices + 6 + count * chunks]
        total, gk_ref, gv_ref = refs[devices + 6 + count * chunks :]
        step = pl.program_id(0)

        own_top = stat_refs[0][0, 0]
        top = own_top
        for ref in stat_refs[1:]:
            top = jnp.maximum(top, ref[0, 0])
        sums = jnp.zeros_like(top)
        inner = jnp.zeros_like(top)
        for ref in stat_refs:
            scale = jnp.exp(ref[0, 0] - top)
            sums = sums + ref[0, 1] * scale
            inner = inner + ref[0, 2] * scale
        scale = jnp.exp(own_top - top) / sums
        inner = inner / sums

        for span in range(spans):
            tok = pl.ds(span * SPAN, SPAN)
            probs = w_ref[0, span] * scale[span : span + 1]
            probs_b = probs.astype(BF)
            grad_scores = (
                probs * (gp_ref[0, span] - inner[span : span + 1]) * factor
            ).astype(BF)
            k, v = k_ref[span], v_ref[span]
            blended = matmul(probs_b, v, 0, 0)
            shifted_grad = matmul(grad_scores, k, 0, 0)
            att_ref[0, tok, :HD] = blended[:SPAN, :HD].astype(BF)
            att_ref[0, tok, HD:] = blended[SPAN:, HD:].astype(BF)
            dq_ref[0, tok, :HD] = shifted_grad[:SPAN, :HD].astype(BF)
            dq_ref[0, tok, HD:] = shifted_grad[SPAN:, HD:].astype(BF)
            gk = matmul(grad_scores, two_heads(q_ref[0, tok, :]))
            gv = matmul(probs_b, two_heads(g_ref[0, tok, :]))
            gk_ref[:, span] = gk.reshape(count, piece_rows, 2 * HD)
            gv_ref[:, span] = gv.reshape(count, piece_rows, 2 * HD)

        flat = (count * spans * piece_rows, 2 * HD)
        term = matmul(gk_ref[...].reshape(flat).astype(BF), wk_ref[...], 1, 1)
        term = term + matmul(gv_ref[...].reshape(flat).astype(BF), wv_ref[...], 1, 1)

        @pl.when(step == 0)
        def _():
            total[...] = term

        @pl.when(step > 0)
        def _():
            total[...] += term

        @pl.when(step == pairs - 1)
        def _():
            each = spans * piece_rows
            for chunk, (start, end) in enumerate(bounds(WIDTHS)):
                for part in range(count):
                    piece = total[part * each : (part + 1) * each, start:end]
                    outs[chunk * count + part][...] = piece.astype(BF)

    weight_spec = pl.BlockSpec((features, 2 * HD), lambda i: (0, i))
    token_spec = pl.BlockSpec((1, tokens, 2 * HD), lambda i: (i // per_group, 0, i % per_group))
    kv_spec = pl.BlockSpec((spans, keys, 2 * HD), lambda i: (0, 0, i))
    score_spec = pl.BlockSpec((1, spans, keys, 2 * SPAN), lambda i: (i, 0, 0, 0))
    stat_spec = pl.BlockSpec((1, 3, spans, 2 * SPAN), lambda i: (i, 0, 0, 0))
    parts = [(spans * piece_rows, w) for w in WIDTHS for _ in range(count)]
    outs = pl.pallas_call(
        kernel,
        grid=(pairs,),
        in_specs=[kv_spec, kv_spec, score_spec, score_spec]
        + [stat_spec] * devices
        + [weight_spec, weight_spec, token_spec, token_spec],
        out_specs=[token_spec, token_spec] + [pl.BlockSpec(p, lambda i: (0, 0)) for p in parts],
        out_shape=[jax.ShapeDtypeStruct((groups, tokens, width), BF)] * 2
        + [jax.ShapeDtypeStruct(p, BF) for p in parts],
        scratch_shapes=[
            pltpu.VMEM((count * spans * piece_rows, features), F32),
            pltpu.VMEM((count, spans, piece_rows, 2 * HD), F32),
            pltpu.VMEM((count, spans, piece_rows, 2 * HD), F32),
        ],
        compiler_params=PARAMS,
        cost_estimate=cost(
            4 * spans * keys * (features + 2 * SPAN) * all_width, 12 * spans * keys * all_width
        ),
        name="blend_spans",
    )(
        key_rows,
        value_rows,
        weights,
        grad_probs,
        *stats,
        key_weight,
        value_weight,
        shifted,
        grad_shift,
    )
    terms = [outs[2 + i * count : 2 + (i + 1) * count] for i in range(chunks)]
    return outs[0], outs[1], terms


def shards(query, d_attended, encoded, key_weight, value_weight, nbr_shard, nbr_row):
    planes = lax.axis_size("z")
    groups = lax.axis_size("x")
    columns = lax.axis_size("y")
    z, y, c = [lax.axis_index(axis).astype(I32) for axis in ("z", "y", "c")]
    spans, neighbours = nbr_shard.shape
    stored, quarter, features = encoded.shape
    rows = planes * stored * PIECE
    plane = z.reshape(1)

    shifted, grad_shift = move_tokens([query, d_attended], True)
    shifted = lax.all_gather(shifted, "x")
    grad_shift = lax.all_gather(grad_shift, "x")

    own = []
    for pieces in split_pieces(encoded, plane):
        own.append(
            jnp.concatenate([send_ring(piece, "z", k) for k, piece in enumerate(pieces)], 0)
        )

    picks = (nbr_shard * stored + nbr_row).reshape(spans * neighbours)
    picks, own[0] = lax.optimization_barrier((picks, own[0]))
    picks = lax.all_gather(picks, ("z", "c"), tiled=True).reshape(planes, 2, -1)
    picks = jnp.roll(jnp.roll(picks, -z, 0), -c, 1).transpose(1, 0, 2)
    store = picks // stored
    away_y = (y - store // 2 % columns) % columns
    away_z = (z - store // (2 * columns)) % planes
    first = away_y * rows + away_z * (stored * PIECE) + picks % stored * PIECE
    first = jnp.where(store % 2 == c, first, -columns * rows)
    target = (first[..., None] + jnp.arange(PIECE, dtype=I32)).reshape(2, -1)

    fetched = []
    for piece in own:
        gathered = [send_ring(piece, "y", a) for a in range(columns)]
        (theirs,) = pick_rows(gathered, target[1].reshape(-1, 1))
        picked = pick_rows(gathered, target[0].reshape(-1, 1), send_ring(theirs, "c", 1))
        fetched.append([send_ring(part, "z", r) for r, part in enumerate(picked)])

    key_rows, value_rows, weights, grad_probs, stats = score_spans(
        fetched, key_weight, value_weight, shifted, grad_shift
    )
    stats = [send_ring(stats, "x", away) for away in range(groups)]
    attended, d_query, terms = blend_spans(
        key_rows,
        value_rows,
        weights,
        grad_probs,
        stats,
        key_weight,
        value_weight,
        shifted,
        grad_shift,
    )
    attended = lax.psum_scatter(attended, "x", scatter_dimension=0)
    d_query = lax.psum_scatter(d_query, "x", scatter_dimension=0)

    returned = []
    for parts in terms:
        home = jnp.concatenate([send_ring(part, "z", -r) for r, part in enumerate(parts)], 0)
        sums = sum_rows([home, send_ring(home, "c", 1)], target.reshape(1, -1), columns, rows)
        whole = add_and_cut([send_ring(part, "y", -a) for a, part in enumerate(sums)], planes)
        returned.append([send_ring(part, "z", -k) for k, part in enumerate(whole)])
    d_encoded = join_pieces(returned, plane, stored, quarter, features)
    attended, d_query = move_tokens([attended, d_query], False)
    return (attended, d_query, d_encoded)


def solution(mesh):
    groups = mesh.devices.shape[1]
    fine = Mesh(mesh.devices.reshape(-1, LANES // 2, 2, groups), ("z", "y", "c", "x"))
    seq = ("z", "y", "c")
    placed = (
        P(seq, "x"),
        P(seq, "x"),
        P(seq, "x", None),
        P(),
        P(),
        P(seq, None),
        P(seq, None),
    )
    return jax.shard_map(
        shards,
        mesh=fine,
        in_specs=placed,
        out_specs=(P(seq, "x"), P(seq, "x"), P(seq, "x", None)),
        check_vma=False,
    )
```

```python
import jax
import jax.numpy as jnp
from jax import lax
from jax.experimental import pallas as pl
from jax.experimental.pallas import tpu as pltpu
from jax.sharding import Mesh, PartitionSpec as P

HD = 128
SPAN = 64
LANES = 8
PIECE = 4
WIDTHS = (512, 384)
BF = jnp.bfloat16
F32 = jnp.float32
I32 = jnp.int32
PARAMS = pltpu.CompilerParams(vmem_limit_bytes=48 * 1024 * 1024)


def matmul(left, right, left_dim=1, right_dim=0):
    return lax.dot_general(
        left, right, (((left_dim,), (right_dim,)), ((), ())), preferred_element_type=F32
    )


def bounds(widths):
    starts = [0]
    for width in widths:
        starts.append(starts[-1] + width)
    return list(zip(starts[:-1], starts[1:]))


def cost(flops, bytes_accessed, transcendentals=0):
    return pl.CostEstimate(
        flops=int(flops), bytes_accessed=int(bytes_accessed), transcendentals=int(transcendentals)
    )


def send_ring(array, axis, step):
    size = lax.axis_size(axis)
    if step % size == 0:
        return array
    return lax.ppermute(array, axis, [(i, (i + step) % size) for i in range(size)])


def piece_matrix(plane_ref, away, stored, quarter):
    plane = (plane_ref[0] + away) % LANES
    shape = (stored * PIECE, stored * quarter)
    to = lax.broadcasted_iota(I32, shape, 0)
    source = lax.broadcasted_iota(I32, shape, 1)
    token = (to // PIECE) * quarter + to % PIECE + plane * PIECE
    return (source == token).astype(F32).astype(BF)


def split_pieces(encoded, plane):
    stored, quarter, features = encoded.shape
    size = stored * quarter

    def kernel(plane_ref, enc_ref, *outs):
        order = jnp.concatenate(
            [piece_matrix(plane_ref, away, stored, quarter) for away in range(LANES)], 0
        )
        step = stored * PIECE
        pieces = matmul(order, enc_ref[...]).astype(BF)
        for away in range(LANES):
            outs[away][...] = pieces[away * step : (away + 1) * step]

    return pl.pallas_call(
        kernel,
        in_specs=[pl.BlockSpec(memory_space=pltpu.SMEM), pl.BlockSpec(memory_space=pltpu.VMEM)],
        out_shape=[jax.ShapeDtypeStruct((stored * PIECE, features), BF)] * LANES,
        compiler_params=PARAMS,
        cost_estimate=cost(2 * size * size * features, 4 * size * features),
        name="split_pieces",
    )(plane, encoded.reshape(size, features))


def join_pieces(parts, plane, stored, quarter, features):
    size = stored * quarter

    def kernel(plane_ref, *refs):
        out_ref = refs[-1]
        order = jnp.concatenate(
            [piece_matrix(plane_ref, away, stored, quarter) for away in range(LANES)], 0
        )
        pieces = jnp.concatenate([ref[...] for ref in refs[:-1]], 0)
        out_ref[...] = matmul(order, pieces, 0, 0).astype(BF)

    joined = pl.pallas_call(
        kernel,
        in_specs=[pl.BlockSpec(memory_space=pltpu.SMEM)]
        + [pl.BlockSpec(memory_space=pltpu.VMEM)] * LANES,
        out_shape=jax.ShapeDtypeStruct((size, features), BF),
        compiler_params=PARAMS,
        cost_estimate=cost(2 * size * size * features, 4 * size * features),
        name="join_pieces",
    )(plane, *parts)
    return joined.reshape(stored, quarter, features)


def pick_rows(stores, target, other=None):
    rows, width = stores[0].shape
    blocks = len(stores)
    picks = target.shape[0]
    parts = 1 if other is None else LANES
    each = picks // parts
    extra = [] if other is None else [other]

    def kernel(target_ref, *refs):
        total = None if other is None else refs[blocks][...].astype(F32)
        outs = refs[blocks + len(extra) :]
        column = lax.broadcasted_iota(I32, (picks, rows), 1)
        for block in range(blocks):
            one_hot = (column == target_ref[...] - block * rows).astype(F32).astype(BF)
            term = matmul(one_hot, refs[block][...])
            total = term if total is None else total + term
        for part in range(parts):
            outs[part][...] = total[part * each : (part + 1) * each].astype(BF)

    return pl.pallas_call(
        kernel,
        out_shape=[jax.ShapeDtypeStruct((each, width), BF)] * parts,
        compiler_params=PARAMS,
        cost_estimate=cost(
            2 * picks * blocks * rows * width, 2 * (picks + blocks * rows) * width
        ),
        name="pick_rows",
    )(target, *stores, *extra)


def sum_rows(terms, target, blocks, rows):
    width = terms[0].shape[1]
    picks = target.shape[1]
    count = len(terms)

    def kernel(target_ref, *refs):
        joined = jnp.concatenate([ref[...] for ref in refs[:count]], 0)
        row = lax.broadcasted_iota(I32, (rows, picks), 0)
        for block in range(blocks):
            one_hot = (row == target_ref[...] - block * rows).astype(F32).astype(BF)
            refs[count + block][...] = matmul(one_hot, joined).astype(BF)

    return pl.pallas_call(
        kernel,
        out_shape=[jax.ShapeDtypeStruct((rows, width), BF)] * blocks,
        compiler_params=PARAMS,
        cost_estimate=cost(
            2 * picks * blocks * rows * width, 2 * (picks + blocks * rows) * width
        ),
        name="sum_rows",
    )(target, *terms)


def add_and_cut(terms, parts):
    rows = terms[0][0].shape[0]
    each = rows // parts
    count = len(terms[0])
    features = sum(WIDTHS)

    def kernel(*refs):
        outs = refs[count * len(terms) :]
        for chunk, (start, end) in enumerate(bounds(WIDTHS)):
            mine = refs[chunk * count : (chunk + 1) * count]
            total = mine[0][...].astype(F32)
            for ref in mine[1:]:
                total = total + ref[...].astype(F32)
            for part in range(parts):
                outs[part][:, start:end] = total[part * each : (part + 1) * each].astype(BF)

    return pl.pallas_call(
        kernel,
        out_shape=[jax.ShapeDtypeStruct((each, features), BF)] * parts,
        compiler_params=PARAMS,
        cost_estimate=cost(count * rows * features, 2 * (count + 1) * rows * features),
        name="add_and_cut",
    )(*[term for chunk in terms for term in chunk])


def move_tokens(arrays, forward):
    tokens, width = arrays[0].shape[-2:]
    spans = tokens // SPAN
    packed = jax.ShapeDtypeStruct((2, tokens, width), BF)
    apart = [jax.ShapeDtypeStruct((tokens, width), BF)] * 2

    def kernel(*refs):
        to = lax.broadcasted_iota(I32, (SPAN, 2 * SPAN), 0)
        source = lax.broadcasted_iota(I32, (SPAN, 2 * SPAN), 1)
        step = SPAN - 1 if forward else 1
        order = (source == to + step).astype(F32).astype(BF)
        blank = jnp.zeros((SPAN, width), BF)
        pack = refs[-1] if forward else refs[0]
        for which, ref in enumerate(refs[:2] if forward else refs[1:]):
            for span in range(spans):
                low = span if forward else span - 1
                pair = []
                for u in (low, low + 1):
                    if not 0 <= u < spans:
                        pair.append(blank)
                    elif forward:
                        pair.append(ref[u * SPAN : (u + 1) * SPAN])
                    else:
                        pair.append(pack[which, u * SPAN : (u + 1) * SPAN])
                moved = matmul(order, jnp.concatenate(pair, 0)).astype(BF)
                if forward:
                    pack[which, span * SPAN : (span + 1) * SPAN] = moved
                else:
                    ref[span * SPAN : (span + 1) * SPAN] = moved

    return pl.pallas_call(
        kernel,
        out_shape=packed if forward else apart,
        compiler_params=PARAMS,
        cost_estimate=cost(8 * tokens * SPAN * width, 8 * tokens * width),
        name="move_tokens",
    )(*arrays)


def two_heads(pair):
    column = lax.broadcasted_iota(I32, (2 * SPAN, 2 * HD), 1)
    row = lax.broadcasted_iota(I32, (2 * SPAN, 2 * HD), 0)
    mask = ((column < HD) == (row < SPAN)).astype(F32).astype(BF)
    return jnp.concatenate([pair, pair], 0) * mask


def score_spans(half, fetched, key_weight, value_weight, moved):
    count = len(fetched[0])
    chunks = len(fetched)
    features, all_width = key_weight.shape
    groups, _, tokens, width = moved.shape
    spans = tokens // SPAN
    piece_rows = fetched[0][0].shape[0] // spans
    keys = count * piece_rows
    per_group = width // (2 * HD)
    pairs = all_width // (2 * HD) // 2
    base = half * pairs
    factor = HD ** (-0.5)

    def kernel(*refs):
        wk_ref, wv_ref, moved_ref = refs[count * chunks : count * chunks + 3]
        k_ref, v_ref, w_ref, gp_ref, stat_ref, rows_ref = refs[count * chunks + 3 :]

        @pl.when(pl.program_id(0) == 0)
        def _():
            for chunk, (start, end) in enumerate(bounds(WIDTHS)):
                parts = [ref[...] for ref in refs[chunk * count : (chunk + 1) * count]]
                rows_ref[:, start:end] = jnp.concatenate(parts, 0)

        rows = rows_ref[...]

        def project(weight):
            out = matmul(rows, weight).reshape(count, spans, piece_rows, 2 * HD)
            return out.transpose(1, 0, 2, 3).reshape(spans, keys, 2 * HD).astype(BF)

        k_ref[...] = project(wk_ref[...])
        v_ref[...] = project(wv_ref[...])
        for span in range(spans):
            tok = pl.ds(span * SPAN, SPAN)
            scores = matmul(k_ref[span], two_heads(moved_ref[0, 0, tok, :]), 1, 1) * factor
            grad = matmul(v_ref[span], two_heads(moved_ref[0, 1, tok, :]), 1, 1)
            top = jnp.max(scores, axis=0, keepdims=True)
            weights = jnp.exp(scores - top)
            w_ref[0, span] = weights
            gp_ref[0, span] = grad
            stat_ref[0, 0, pl.ds(span, 1), :] = top
            stat_ref[0, 1, pl.ds(span, 1), :] = jnp.sum(weights, axis=0, keepdims=True)
            stat_ref[0, 2, pl.ds(span, 1), :] = jnp.sum(weights * grad, axis=0, keepdims=True)

    whole = [
        pl.BlockSpec((spans * piece_rows, w), lambda i: (0, 0)) for w in WIDTHS for _ in range(count)
    ]
    weight_spec = pl.BlockSpec((features, 2 * HD), lambda i: (0, i + base))
    token_spec = pl.BlockSpec(
        (1, 2, tokens, 2 * HD), lambda i: ((i + base) // per_group, 0, 0, (i + base) % per_group)
    )
    kv_spec = pl.BlockSpec((spans, keys, 2 * HD), lambda i: (0, 0, i))
    score_spec = pl.BlockSpec((1, spans, keys, 2 * SPAN), lambda i: (i, 0, 0, 0))
    return pl.pallas_call(
        kernel,
        grid=(pairs,),
        in_specs=whole + [weight_spec, weight_spec, token_spec],
        out_specs=[
            kv_spec,
            kv_spec,
            score_spec,
            score_spec,
            pl.BlockSpec((1, 3, spans, 2 * SPAN), lambda i: (i, 0, 0, 0)),
        ],
        out_shape=[
            jax.ShapeDtypeStruct((spans, keys, all_width // 2), BF),
            jax.ShapeDtypeStruct((spans, keys, all_width // 2), BF),
            jax.ShapeDtypeStruct((pairs, spans, keys, 2 * SPAN), F32),
            jax.ShapeDtypeStruct((pairs, spans, keys, 2 * SPAN), F32),
            jax.ShapeDtypeStruct((pairs, 3, spans, 2 * SPAN), F32),
        ],
        scratch_shapes=[pltpu.VMEM((count * spans * piece_rows, features), BF)],
        compiler_params=PARAMS,
        cost_estimate=cost(
            2 * spans * keys * (features + SPAN) * all_width,
            4 * spans * keys * all_width,
            spans * keys * SPAN * 2 * pairs,
        ),
        name="score_spans",
    )(*[part for parts in fetched for part in parts], key_weight, value_weight, moved)


def blend_spans(half, scored, stats, key_weight, value_weight, moved, before):
    key_rows, value_rows, weights, grad_probs = scored
    features, all_width = key_weight.shape
    groups, _, tokens, width = moved.shape
    spans, keys, _ = key_rows.shape
    count = LANES
    chunks = len(WIDTHS)
    piece_rows = keys // count
    per_group = width // (2 * HD)
    pairs = all_width // (2 * HD) // 2
    base = half * pairs
    factor = HD ** (-0.5)
    devices = len(stats)

    def kernel(k_ref, v_ref, w_ref, gp_ref, *refs):
        stat_refs = refs[:devices]
        wk_ref, wv_ref, moved_ref = refs[devices : devices + 3]
        refs = refs[devices + 3 :]
        if half:
            before_ref, refs = refs[0], refs[2:]
        out_ref, outs = refs[0], refs[1:-3]
        total, gk_ref, gv_ref = refs[-3:]
        step = pl.program_id(0)

        own_top = stat_refs[0][0, 0]
        top = own_top
        for ref in stat_refs[1:]:
            top = jnp.maximum(top, ref[0, 0])
        sums = jnp.zeros_like(top)
        inner = jnp.zeros_like(top)
        for ref in stat_refs:
            scale = jnp.exp(ref[0, 0] - top)
            sums = sums + ref[0, 1] * scale
            inner = inner + ref[0, 2] * scale
        scale = jnp.exp(own_top - top) / sums
        inner = inner / sums

        for span in range(spans):
            tok = pl.ds(span * SPAN, SPAN)
            probs = w_ref[0, span] * scale[span : span + 1]
            probs_b = probs.astype(BF)
            grad_scores = (
                probs * (gp_ref[0, span] - inner[span : span + 1]) * factor
            ).astype(BF)
            k, v = k_ref[span], v_ref[span]
            blended = matmul(probs_b, v, 0, 0)
            shifted_grad = matmul(grad_scores, k, 0, 0)
            out_ref[0, 0, tok, :HD] = blended[:SPAN, :HD].astype(BF)
            out_ref[0, 0, tok, HD:] = blended[SPAN:, HD:].astype(BF)
            out_ref[0, 1, tok, :HD] = shifted_grad[:SPAN, :HD].astype(BF)
            out_ref[0, 1, tok, HD:] = shifted_grad[SPAN:, HD:].astype(BF)
            gk = matmul(grad_scores, two_heads(moved_ref[0, 0, tok, :]))
            gv = matmul(probs_b, two_heads(moved_ref[0, 1, tok, :]))
            gk_ref[:, span] = gk.reshape(count, piece_rows, 2 * HD)
            gv_ref[:, span] = gv.reshape(count, piece_rows, 2 * HD)

        flat = (count * spans * piece_rows, 2 * HD)
        term = matmul(gk_ref[...].reshape(flat).astype(BF), wk_ref[...], 1, 1)
        term = term + matmul(gv_ref[...].reshape(flat).astype(BF), wv_ref[...], 1, 1)

        @pl.when(step == 0)
        def _():
            total[...] = term + before_ref[...] if half else term

        @pl.when(step > 0)
        def _():
            total[...] += term

        @pl.when(step == pairs - 1)
        def _():
            if not half:
                outs[0][...] = total[...]
                return
            each = spans * piece_rows
            for chunk, (start, end) in enumerate(bounds(WIDTHS)):
                for part in range(count):
                    piece = total[part * each : (part + 1) * each, start:end]
                    outs[chunk * count + part][...] = piece.astype(BF)

    weight_spec = pl.BlockSpec((features, 2 * HD), lambda i: (0, i + base))
    token_spec = pl.BlockSpec(
        (1, 2, tokens, 2 * HD), lambda i: ((i + base) // per_group, 0, 0, (i + base) % per_group)
    )
    kv_spec = pl.BlockSpec((spans, keys, 2 * HD), lambda i: (0, 0, i))
    score_spec = pl.BlockSpec((1, spans, keys, 2 * SPAN), lambda i: (i, 0, 0, 0))
    stat_spec = pl.BlockSpec((1, 3, spans, 2 * SPAN), lambda i: (i, 0, 0, 0))
    whole = (count * spans * piece_rows, features)
    extra_specs, extra, aliases = [], [], {}
    parts, kind = [whole], F32
    if half:
        extra_specs = [pl.BlockSpec(whole, lambda i: (0, 0)), pl.BlockSpec(memory_space=pl.ANY)]
        extra = [before[1], before[0]]
        aliases = {4 + devices + 3 + 1: 0}
        parts, kind = [(spans * piece_rows, w) for w in WIDTHS for _ in range(count)], BF
    outs = pl.pallas_call(
        kernel,
        grid=(pairs,),
        in_specs=[kv_spec, kv_spec, score_spec, score_spec]
        + [stat_spec] * devices
        + [weight_spec, weight_spec, token_spec]
        + extra_specs,
        out_specs=[token_spec] + [pl.BlockSpec(p, lambda i: (0, 0)) for p in parts],
        out_shape=[jax.ShapeDtypeStruct((groups, 2, tokens, width), BF)]
        + [jax.ShapeDtypeStruct(p, kind) for p in parts],
        input_output_aliases=aliases,
        scratch_shapes=[
            pltpu.VMEM((count * spans * piece_rows, features), F32),
            pltpu.VMEM((count, spans, piece_rows, 2 * HD), F32),
            pltpu.VMEM((count, spans, piece_rows, 2 * HD), F32),
        ],
        compiler_params=PARAMS,
        cost_estimate=cost(
            2 * spans * keys * (features + 2 * SPAN) * all_width, 6 * spans * keys * all_width
        ),
        name="blend_spans",
    )(key_rows, value_rows, weights, grad_probs, *stats, key_weight, value_weight, moved, *extra)
    if not half:
        return outs
    return outs[0], [outs[1 + i * count : 1 + (i + 1) * count] for i in range(chunks)]


def after(value, *others):
    return lax.optimization_barrier((value, *others))[0]


def shards(query, d_attended, encoded, key_weight, value_weight, nbr_shard, nbr_row):
    planes = lax.axis_size("z")
    groups = lax.axis_size("x")
    columns = lax.axis_size("y")
    z, y, c = [lax.axis_index(axis).astype(I32) for axis in ("z", "y", "c")]
    spans, neighbours = nbr_shard.shape
    stored, quarter, features = encoded.shape
    rows = planes * stored * PIECE
    plane = z.reshape(1)

    pieces = split_pieces(encoded, plane)

    moved = move_tokens([after(query, pieces[0]), d_attended], True)
    moved = lax.all_gather(moved, "x")

    pieces = [send_ring(piece, "z", k) for k, piece in enumerate(pieces)]
    own = [
        jnp.concatenate([piece[:, start:end] for piece in pieces], 0)
        for start, end in bounds(WIDTHS)
    ]

    picks = (nbr_shard * stored + nbr_row).reshape(spans * neighbours)
    picks = lax.all_gather(after(picks, own[0]), ("z", "c"), tiled=True).reshape(planes, 2, -1)
    picks = jnp.roll(jnp.roll(picks, -z, 0), -c, 1).transpose(1, 0, 2)
    store = picks // stored
    away_y = (y - store // 2 % columns) % columns
    away_z = (z - store // (2 * columns)) % planes
    first = away_y * rows + away_z * (stored * PIECE) + picks % stored * PIECE
    first = jnp.where(store % 2 == c, first, -columns * rows)
    target = (first[..., None] + jnp.arange(PIECE, dtype=I32)).reshape(2, -1)

    fetched, gathered = [], []
    for piece in own:
        piece = after(piece, *gathered)
        gathered = [send_ring(piece, "y", a) for a in range(columns)]
        (theirs,) = pick_rows(gathered, target[1].reshape(-1, 1))
        picked = pick_rows(gathered, target[0].reshape(-1, 1), send_ring(theirs, "c", 1))
        fetched.append([send_ring(part, "z", r) for r, part in enumerate(picked)])

    scored, stats = [], []
    for half in range(2):
        *score, stat = score_spans(half, fetched, key_weight, value_weight, moved)
        scored.append(score)
        stats.append([send_ring(stat, "x", away) for away in range(groups)])
    result = None
    for half in range(2):
        result = blend_spans(
            half, scored[half], stats[half], key_weight, value_weight, moved, result
        )
    output, terms = result
    output = lax.psum_scatter(output, "x", scatter_dimension=0)

    whole, home = [], []
    for parts in terms:
        parts = [after(part, *home) for part in parts] if home else parts
        home = [send_ring(part, "z", -r) for r, part in enumerate(parts)]
        joined = jnp.concatenate(home, 0)
        sums = sum_rows([joined, send_ring(joined, "c", 1)], target.reshape(1, -1), columns, rows)
        whole.append([send_ring(part, "y", -a) for a, part in enumerate(sums)])
    returned = add_and_cut(whole, planes)
    returned = [send_ring(part, "z", -k) for k, part in enumerate(returned)]
    d_encoded = join_pieces(returned, plane, stored, quarter, features)
    attended, d_query = move_tokens([output], False)
    return (attended, d_query, d_encoded)


def solution(mesh):
    groups = mesh.devices.shape[1]
    fine = Mesh(mesh.devices.reshape(-1, LANES // 2, 2, groups), ("z", "y", "c", "x"))
    seq = ("z", "y", "c")
    placed = (
        P(seq, "x"),
        P(seq, "x"),
        P(seq, "x", None),
        P(),
        P(),
        P(seq, None),
        P(seq, None),
    )
    return jax.shard_map(
        shards,
        mesh=fine,
        in_specs=placed,
        out_specs=(P(seq, "x"), P(seq, "x"), P(seq, "x", None)),
        check_vma=False,
    )
```

```python
import jax
import jax.numpy as jnp
from jax import lax
from jax.experimental import pallas as pl
from jax.experimental.pallas import tpu as pltpu
from jax.sharding import Mesh, PartitionSpec as P

HD = 128
SPAN = 64
PIECE = 4
PART = 256
BF = jnp.bfloat16
F32 = jnp.float32
I32 = jnp.int32
PARAMS = pltpu.CompilerParams(vmem_limit_bytes=48 * 1024 * 1024)


def matmul(left, right, left_dim=1, right_dim=0):
    return lax.dot_general(
        left, right, (((left_dim,), (right_dim,)), ((), ())), preferred_element_type=F32
    )


def cost(flops, bytes_accessed, transcendentals=0):
    return pl.CostEstimate(
        flops=int(flops), bytes_accessed=int(bytes_accessed), transcendentals=int(transcendentals)
    )


def send_ring(array, axis, step):
    size = lax.axis_size(axis)
    if step % size == 0:
        return array
    return lax.ppermute(array, axis, [(i, (i + step) % size) for i in range(size)])


def cuts(features):
    return [
        (part, start, min(start + PART, features))
        for part, start in enumerate(range(0, features, PART))
    ]


def piece_matrix(stored, quarter):
    shape = (stored * quarter, stored * quarter)
    to = lax.broadcasted_iota(I32, shape, 0)
    source = lax.broadcasted_iota(I32, shape, 1)
    token = to % stored * quarter + to // stored
    return (source == token).astype(F32).astype(BF)


def split_pieces(encoded, planes, columns):
    stored, quarter, features = encoded.shape
    size = stored * quarter

    def kernel(enc_ref, out_ref):
        pieces = matmul(piece_matrix(stored, quarter), enc_ref[...]).astype(BF)
        for plane in range(planes):
            for token in range(PIECE):
                first = (plane * PIECE + token) * stored
                for part, start, end in cuts(features):
                    at = token * PART
                    block = pieces[first : first + stored, start:end]
                    out_ref[plane * columns + part, :, at : at + end - start] = block
                    if end - start < PART:
                        blank = jnp.zeros((stored, PART - end + start), BF)
                        out_ref[plane * columns + part, :, at + end - start : at + PART] = blank

    return pl.pallas_call(
        kernel,
        out_shape=jax.ShapeDtypeStruct((planes * columns, stored, PIECE * PART), BF),
        compiler_params=PARAMS,
        cost_estimate=cost(2 * size * size * features, 4 * size * features),
        name="split_pieces",
    )(encoded.reshape(size, features))


def join_pieces(parts, planes, columns, quarter, features):
    stored = parts.shape[1]
    size = stored * quarter

    def kernel(part_ref, out_ref, rows_ref):
        for plane in range(planes):
            for token in range(PIECE):
                first = (plane * PIECE + token) * stored
                for part, start, end in cuts(features):
                    at = token * PART
                    block = part_ref[plane * columns + part, :, at : at + end - start]
                    rows_ref[first : first + stored, start:end] = block
        order = piece_matrix(stored, quarter)
        out_ref[...] = matmul(order, rows_ref[...], 0, 0).astype(BF)

    joined = pl.pallas_call(
        kernel,
        out_shape=jax.ShapeDtypeStruct((size, features), BF),
        scratch_shapes=[pltpu.VMEM((size, features), BF)],
        compiler_params=PARAMS,
        cost_estimate=cost(2 * size * size * features, 4 * size * features),
        name="join_pieces",
    )(parts)
    return joined.reshape(stored, quarter, features)


def pick_rows(store, target, other=None):
    rows, width = store.shape
    picks = target.shape[0]
    last = other is not None

    def kernel(target_ref, store_ref, *refs):
        column = lax.broadcasted_iota(I32, (picks, rows), 1)
        one_hot = (column == target_ref[...]).astype(F32).astype(BF)
        if not last:
            refs[0][...] = matmul(one_hot, store_ref[...]).astype(BF)
            return
        other_ref, out_ref, spread = refs
        for token in range(PIECE):
            for half in range(PART // HD):
                at = token * PART + half * HD
                total = matmul(one_hot, store_ref[:, at : at + HD])
                total = total + other_ref[:, at : at + HD].astype(F32)
                spread[half, pl.ds(token, picks, stride=PIECE), :] = total
        for half in range(PART // HD):
            out_ref[:, half * HD : (half + 1) * HD] = spread[half].astype(BF)

    shape = (picks * PIECE, PART) if last else (picks, width)
    return pl.pallas_call(
        kernel,
        out_shape=jax.ShapeDtypeStruct(shape, BF),
        scratch_shapes=[pltpu.VMEM((PART // HD, picks * PIECE, HD), F32)] if last else [],
        compiler_params=PARAMS,
        cost_estimate=cost(2 * picks * rows * width, 2 * (picks + rows) * width),
        name="pick_rows",
    )(target, store, *([other] if last else []))


def sum_rows(terms, target, rows):
    count = len(terms)
    picks = target.shape[1] // count
    width = PIECE * PART

    def kernel(target_ref, *refs):
        out_ref, spread = refs[count:]
        row = lax.broadcasted_iota(I32, (rows, count * picks), 0)
        one_hot = (row == target_ref[...]).astype(F32).astype(BF)
        for half in range(PART // HD):
            for which in range(count):
                spread[which, half] = refs[which][:, half * HD : (half + 1) * HD].astype(F32)
        for token in range(PIECE):
            for half in range(PART // HD):
                at = token * PART + half * HD
                joined = [
                    spread[which, half, pl.ds(token, picks, stride=PIECE), :].astype(BF)
                    for which in range(count)
                ]
                out_ref[:, at : at + HD] = matmul(one_hot, jnp.concatenate(joined, 0)).astype(BF)

    return pl.pallas_call(
        kernel,
        out_shape=jax.ShapeDtypeStruct((rows, width), BF),
        scratch_shapes=[pltpu.VMEM((count, PART // HD, picks * PIECE, HD), F32)],
        compiler_params=PARAMS,
        cost_estimate=cost(2 * count * picks * rows * width, 2 * (count * picks + rows) * width),
        name="sum_rows",
    )(target, *terms)


def move_tokens(arrays, forward):
    tokens, width = arrays[0].shape[-2:]
    spans = tokens // SPAN
    packed = jax.ShapeDtypeStruct((2, tokens, width), BF)
    apart = [jax.ShapeDtypeStruct((tokens, width), BF)] * 2

    def kernel(*refs):
        to = lax.broadcasted_iota(I32, (SPAN, 2 * SPAN), 0)
        source = lax.broadcasted_iota(I32, (SPAN, 2 * SPAN), 1)
        step = SPAN - 1 if forward else 1
        order = (source == to + step).astype(F32).astype(BF)
        blank = jnp.zeros((SPAN, width), BF)
        pack = refs[-1] if forward else refs[0]
        for which, ref in enumerate(refs[:2] if forward else refs[1:]):
            for span in range(spans):
                low = span if forward else span - 1
                pair = []
                for u in (low, low + 1):
                    if not 0 <= u < spans:
                        pair.append(blank)
                    elif forward:
                        pair.append(ref[u * SPAN : (u + 1) * SPAN])
                    else:
                        pair.append(pack[which, u * SPAN : (u + 1) * SPAN])
                moved = matmul(order, jnp.concatenate(pair, 0)).astype(BF)
                if forward:
                    pack[which, span * SPAN : (span + 1) * SPAN] = moved
                else:
                    ref[span * SPAN : (span + 1) * SPAN] = moved

    return pl.pallas_call(
        kernel,
        out_shape=packed if forward else apart,
        compiler_params=PARAMS,
        cost_estimate=cost(8 * tokens * SPAN * width, 8 * tokens * width),
        name="move_tokens",
    )(*arrays)


def two_heads(pair):
    column = lax.broadcasted_iota(I32, (2 * SPAN, 2 * HD), 1)
    row = lax.broadcasted_iota(I32, (2 * SPAN, 2 * HD), 0)
    mask = ((column < HD) == (row < SPAN)).astype(F32).astype(BF)
    return jnp.concatenate([pair, pair], 0) * mask


def score_spans(fetched, key_weight, value_weight, moved):
    count, columns = fetched.shape[:2]
    features, all_width = key_weight.shape
    groups, _, tokens, width = moved.shape
    spans = tokens // SPAN
    piece_rows = fetched.shape[2] // spans
    keys = count * piece_rows
    per_group = width // (2 * HD)
    pairs = all_width // (2 * HD)
    factor = HD ** (-0.5)

    def kernel(
        part_ref, wk_ref, wv_ref, moved_ref, k_ref, v_ref, w_ref, gp_ref, stat_ref, rows_ref
    ):
        @pl.when(pl.program_id(0) == 0)
        def _():
            for part, start, end in cuts(features):
                block = part_ref[:, part, :, : end - start]
                rows_ref[:, start:end] = block.reshape(count * spans * piece_rows, end - start)

        rows = rows_ref[...]

        def project(weight):
            out = matmul(rows, weight).reshape(count, spans, piece_rows, 2 * HD)
            return out.transpose(1, 0, 2, 3).reshape(spans, keys, 2 * HD).astype(BF)

        k_ref[...] = project(wk_ref[...])
        v_ref[...] = project(wv_ref[...])
        for span in range(spans):
            tok = pl.ds(span * SPAN, SPAN)
            scores = matmul(k_ref[span], two_heads(moved_ref[0, 0, tok, :]), 1, 1) * factor
            grad = matmul(v_ref[span], two_heads(moved_ref[0, 1, tok, :]), 1, 1)
            top = jnp.max(scores, axis=0, keepdims=True)
            weights = jnp.exp(scores - top)
            w_ref[0, span] = weights
            gp_ref[0, span] = grad
            stat_ref[0, 0, pl.ds(span, 1), :] = top
            stat_ref[0, 1, pl.ds(span, 1), :] = jnp.sum(weights, axis=0, keepdims=True)
            stat_ref[0, 2, pl.ds(span, 1), :] = jnp.sum(weights * grad, axis=0, keepdims=True)

    whole = pl.BlockSpec(fetched.shape, lambda i: (0, 0, 0, 0))
    weight_spec = pl.BlockSpec((features, 2 * HD), lambda i: (0, i))
    token_spec = pl.BlockSpec(
        (1, 2, tokens, 2 * HD), lambda i: (i // per_group, 0, 0, i % per_group)
    )
    kv_spec = pl.BlockSpec((spans, keys, 2 * HD), lambda i: (0, 0, i))
    score_spec = pl.BlockSpec((1, spans, keys, 2 * SPAN), lambda i: (i, 0, 0, 0))
    return pl.pallas_call(
        kernel,
        grid=(pairs,),
        in_specs=[whole, weight_spec, weight_spec, token_spec],
        out_specs=[
            kv_spec,
            kv_spec,
            score_spec,
            score_spec,
            pl.BlockSpec((1, 3, spans, 2 * SPAN), lambda i: (i, 0, 0, 0)),
        ],
        out_shape=[
            jax.ShapeDtypeStruct((spans, keys, all_width), BF),
            jax.ShapeDtypeStruct((spans, keys, all_width), BF),
            jax.ShapeDtypeStruct((pairs, spans, keys, 2 * SPAN), F32),
            jax.ShapeDtypeStruct((pairs, spans, keys, 2 * SPAN), F32),
            jax.ShapeDtypeStruct((pairs, 3, spans, 2 * SPAN), F32),
        ],
        scratch_shapes=[pltpu.VMEM((count * spans * piece_rows, features), BF)],
        compiler_params=PARAMS,
        cost_estimate=cost(
            4 * spans * keys * (features + SPAN) * all_width,
            8 * spans * keys * all_width,
            spans * keys * SPAN * 2 * pairs,
        ),
        name="score_spans",
    )(fetched, key_weight, value_weight, moved)


def blend_spans(scored, stats, key_weight, value_weight, moved, planes, columns):
    key_rows, value_rows, weights, grad_probs = scored
    features, all_width = key_weight.shape
    groups, _, tokens, width = moved.shape
    spans, keys, _ = key_rows.shape
    count = planes
    piece_rows = keys // count
    per_group = width // (2 * HD)
    pairs = all_width // (2 * HD)
    factor = HD ** (-0.5)
    devices = len(stats)

    def kernel(k_ref, v_ref, w_ref, gp_ref, *refs):
        stat_refs = refs[:devices]
        wk_ref, wv_ref, moved_ref, out_ref, part_ref, total, gk_ref, gv_ref = refs[devices:]
        step = pl.program_id(0)

        own_top = stat_refs[0][0, 0]
        top = own_top
        for ref in stat_refs[1:]:
            top = jnp.maximum(top, ref[0, 0])
        sums = jnp.zeros_like(top)
        inner = jnp.zeros_like(top)
        for ref in stat_refs:
            scale = jnp.exp(ref[0, 0] - top)
            sums = sums + ref[0, 1] * scale
            inner = inner + ref[0, 2] * scale
        scale = jnp.exp(own_top - top) / sums
        inner = inner / sums

        for span in range(spans):
            tok = pl.ds(span * SPAN, SPAN)
            probs = w_ref[0, span] * scale[span : span + 1]
            probs_b = probs.astype(BF)
            grad_scores = (
                probs * (gp_ref[0, span] - inner[span : span + 1]) * factor
            ).astype(BF)
            k, v = k_ref[span], v_ref[span]
            blended = matmul(probs_b, v, 0, 0)
            shifted_grad = matmul(grad_scores, k, 0, 0)
            out_ref[0, 0, tok, :HD] = blended[:SPAN, :HD].astype(BF)
            out_ref[0, 0, tok, HD:] = blended[SPAN:, HD:].astype(BF)
            out_ref[0, 1, tok, :HD] = shifted_grad[:SPAN, :HD].astype(BF)
            out_ref[0, 1, tok, HD:] = shifted_grad[SPAN:, HD:].astype(BF)
            gk = matmul(grad_scores, two_heads(moved_ref[0, 0, tok, :]))
            gv = matmul(probs_b, two_heads(moved_ref[0, 1, tok, :]))
            gk_ref[:, span] = gk.reshape(count, piece_rows, 2 * HD)
            gv_ref[:, span] = gv.reshape(count, piece_rows, 2 * HD)

        flat = (count * spans * piece_rows, 2 * HD)
        term = matmul(gk_ref[...].reshape(flat).astype(BF), wk_ref[...], 1, 1)
        term = term + matmul(gv_ref[...].reshape(flat).astype(BF), wv_ref[...], 1, 1)

        @pl.when(step == 0)
        def _():
            total[...] = term

        @pl.when(step > 0)
        def _():
            total[...] += term

        @pl.when(step == pairs - 1)
        def _():
            each = spans * piece_rows
            for part, start, end in cuts(features):
                for plane in range(count):
                    piece = total[plane * each : (plane + 1) * each, start:end].astype(BF)
                    part_ref[plane, part, :, : end - start] = piece
                    if end - start < PART:
                        blank = jnp.zeros((each, PART - end + start), BF)
                        part_ref[plane, part, :, end - start :] = blank

    weight_spec = pl.BlockSpec((features, 2 * HD), lambda i: (0, i))
    token_spec = pl.BlockSpec(
        (1, 2, tokens, 2 * HD), lambda i: (i // per_group, 0, 0, i % per_group)
    )
    kv_spec = pl.BlockSpec((spans, keys, 2 * HD), lambda i: (0, 0, i))
    score_spec = pl.BlockSpec((1, spans, keys, 2 * SPAN), lambda i: (i, 0, 0, 0))
    stat_spec = pl.BlockSpec((1, 3, spans, 2 * SPAN), lambda i: (i, 0, 0, 0))
    result = (count, columns, spans * piece_rows, PART)
    return pl.pallas_call(
        kernel,
        grid=(pairs,),
        in_specs=[kv_spec, kv_spec, score_spec, score_spec]
        + [stat_spec] * devices
        + [weight_spec, weight_spec, token_spec],
        out_specs=[token_spec, pl.BlockSpec(result, lambda i: (0, 0, 0, 0))],
        out_shape=[
            jax.ShapeDtypeStruct((groups, 2, tokens, width), BF),
            jax.ShapeDtypeStruct(result, BF),
        ],
        scratch_shapes=[
            pltpu.VMEM((count * spans * piece_rows, features), F32),
            pltpu.VMEM((count, spans, piece_rows, 2 * HD), F32),
            pltpu.VMEM((count, spans, piece_rows, 2 * HD), F32),
        ],
        compiler_params=PARAMS,
        cost_estimate=cost(
            4 * spans * keys * (features + 2 * SPAN) * all_width, 12 * spans * keys * all_width
        ),
        name="blend_spans",
    )(key_rows, value_rows, weights, grad_probs, *stats, key_weight, value_weight, moved)


def after(value, *others):
    return lax.optimization_barrier((value, *others))[0]


def shards(query, d_attended, encoded, key_weight, value_weight, nbr_shard, nbr_row):
    planes = lax.axis_size("z")
    columns = lax.axis_size("y")
    groups = lax.axis_size("x")
    c = lax.axis_index("c").astype(I32)
    spans, neighbours = nbr_shard.shape
    stored, quarter, features = encoded.shape
    lanes = planes * columns
    rows = lanes * stored
    requested = spans * neighbours

    pieces = split_pieces(encoded, planes, columns)
    store = lax.all_to_all(pieces, ("z", "y"), 0, 0, tiled=True).reshape(rows, PIECE * PART)

    moved = move_tokens([after(query, pieces), d_attended], True)
    moved = lax.all_gather(moved, "x")

    picks = (nbr_shard * stored + nbr_row).reshape(requested)
    picks = lax.all_gather(after(picks, pieces), ("z", "y", "c"), tiled=True)
    picks = picks.reshape(lanes, 2, requested)
    picks = jnp.stack([jnp.where(c == 0, picks[:, i], picks[:, 1 - i]) for i in range(2)])
    owner = picks // stored
    target = jnp.where(owner % 2 == c, owner // 2 * stored + picks % stored, -1)
    target = target.reshape(2, lanes * requested)

    theirs = pick_rows(store, target[1].reshape(-1, 1))
    picked = pick_rows(store, target[0].reshape(-1, 1), send_ring(theirs, "c", 1))
    picked = picked.reshape(lanes, requested * PIECE, PART)
    fetched = lax.all_to_all(picked, ("z", "y"), 0, 0, tiled=True)

    *scored, stat = score_spans(
        fetched.reshape(planes, columns, requested * PIECE, PART), key_weight, value_weight, moved
    )
    stats = [send_ring(stat, "x", away) for away in range(groups)]
    output, terms = blend_spans(scored, stats, key_weight, value_weight, moved, planes, columns)
    output = lax.psum_scatter(output, "x", scatter_dimension=0)

    terms = terms.reshape(lanes, requested * PIECE, PART)
    home = lax.all_to_all(terms, ("z", "y"), 0, 0, tiled=True)
    home = home.reshape(lanes * requested * PIECE, PART)
    sums = sum_rows([home, send_ring(home, "c", 1)], target.reshape(1, -1), rows)
    returned = sums.reshape(lanes, stored, PIECE * PART)
    returned = lax.all_to_all(returned, ("z", "y"), 0, 0, tiled=True)
    d_encoded = join_pieces(returned, planes, columns, quarter, features)
    attended, d_query = move_tokens([output], False)
    return (attended, d_query, d_encoded)


def solution(mesh):
    groups = mesh.devices.shape[1]
    fine = Mesh(mesh.devices.reshape(-1, 4, 2, groups), ("z", "y", "c", "x"))
    seq = ("z", "y", "c")
    placed = (
        P(seq, "x"),
        P(seq, "x"),
        P(seq, "x", None),
        P(),
        P(),
        P(seq, None),
        P(seq, None),
    )
    return jax.shard_map(
        shards,
        mesh=fine,
        in_specs=placed,
        out_specs=(P(seq, "x"), P(seq, "x"), P(seq, "x", None)),
        check_vma=False,
    )
```

```python
import jax
import jax.numpy as jnp
from jax import lax
from jax.experimental import pallas as pl
from jax.experimental.pallas import tpu as pltpu
from jax.sharding import Mesh, PartitionSpec as P

HD = 128
SPAN = 64
NBRS = 2
SPARE = 128
BF = jnp.bfloat16
F32 = jnp.float32
I32 = jnp.int32
PARAMS = pltpu.CompilerParams(vmem_limit_bytes=48 * 1024 * 1024)


def matmul(left, right, left_dim=1, right_dim=0):
    return lax.dot_general(
        left, right, (((left_dim,), (right_dim,)), ((), ())), preferred_element_type=F32
    )


def cost(flops, bytes_accessed, transcendentals=0):
    return pl.CostEstimate(
        flops=int(flops), bytes_accessed=int(bytes_accessed), transcendentals=int(transcendentals)
    )


def send_ring(array, axis, step):
    size = lax.axis_size(axis)
    if step % size == 0:
        return array
    return lax.ppermute(array, axis, [(i, (i + step) % size) for i in range(size)])


def piece_matrix(stored, quarter):
    shape = (stored * quarter, stored * quarter)
    to = lax.broadcasted_iota(I32, shape, 0)
    source = lax.broadcasted_iota(I32, shape, 1)
    token = to % stored * quarter + to // stored
    return (source == token).astype(F32).astype(BF)


def split_pieces(encoded, nbr_shard, nbr_row):
    stored, quarter, features = encoded.shape
    size = stored * quarter
    spans, neighbours = nbr_shard.shape

    def kernel(enc_ref, shard_ref, row_ref, out_ref, names):
        names[...] = jnp.zeros_like(names)
        names[:spans, :neighbours] = shard_ref[...].astype(F32)
        names[:spans, neighbours : 2 * neighbours] = row_ref[...].astype(F32)
        named = names[...].astype(BF)
        pieces = matmul(piece_matrix(stored, quarter), enc_ref[...]).astype(BF)
        for token in range(quarter):
            out_ref[token, :, :features] = pieces[token * stored : (token + 1) * stored]
            out_ref[token, :, features:] = named

    return pl.pallas_call(
        kernel,
        out_shape=jax.ShapeDtypeStruct((quarter, stored, features + SPARE), BF),
        scratch_shapes=[pltpu.VMEM((stored, SPARE), F32)],
        compiler_params=PARAMS,
        cost_estimate=cost(2 * size * size * features, 4 * size * features),
        name="split_pieces",
    )(encoded.reshape(size, features), nbr_shard, nbr_row)


def join_pieces(parts):
    quarter, stored, features = parts.shape
    size = stored * quarter

    def kernel(part_ref, out_ref):
        out_ref[...] = matmul(piece_matrix(stored, quarter), part_ref[...], 0, 0).astype(BF)

    joined = pl.pallas_call(
        kernel,
        out_shape=jax.ShapeDtypeStruct((size, features), BF),
        compiler_params=PARAMS,
        cost_estimate=cost(2 * size * size * features, 4 * size * features),
        name="join_pieces",
    )(parts.reshape(size, features))
    return joined.reshape(stored, quarter, features)


def message_rows(picks, blocks):
    return -(-picks * blocks // 8) * 8


def pick_rows(stores, target, lanes, picks, features):
    rows = stores[0].shape[0]
    each = target.shape[0] // lanes
    blocks = features // HD
    length = message_rows(picks, blocks)

    def kernel(target_ref, own_ref, other_ref, out_ref, spread):
        column = lax.broadcasted_iota(I32, (lanes * each, rows), 1)
        own_hot = (column == target_ref[...]).astype(F32).astype(BF)
        other_hot = (column == target_ref[...] - rows).astype(F32).astype(BF)
        spread[:, length - 8 :, :] = jnp.zeros((lanes, 8, HD), F32)
        for block in range(blocks):
            cols = slice(block * HD, (block + 1) * HD)
            total = matmul(own_hot, own_ref[:, cols]) + matmul(other_hot, other_ref[:, cols])
            for lane in range(lanes):
                part = total[lane * each : lane * each + picks]
                spread[lane, pl.ds(block, picks, stride=blocks), :] = part
        out_ref[...] = spread[...].astype(BF)

    return pl.pallas_call(
        kernel,
        out_shape=jax.ShapeDtypeStruct((lanes, length, HD), BF),
        scratch_shapes=[pltpu.VMEM((lanes, length, HD), F32)],
        compiler_params=PARAMS,
        cost_estimate=cost(
            4 * lanes * each * rows * features, 2 * (lanes * each + 2 * rows) * features
        ),
        name="pick_rows",
    )(target, *stores)


def sum_rows(terms, target, picks, rows, features):
    count = len(terms)
    lanes, length, _ = terms[0].shape
    each = target.shape[1] // (count * lanes)
    blocks = features // HD
    size = count * lanes * each

    def kernel(target_ref, *refs):
        out_ref, spread, flat = refs[count:]
        row = lax.broadcasted_iota(I32, (rows, size), 0)
        one_hot = (row == target_ref[...]).astype(F32).astype(BF)
        for which in range(count):
            spread[which] = refs[which][...].astype(F32)
        for lane in range(count * lanes):
            low = lane * each + picks // 8 * 8
            flat[low : (lane + 1) * each, :] = jnp.zeros(((lane + 1) * each - low, HD), F32)
        for block in range(blocks):
            for which in range(count):
                for lane in range(lanes):
                    at = (which * lanes + lane) * each
                    flat[at : at + picks, :] = spread[
                        which, lane, pl.ds(block, picks, stride=blocks), :
                    ]
            total = matmul(one_hot, flat[...].astype(BF))
            out_ref[:, block * HD : (block + 1) * HD] = total.astype(BF)

    return pl.pallas_call(
        kernel,
        out_shape=jax.ShapeDtypeStruct((rows, features), BF),
        scratch_shapes=[pltpu.VMEM((count, lanes, length, HD), F32), pltpu.VMEM((size, HD), F32)],
        compiler_params=PARAMS,
        cost_estimate=cost(2 * size * rows * features, 2 * (size + rows) * features),
        name="sum_rows",
    )(target, *terms)


def move_tokens(arrays, forward):
    tokens, width = arrays[0].shape[-2:]
    spans = tokens // SPAN
    packed = jax.ShapeDtypeStruct((2, tokens, width), BF)
    apart = [jax.ShapeDtypeStruct((tokens, width), BF)] * 2

    def kernel(*refs):
        to = lax.broadcasted_iota(I32, (SPAN, 2 * SPAN), 0)
        source = lax.broadcasted_iota(I32, (SPAN, 2 * SPAN), 1)
        step = SPAN - 1 if forward else 1
        order = (source == to + step).astype(F32).astype(BF)
        blank = jnp.zeros((SPAN, width), BF)
        pack = refs[-1] if forward else refs[0]
        for which, ref in enumerate(refs[:2] if forward else refs[1:]):
            for span in range(spans):
                low = span if forward else span - 1
                pair = []
                for u in (low, low + 1):
                    if not 0 <= u < spans:
                        pair.append(blank)
                    elif forward:
                        pair.append(ref[u * SPAN : (u + 1) * SPAN])
                    else:
                        pair.append(pack[which, u * SPAN : (u + 1) * SPAN])
                moved = matmul(order, jnp.concatenate(pair, 0)).astype(BF)
                if forward:
                    pack[which, span * SPAN : (span + 1) * SPAN] = moved
                else:
                    ref[span * SPAN : (span + 1) * SPAN] = moved

    return pl.pallas_call(
        kernel,
        out_shape=packed if forward else apart,
        compiler_params=PARAMS,
        cost_estimate=cost(8 * tokens * SPAN * width, 8 * tokens * width),
        name="move_tokens",
    )(*arrays)


def two_heads(pair):
    column = lax.broadcasted_iota(I32, (2 * SPAN, 2 * HD), 1)
    row = lax.broadcasted_iota(I32, (2 * SPAN, 2 * HD), 0)
    mask = ((column < HD) == (row < SPAN)).astype(F32).astype(BF)
    return jnp.concatenate([pair, pair], 0) * mask


def score_spans(fetched, key_weight, value_weight, moved):
    lanes = fetched.shape[0]
    features, all_width = key_weight.shape
    groups, _, tokens, width = moved.shape
    spans = tokens // SPAN
    keys = lanes * NBRS
    count = keys // 8
    blocks = features // HD
    per_group = width // (2 * HD)
    pairs = all_width // (2 * HD)
    factor = HD ** (-0.5)

    def kernel(
        part_ref,
        wk_ref,
        wv_ref,
        moved_ref,
        k_ref,
        v_ref,
        w_ref,
        gp_ref,
        stat_ref,
        rows_ref,
        spread,
        flat,
    ):
        @pl.when(pl.program_id(0) == 0)
        def _():
            spread[...] = part_ref[...].astype(F32)
            for block in range(blocks):
                for lane in range(lanes):
                    for nbr in range(NBRS):
                        to = lane * NBRS // 8 * 8 * spans + lane * NBRS % 8 + nbr
                        flat[pl.ds(to, spans, stride=8), :] = spread[
                            lane, pl.ds(nbr * blocks + block, spans, stride=NBRS * blocks), :
                        ]
                rows_ref[:, block * HD : (block + 1) * HD] = flat[...].astype(BF)

        rows = rows_ref[...]

        def project(weight):
            out = matmul(rows, weight).reshape(count, spans, 8, 2 * HD)
            return out.transpose(1, 0, 2, 3).reshape(spans, keys, 2 * HD).astype(BF)

        k_ref[...] = project(wk_ref[...])
        v_ref[...] = project(wv_ref[...])
        for span in range(spans):
            tok = pl.ds(span * SPAN, SPAN)
            scores = matmul(k_ref[span], two_heads(moved_ref[0, 0, tok, :]), 1, 1) * factor
            grad = matmul(v_ref[span], two_heads(moved_ref[0, 1, tok, :]), 1, 1)
            top = jnp.max(scores, axis=0, keepdims=True)
            weights = jnp.exp(scores - top)
            w_ref[0, span] = weights
            gp_ref[0, span] = grad
            stat_ref[0, 0, pl.ds(span, 1), :] = top
            stat_ref[0, 1, pl.ds(span, 1), :] = jnp.sum(weights, axis=0, keepdims=True)
            stat_ref[0, 2, pl.ds(span, 1), :] = jnp.sum(weights * grad, axis=0, keepdims=True)

    whole = pl.BlockSpec(fetched.shape, lambda i: (0, 0, 0))
    weight_spec = pl.BlockSpec((features, 2 * HD), lambda i: (0, i))
    token_spec = pl.BlockSpec(
        (1, 2, tokens, 2 * HD), lambda i: (i // per_group, 0, 0, i % per_group)
    )
    kv_spec = pl.BlockSpec((spans, keys, 2 * HD), lambda i: (0, 0, i))
    score_spec = pl.BlockSpec((1, spans, keys, 2 * SPAN), lambda i: (i, 0, 0, 0))
    return pl.pallas_call(
        kernel,
        grid=(pairs,),
        in_specs=[whole, weight_spec, weight_spec, token_spec],
        out_specs=[
            kv_spec,
            kv_spec,
            score_spec,
            score_spec,
            pl.BlockSpec((1, 3, spans, 2 * SPAN), lambda i: (i, 0, 0, 0)),
        ],
        out_shape=[
            jax.ShapeDtypeStruct((spans, keys, all_width), BF),
            jax.ShapeDtypeStruct((spans, keys, all_width), BF),
            jax.ShapeDtypeStruct((pairs, spans, keys, 2 * SPAN), F32),
            jax.ShapeDtypeStruct((pairs, spans, keys, 2 * SPAN), F32),
            jax.ShapeDtypeStruct((pairs, 3, spans, 2 * SPAN), F32),
        ],
        scratch_shapes=[
            pltpu.VMEM((spans * keys, features), BF),
            pltpu.VMEM(fetched.shape, F32),
            pltpu.VMEM((spans * keys, HD), F32),
        ],
        compiler_params=PARAMS,
        cost_estimate=cost(
            4 * spans * keys * (features + SPAN) * all_width,
            8 * spans * keys * all_width,
            spans * keys * SPAN * 2 * pairs,
        ),
        name="score_spans",
    )(fetched, key_weight, value_weight, moved)


def blend_spans(scored, stats, key_weight, value_weight, moved):
    key_rows, value_rows, weights, grad_probs = scored
    features, all_width = key_weight.shape
    groups, _, tokens, width = moved.shape
    spans, keys, _ = key_rows.shape
    count = keys // 8
    lanes = keys // NBRS
    blocks = features // HD
    per_group = width // (2 * HD)
    pairs = all_width // (2 * HD)
    factor = HD ** (-0.5)
    devices = len(stats)

    def kernel(k_ref, v_ref, w_ref, gp_ref, *refs):
        stat_refs = refs[:devices]
        wk_ref, wv_ref, moved_ref, out_ref, part_ref = refs[devices : devices + 5]
        total, gk_ref, gv_ref, spread = refs[devices + 5 :]
        step = pl.program_id(0)

        own_top = stat_refs[0][0, 0]
        top = own_top
        for ref in stat_refs[1:]:
            top = jnp.maximum(top, ref[0, 0])
        sums = jnp.zeros_like(top)
        inner = jnp.zeros_like(top)
        for ref in stat_refs:
            scale = jnp.exp(ref[0, 0] - top)
            sums = sums + ref[0, 1] * scale
            inner = inner + ref[0, 2] * scale
        scale = jnp.exp(own_top - top) / sums
        inner = inner / sums

        for span in range(spans):
            tok = pl.ds(span * SPAN, SPAN)
            probs = w_ref[0, span] * scale[span : span + 1]
            probs_b = probs.astype(BF)
            grad_scores = (
                probs * (gp_ref[0, span] - inner[span : span + 1]) * factor
            ).astype(BF)
            k, v = k_ref[span], v_ref[span]
            blended = matmul(probs_b, v, 0, 0)
            shifted_grad = matmul(grad_scores, k, 0, 0)
            out_ref[0, 0, tok, :HD] = blended[:SPAN, :HD].astype(BF)
            out_ref[0, 0, tok, HD:] = blended[SPAN:, HD:].astype(BF)
            out_ref[0, 1, tok, :HD] = shifted_grad[:SPAN, :HD].astype(BF)
            out_ref[0, 1, tok, HD:] = shifted_grad[SPAN:, HD:].astype(BF)
            gk = matmul(grad_scores, two_heads(moved_ref[0, 0, tok, :]))
            gv = matmul(probs_b, two_heads(moved_ref[0, 1, tok, :]))
            gk_ref[:, span] = gk.reshape(count, 8, 2 * HD)
            gv_ref[:, span] = gv.reshape(count, 8, 2 * HD)

        flat = (spans * keys, 2 * HD)
        term = matmul(gk_ref[...].reshape(flat).astype(BF), wk_ref[...], 1, 1)
        term = term + matmul(gv_ref[...].reshape(flat).astype(BF), wv_ref[...], 1, 1)

        @pl.when(step == 0)
        def _():
            for block in range(blocks):
                total[block] = term[:, block * HD : (block + 1) * HD]

        @pl.when(step > 0)
        def _():
            for block in range(blocks):
                total[block] += term[:, block * HD : (block + 1) * HD]

        @pl.when(step == pairs - 1)
        def _():
            spread[:, length - 8 :, :] = jnp.zeros((lanes, 8, HD), F32)
            for block in range(blocks):
                for lane in range(lanes):
                    for nbr in range(NBRS):
                        at = lane * NBRS // 8 * 8 * spans + lane * NBRS % 8 + nbr
                        to = pl.ds(nbr * blocks + block, spans, stride=NBRS * blocks)
                        spread[lane, to, :] = total[block, pl.ds(at, spans, stride=8), :]
            part_ref[...] = spread[...].astype(BF)

    weight_spec = pl.BlockSpec((features, 2 * HD), lambda i: (0, i))
    token_spec = pl.BlockSpec(
        (1, 2, tokens, 2 * HD), lambda i: (i // per_group, 0, 0, i % per_group)
    )
    kv_spec = pl.BlockSpec((spans, keys, 2 * HD), lambda i: (0, 0, i))
    score_spec = pl.BlockSpec((1, spans, keys, 2 * SPAN), lambda i: (i, 0, 0, 0))
    stat_spec = pl.BlockSpec((1, 3, spans, 2 * SPAN), lambda i: (i, 0, 0, 0))
    length = message_rows(spans * NBRS, blocks)
    result = (lanes, length, HD)
    return pl.pallas_call(
        kernel,
        grid=(pairs,),
        in_specs=[kv_spec, kv_spec, score_spec, score_spec]
        + [stat_spec] * devices
        + [weight_spec, weight_spec, token_spec],
        out_specs=[token_spec, pl.BlockSpec(result, lambda i: (0, 0, 0))],
        out_shape=[
            jax.ShapeDtypeStruct((groups, 2, tokens, width), BF),
            jax.ShapeDtypeStruct(result, BF),
        ],
        scratch_shapes=[
            pltpu.VMEM((blocks, spans * keys, HD), F32),
            pltpu.VMEM((count, spans, 8, 2 * HD), F32),
            pltpu.VMEM((count, spans, 8, 2 * HD), F32),
            pltpu.VMEM(result, F32),
        ],
        compiler_params=PARAMS,
        cost_estimate=cost(
            4 * spans * keys * (features + 2 * SPAN) * all_width, 12 * spans * keys * all_width
        ),
        name="blend_spans",
    )(key_rows, value_rows, weights, grad_probs, *stats, key_weight, value_weight, moved)


def after(value, *others):
    return lax.optimization_barrier((value, *others))[0]


def shards(query, d_attended, encoded, key_weight, value_weight, nbr_shard, nbr_row):
    lanes = lax.axis_size(("z", "y"))
    groups = lax.axis_size("x")
    c = lax.axis_index("c").astype(I32)
    spans, neighbours = nbr_shard.shape
    stored, quarter, features = encoded.shape
    rows = lanes * stored
    picks = spans * neighbours

    pieces = split_pieces(encoded, nbr_shard, nbr_row)
    store = lax.all_to_all(pieces, ("z", "y"), 0, 0, tiled=True).reshape(rows, features + SPARE)

    moved = move_tokens([after(query, pieces), d_attended], True)
    moved = lax.all_gather(moved, "x")

    stores = [store, send_ring(store, "c", 1)]
    live = (jnp.arange(stored) < spans)[None, :, None]

    def places(held):
        named = held[:, features : features + 2 * neighbours].astype(I32)
        named = named.reshape(lanes, stored, 2 * neighbours)
        owner, row = named[..., :neighbours], named[..., neighbours:]
        place = owner // 2 * stored + row
        return place, owner % 2 == c, live

    place, here, valid = places(stores[0])
    target = jnp.where(valid, jnp.where(here, place, place + rows), -1)
    picked = pick_rows(stores, target.reshape(-1, 1), lanes, picks, features)
    fetched = lax.all_to_all(picked, ("z", "y"), 0, 0, tiled=True)

    *scored, stat = score_spans(fetched, key_weight, value_weight, moved)
    stats = [send_ring(stat, "x", away) for away in range(groups)]
    output, terms = blend_spans(scored, stats, key_weight, value_weight, moved)
    output = lax.psum_scatter(output, "x", scatter_dimension=0)

    home = lax.all_to_all(terms, ("z", "y"), 0, 0, tiled=True)
    target = []
    for held in stores:
        place, here, valid = places(held)
        target.append(jnp.where(valid & here, place, -1).reshape(1, -1))
    target = jnp.concatenate(target, 1)
    sums = sum_rows([home, send_ring(home, "c", 1)], target, picks, rows, features)
    returned = sums.reshape(lanes, stored, features)
    returned = lax.all_to_all(returned, ("z", "y"), 0, 0, tiled=True)
    attended, d_query = move_tokens([output], False)
    d_encoded = join_pieces(after(returned, attended))
    return (attended, d_query, d_encoded)


def solution(mesh):
    groups = mesh.devices.shape[1]
    fine = Mesh(mesh.devices.reshape(-1, 4, 2, groups), ("z", "y", "c", "x"))
    seq = ("z", "y", "c")
    placed = (
        P(seq, "x"),
        P(seq, "x"),
        P(seq, "x", None),
        P(),
        P(),
        P(seq, None),
        P(seq, None),
    )
    return jax.shard_map(
        shards,
        mesh=fine,
        in_specs=placed,
        out_specs=(P(seq, "x"), P(seq, "x"), P(seq, "x", None)),
        check_vma=False,
    )
```

```python
import jax
import jax.numpy as jnp
from jax import lax
from jax.experimental import pallas as pl
from jax.experimental.pallas import tpu as pltpu
from jax.sharding import Mesh, PartitionSpec as P

HD = 128
SPAN = 64
NBRS = 2
SPARE = 128
BF = jnp.bfloat16
F32 = jnp.float32
I32 = jnp.int32
PARAMS = pltpu.CompilerParams(vmem_limit_bytes=48 * 1024 * 1024)
SMALL = pltpu.CompilerParams(vmem_limit_bytes=28 * 1024 * 1024)


def matmul(left, right, left_dim=1, right_dim=0):
    return lax.dot_general(
        left, right, (((left_dim,), (right_dim,)), ((), ())), preferred_element_type=F32
    )


def cost(flops, bytes_accessed, transcendentals=0):
    return pl.CostEstimate(
        flops=int(flops), bytes_accessed=int(bytes_accessed), transcendentals=int(transcendentals)
    )


def send_ring(array, axis, step):
    size = lax.axis_size(axis)
    if step % size == 0:
        return array
    return lax.ppermute(array, axis, [(i, (i + step) % size) for i in range(size)])


def piece_matrix(stored, quarter):
    shape = (stored * quarter, stored * quarter)
    to = lax.broadcasted_iota(I32, shape, 0)
    source = lax.broadcasted_iota(I32, shape, 1)
    token = to % stored * quarter + to // stored
    return (source == token).astype(F32).astype(BF)


def shift_matrix(step):
    to = lax.broadcasted_iota(I32, (SPAN, 2 * SPAN), 0)
    source = lax.broadcasted_iota(I32, (SPAN, 2 * SPAN), 1)
    return (source == to + step).astype(F32).astype(BF)


def prepare(encoded, nbr_shard, nbr_row, query, d_attended):
    stored, quarter, features = encoded.shape
    size = stored * quarter
    spans, neighbours = nbr_shard.shape
    tokens, width = query.shape

    def kernel(enc_ref, shard_ref, row_ref, q_ref, g_ref, out_ref, moved_ref, names):
        names[...] = jnp.zeros_like(names)
        names[:neighbours, :spans] = shard_ref[...].astype(F32)
        names[neighbours : 2 * neighbours, :spans] = row_ref[...].astype(F32)
        named = names[...].astype(BF)
        pieces = matmul(piece_matrix(stored, quarter), enc_ref[...]).astype(BF)
        for token in range(quarter):
            out_ref[token, :, :features] = pieces[token * stored : (token + 1) * stored]
            out_ref[token, :, features:] = named
        order = shift_matrix(SPAN - 1)
        blank = jnp.zeros((SPAN, width), BF)
        for which, ref in enumerate((q_ref, g_ref)):
            for span in range(spans):
                at = span * SPAN
                after = ref[at + SPAN : at + 2 * SPAN] if span < spans - 1 else blank
                pair = jnp.concatenate([ref[at : at + SPAN], after], 0)
                moved_ref[which, at : at + SPAN] = matmul(order, pair).astype(BF)

    return pl.pallas_call(
        kernel,
        out_shape=[
            jax.ShapeDtypeStruct((quarter, stored, features + SPARE), BF),
            jax.ShapeDtypeStruct((2, tokens, width), BF),
        ],
        scratch_shapes=[pltpu.VMEM((stored, SPARE), F32)],
        compiler_params=PARAMS,
        cost_estimate=cost(2 * size * size * features, 4 * size * features + 8 * tokens * width),
        name="prepare",
    )(encoded.reshape(size, features), nbr_shard.T, nbr_row.T, query, d_attended)


def join_pieces(parts):
    quarter, stored, features = parts.shape
    size = stored * quarter

    def kernel(part_ref, out_ref):
        out_ref[...] = matmul(piece_matrix(stored, quarter), part_ref[...], 0, 0).astype(BF)

    joined = pl.pallas_call(
        kernel,
        out_shape=jax.ShapeDtypeStruct((size, features), BF),
        compiler_params=PARAMS,
        cost_estimate=cost(2 * size * size * features, 4 * size * features),
        name="join_pieces",
    )(parts.reshape(size, features))
    return joined.reshape(stored, quarter, features)


def message_rows(picks, blocks):
    return -(-picks * blocks // 8) * 8


def pick_rows(store, target, lanes, picks, features, before=None):
    rows = store.shape[0]
    size = target.shape[0]
    each = size // lanes
    blocks = features // HD
    length = message_rows(picks, blocks)

    def kernel(target_ref, store_ref, *refs):
        column = lax.broadcasted_iota(I32, (size, rows), 1)
        one_hot = (column == target_ref[...]).astype(F32).astype(BF)
        if before is None:
            refs[0][...] = matmul(one_hot, store_ref[:, :features]).astype(BF)
            return
        before_ref, out_ref, spread = refs
        spread[:, length - 8 :, :] = jnp.zeros((lanes, 8, HD), F32)
        for block in range(blocks):
            cols = slice(block * HD, (block + 1) * HD)
            total = matmul(one_hot, store_ref[:, cols]) + before_ref[:, cols].astype(F32)
            for lane in range(lanes):
                part = total[lane * each : lane * each + picks]
                spread[lane, pl.ds(block, picks, stride=blocks), :] = part
        out_ref[...] = spread[...].astype(BF)

    last = before is not None
    shape = (lanes, length, HD) if last else (size, features)
    return pl.pallas_call(
        kernel,
        out_shape=jax.ShapeDtypeStruct(shape, BF),
        scratch_shapes=[pltpu.VMEM(shape, F32)] if last else [],
        compiler_params=PARAMS,
        cost_estimate=cost(2 * size * rows * features, 2 * (2 * size + rows) * features),
        name="pick_rows",
    )(target, store, *([before] if last else []))


def sum_rows(term, target, picks, rows, features, before=None):
    lanes, length, _ = term.shape
    size = target.shape[1]
    each = size // lanes
    blocks = features // HD
    last = before is not None

    def kernel(target_ref, term_ref, *refs):
        out_ref, spread, flat = refs[-3:]
        row = lax.broadcasted_iota(I32, (rows, size), 0)
        one_hot = (row == target_ref[...]).astype(F32).astype(BF)
        spread[...] = term_ref[...].astype(F32)
        for lane in range(lanes):
            low = lane * each + picks // 8 * 8
            flat[low : (lane + 1) * each, :] = jnp.zeros(((lane + 1) * each - low, HD), F32)
        for block in range(blocks):
            cols = slice(block * HD, (block + 1) * HD)
            for lane in range(lanes):
                part = spread[lane, pl.ds(block, picks, stride=blocks), :]
                flat[lane * each : lane * each + picks, :] = part
            total = matmul(one_hot, flat[...].astype(BF))
            if last:
                total = total + refs[0][:, cols]
            out_ref[:, cols] = total.astype(out_ref.dtype)

    return pl.pallas_call(
        kernel,
        out_shape=jax.ShapeDtypeStruct((rows, features), BF if last else F32),
        scratch_shapes=[pltpu.VMEM((lanes, length, HD), F32), pltpu.VMEM((size, HD), F32)],
        compiler_params=PARAMS,
        cost_estimate=cost(2 * size * rows * features, 2 * (size + 2 * rows) * features),
        name="sum_rows",
    )(target, term, *([before] if last else []))


def move_back(moved):
    tokens, width = moved.shape[-2:]
    spans = tokens // SPAN

    def kernel(moved_ref, *outs):
        order = shift_matrix(1)
        blank = jnp.zeros((SPAN, width), BF)
        for which, out in enumerate(outs):
            for span in range(spans):
                at = span * SPAN
                before = moved_ref[which, at - SPAN : at] if span else blank
                pair = jnp.concatenate([before, moved_ref[which, at : at + SPAN]], 0)
                out[at : at + SPAN] = matmul(order, pair).astype(BF)

    return pl.pallas_call(
        kernel,
        out_shape=[jax.ShapeDtypeStruct((tokens, width), BF)] * 2,
        compiler_params=PARAMS,
        cost_estimate=cost(8 * tokens * SPAN * width, 8 * tokens * width),
        name="move_back",
    )(moved.reshape(2, tokens, width))


def two_heads(pair):
    blank = jnp.zeros((SPAN, HD), pair.dtype)
    upper = jnp.concatenate([pair[:, :HD], blank], 1)
    lower = jnp.concatenate([blank, pair[:, HD:]], 1)
    return jnp.concatenate([upper, lower], 0)


def score_spans(fetched, key_weight, value_weight, moved):
    lanes = fetched.shape[0]
    features, all_width = key_weight.shape
    groups, _, tokens, width = moved.shape
    spans = tokens // SPAN
    keys = lanes * NBRS
    count = keys // 8
    blocks = features // HD
    per_group = width // (2 * HD)
    pairs = all_width // (2 * HD)
    factor = HD ** (-0.5)

    def kernel(
        part_ref,
        wk_ref,
        wv_ref,
        moved_ref,
        k_ref,
        v_ref,
        w_ref,
        gp_ref,
        top_ref,
        stat_ref,
        rows_ref,
        spread,
        flat,
    ):
        @pl.when(pl.program_id(0) == 0)
        def _():
            spread[...] = part_ref[...].astype(F32)
            for block in range(blocks):
                for lane in range(lanes):
                    for nbr in range(NBRS):
                        to = lane * NBRS // 8 * 8 * spans + lane * NBRS % 8 + nbr
                        flat[pl.ds(to, spans, stride=8), :] = spread[
                            lane, pl.ds(nbr * blocks + block, spans, stride=NBRS * blocks), :
                        ]
                rows_ref[:, block * HD : (block + 1) * HD] = flat[...].astype(BF)

        rows = rows_ref[...]

        def project(weight):
            out = matmul(rows, weight).reshape(count, spans, 8, 2 * HD)
            return out.transpose(1, 0, 2, 3).reshape(spans, keys, 2 * HD).astype(BF)

        step = pl.program_id(0)
        k_ref[step] = project(wk_ref[...])
        v_ref[step] = project(wv_ref[...])
        for span in range(spans):
            tok = pl.ds(span * SPAN, SPAN)
            scores = matmul(k_ref[step, span], two_heads(moved_ref[0, 0, tok, :]), 1, 1) * factor
            grad = matmul(v_ref[step, span], two_heads(moved_ref[0, 1, tok, :]), 1, 1)
            top = jnp.max(scores, axis=0, keepdims=True)
            weights = jnp.exp(scores - top)
            w_ref[step, span] = weights
            gp_ref[step, span] = grad
            mass = jnp.sum(weights, axis=0, keepdims=True)
            mean = jnp.sum(weights * grad, axis=0, keepdims=True) / mass
            top_ref[step, pl.ds(span, 1), :] = top
            stat_ref[pl.ds(2 * spans * step + span, 1), :] = top + jnp.log(mass)
            stat_ref[pl.ds(2 * spans * step + spans + span, 1), :] = mean

    whole = pl.BlockSpec(fetched.shape, lambda i: (0, 0, 0))
    weight_spec = pl.BlockSpec((features, 2 * HD), lambda i: (0, i))
    token_spec = pl.BlockSpec(
        (1, 2, tokens, 2 * HD), lambda i: (i // per_group, 0, 0, i % per_group)
    )
    held = pl.BlockSpec(memory_space=pltpu.VMEM)
    size = (2 * spans * pairs, 2 * SPAN)
    return pl.pallas_call(
        kernel,
        grid=(pairs,),
        in_specs=[whole, weight_spec, weight_spec, token_spec],
        out_specs=[held] * 5 + [pl.BlockSpec(size, lambda i: (0, 0))],
        out_shape=[
            pltpu.VMEM((pairs, spans, keys, 2 * HD), BF),
            pltpu.VMEM((pairs, spans, keys, 2 * HD), BF),
            pltpu.VMEM((pairs, spans, keys, 2 * SPAN), F32),
            pltpu.VMEM((pairs, spans, keys, 2 * SPAN), F32),
            pltpu.VMEM((pairs, spans, 2 * SPAN), F32),
            jax.ShapeDtypeStruct(size, F32),
        ],
        scratch_shapes=[
            pltpu.VMEM((spans * keys, features), BF),
            pltpu.VMEM(fetched.shape, F32),
            pltpu.VMEM((spans * keys, HD), F32),
        ],
        compiler_params=SMALL,
        cost_estimate=cost(
            4 * spans * keys * (features + SPAN) * all_width,
            8 * spans * keys * all_width,
            spans * keys * SPAN * 2 * pairs,
        ),
        name="score_spans",
    )(fetched, key_weight, value_weight, moved)


def blend_spans(scored, stats, key_weight, value_weight, moved):
    scored = [pltpu.with_memory_space_constraint(array, pltpu.VMEM) for array in scored]
    features, all_width = key_weight.shape
    groups, _, tokens, width = moved.shape
    _, spans, keys, _ = scored[0].shape
    count = keys // 8
    lanes = keys // NBRS
    blocks = features // HD
    per_group = width // (2 * HD)
    pairs = all_width // (2 * HD)
    factor = HD ** (-0.5)
    devices = len(stats)

    def kernel(k_ref, v_ref, w_ref, gp_ref, top_ref, *refs):
        stat_refs = refs[:devices]
        wk_ref, wv_ref, moved_ref, out_ref, part_ref = refs[devices : devices + 5]
        total, gk_ref, gv_ref, spread = refs[devices + 5 :]
        step = pl.program_id(0)

        first = 2 * spans * step
        logs = [ref[pl.ds(first, spans), :] for ref in stat_refs]
        means = [ref[pl.ds(first + spans, spans), :] for ref in stat_refs]
        most = logs[0]
        for log in logs[1:]:
            most = jnp.maximum(most, log)
        shares = [jnp.exp(log - most) for log in logs]
        whole = shares[0]
        inner = shares[0] * means[0]
        for share, mean in zip(shares[1:], means[1:]):
            whole = whole + share
            inner = inner + share * mean
        inner = inner / whole
        scale = jnp.exp(top_ref[step] - most) / whole

        for span in range(spans):
            tok = pl.ds(span * SPAN, SPAN)
            probs = w_ref[step, span] * scale[span : span + 1]
            probs_b = probs.astype(BF)
            grad_scores = (
                probs * (gp_ref[step, span] - inner[span : span + 1]) * factor
            ).astype(BF)
            k, v = k_ref[step, span], v_ref[step, span]
            blended = matmul(probs_b, v, 0, 0)
            shifted_grad = matmul(grad_scores, k, 0, 0)
            out_ref[0, 0, tok, :HD] = blended[:SPAN, :HD].astype(BF)
            out_ref[0, 0, tok, HD:] = blended[SPAN:, HD:].astype(BF)
            out_ref[0, 1, tok, :HD] = shifted_grad[:SPAN, :HD].astype(BF)
            out_ref[0, 1, tok, HD:] = shifted_grad[SPAN:, HD:].astype(BF)
            gk = matmul(grad_scores, two_heads(moved_ref[0, 0, tok, :]))
            gv = matmul(probs_b, two_heads(moved_ref[0, 1, tok, :]))
            gk_ref[:, span] = gk.reshape(count, 8, 2 * HD)
            gv_ref[:, span] = gv.reshape(count, 8, 2 * HD)

        flat = (spans * keys, 2 * HD)
        term = matmul(gk_ref[...].reshape(flat).astype(BF), wk_ref[...], 1, 1)
        term = term + matmul(gv_ref[...].reshape(flat).astype(BF), wv_ref[...], 1, 1)

        @pl.when(step == 0)
        def _():
            for block in range(blocks):
                total[block] = term[:, block * HD : (block + 1) * HD]

        @pl.when(step > 0)
        def _():
            for block in range(blocks):
                total[block] += term[:, block * HD : (block + 1) * HD]

        @pl.when(step == pairs - 1)
        def _():
            spread[:, length - 8 :, :] = jnp.zeros((lanes, 8, HD), F32)
            for block in range(blocks):
                for lane in range(lanes):
                    for nbr in range(NBRS):
                        at = lane * NBRS // 8 * 8 * spans + lane * NBRS % 8 + nbr
                        to = pl.ds(nbr * blocks + block, spans, stride=NBRS * blocks)
                        spread[lane, to, :] = total[block, pl.ds(at, spans, stride=8), :]
            part_ref[...] = spread[...].astype(BF)

    weight_spec = pl.BlockSpec((features, 2 * HD), lambda i: (0, i))
    token_spec = pl.BlockSpec(
        (1, 2, tokens, 2 * HD), lambda i: (i // per_group, 0, 0, i % per_group)
    )
    held = pl.BlockSpec(memory_space=pltpu.VMEM)
    stat_spec = pl.BlockSpec(stats[0].shape, lambda i: (0, 0))
    length = message_rows(spans * NBRS, blocks)
    result = (lanes, length, HD)
    return pl.pallas_call(
        kernel,
        grid=(pairs,),
        in_specs=[held] * 5
        + [stat_spec] * devices
        + [weight_spec, weight_spec, token_spec],
        out_specs=[token_spec, pl.BlockSpec(result, lambda i: (0, 0, 0))],
        out_shape=[
            jax.ShapeDtypeStruct((groups, 2, tokens, width), BF),
            jax.ShapeDtypeStruct(result, BF),
        ],
        scratch_shapes=[
            pltpu.VMEM((blocks, spans * keys, HD), F32),
            pltpu.VMEM((count, spans, 8, 2 * HD), F32),
            pltpu.VMEM((count, spans, 8, 2 * HD), F32),
            pltpu.VMEM(result, F32),
        ],
        compiler_params=SMALL,
        cost_estimate=cost(
            4 * spans * keys * (features + 2 * SPAN) * all_width, 12 * spans * keys * all_width
        ),
        name="blend_spans",
    )(*scored, *stats, key_weight, value_weight, moved)


def after(value, *others):
    return lax.optimization_barrier((value, *others))[0]


def shards(query, d_attended, encoded, key_weight, value_weight, nbr_shard, nbr_row):
    lanes = lax.axis_size(("z", "y"))
    groups = lax.axis_size("x")
    c = lax.axis_index("c").astype(I32)
    spans, neighbours = nbr_shard.shape
    stored, quarter, features = encoded.shape
    rows = lanes * stored
    picks = spans * neighbours

    pieces, moved = prepare(encoded, nbr_shard, nbr_row, query, d_attended)
    store = lax.all_to_all(pieces, ("z", "y"), 0, 0, tiled=True).reshape(rows, features + SPARE)

    moved = lax.all_gather(moved, "x")

    def places(held):
        named = held.reshape(lanes, stored, -1)[:, : 2 * neighbours, features : features + stored]
        named = named.astype(I32).transpose(0, 2, 1)
        owner, row = named[..., :neighbours], named[..., neighbours:]
        place = owner // 2 * stored + row
        live = (jnp.arange(stored) < spans)[None, :, None]
        here = owner % 2 == c
        return [jnp.where(live & there, place, -1).reshape(-1) for there in (here, ~here)]

    others = send_ring(store, "c", 1)
    own_here, own_there = places(store)
    picked = pick_rows(store, own_here.reshape(-1, 1), lanes, picks, features)
    picked = pick_rows(others, own_there.reshape(-1, 1), lanes, picks, features, picked)
    fetched = lax.all_to_all(picked, ("z", "y"), 0, 0, tiled=True)

    *scored, stat = score_spans(fetched, key_weight, value_weight, moved)
    stats = [send_ring(stat, "x", away) for away in range(groups)]
    output, terms = blend_spans(scored, stats, key_weight, value_weight, moved)
    output = lax.psum_scatter(output, "x", scatter_dimension=0)

    home = lax.all_to_all(terms, ("z", "y"), 0, 0, tiled=True)
    others_here = places(others)[0]
    sums = sum_rows(home, own_here.reshape(1, -1), picks, rows, features)
    home = send_ring(home, "c", 1)
    sums = sum_rows(home, others_here.reshape(1, -1), picks, rows, features, sums)
    returned = sums.reshape(lanes, stored, features)
    returned = lax.all_to_all(returned, ("z", "y"), 0, 0, tiled=True)
    attended, d_query = move_back(output)
    d_encoded = join_pieces(after(returned, attended))
    return (attended, d_query, d_encoded)


def solution(mesh):
    groups = mesh.devices.shape[1]
    fine = Mesh(mesh.devices.reshape(-1, 4, 2, groups), ("z", "y", "c", "x"))
    seq = ("z", "y", "c")
    placed = (
        P(seq, "x"),
        P(seq, "x"),
        P(seq, "x", None),
        P(),
        P(),
        P(seq, None),
        P(seq, None),
    )
    return jax.shard_map(
        shards,
        mesh=fine,
        in_specs=placed,
        out_specs=(P(seq, "x"), P(seq, "x"), P(seq, "x", None)),
        check_vma=False,
    )
```

```python
import jax
import jax.numpy as jnp
from jax import lax
from jax.experimental import pallas as pl
from jax.experimental.pallas import tpu as pltpu
from jax.sharding import Mesh, PartitionSpec as P

HD = 128
SPAN = 64
NBRS = 2
SPARE = 128
BF = jnp.bfloat16
F32 = jnp.float32
I32 = jnp.int32
PARAMS = pltpu.CompilerParams(vmem_limit_bytes=48 * 1024 * 1024)
SMALL = pltpu.CompilerParams(vmem_limit_bytes=48 * 1024 * 1024)


def matmul(left, right, left_dim=1, right_dim=0):
    return lax.dot_general(
        left, right, (((left_dim,), (right_dim,)), ((), ())), preferred_element_type=F32
    )


def cost(flops, bytes_accessed, transcendentals=0):
    return pl.CostEstimate(
        flops=int(flops), bytes_accessed=int(bytes_accessed), transcendentals=int(transcendentals)
    )


def send_ring(array, axis, step):
    size = lax.axis_size(axis)
    if step % size == 0:
        return array
    return lax.ppermute(array, axis, [(i, (i + step) % size) for i in range(size)])


def piece_matrix(stored, quarter):
    shape = (stored * quarter, stored * quarter)
    to = lax.broadcasted_iota(I32, shape, 0)
    source = lax.broadcasted_iota(I32, shape, 1)
    token = to % stored * quarter + to // stored
    return (source == token).astype(F32).astype(BF)


def shift_matrix(step):
    to = lax.broadcasted_iota(I32, (SPAN, 2 * SPAN), 0)
    source = lax.broadcasted_iota(I32, (SPAN, 2 * SPAN), 1)
    return (source == to + step).astype(F32).astype(BF)


def prepare(encoded, nbr_shard, nbr_row, query, d_attended):
    stored, quarter, features = encoded.shape
    size = stored * quarter
    spans, neighbours = nbr_shard.shape
    tokens, width = query.shape

    operands = [encoded.reshape(size, features), nbr_shard.T, nbr_row.T, query, d_attended]
    held = [pltpu.with_memory_space_constraint(array, pltpu.HBM) for array in operands]

    def kernel(*refs):
        sources = refs[:5]
        out_ref, moved_ref, names = refs[5:8]
        landed, sems = refs[8:13], refs[13]
        copies = [
            pltpu.make_async_copy(source, target, sems.at[i])
            for i, (source, target) in enumerate(zip(sources, landed))
        ]
        for copy in copies:
            copy.start()
        enc_ref, shard_ref, row_ref, q_ref, g_ref = landed
        names[...] = jnp.zeros_like(names)
        source_matrix = piece_matrix(stored, quarter)
        for copy in copies[:3]:
            copy.wait()
        names[:neighbours, :spans] = shard_ref[...].astype(F32)
        names[neighbours : 2 * neighbours, :spans] = row_ref[...].astype(F32)
        named = names[...].astype(BF)
        pieces = matmul(source_matrix, enc_ref[...]).astype(BF)
        for token in range(quarter):
            out_ref[token, :, :features] = pieces[token * stored : (token + 1) * stored]
            out_ref[token, :, features:] = named
        order = shift_matrix(SPAN - 1)
        for copy in copies[3:]:
            copy.wait()
        blank = jnp.zeros((SPAN, width), BF)
        for which, ref in enumerate((q_ref, g_ref)):
            for span in range(spans):
                at = span * SPAN
                after = ref[at + SPAN : at + 2 * SPAN] if span < spans - 1 else blank
                pair = jnp.concatenate([ref[at : at + SPAN], after], 0)
                moved_ref[which, at : at + SPAN] = matmul(order, pair).astype(BF)

    return pl.pallas_call(
        kernel,
        out_shape=[
            jax.ShapeDtypeStruct((quarter, stored, features + SPARE), BF),
            jax.ShapeDtypeStruct((2, tokens, width), BF),
        ],
        in_specs=[pl.BlockSpec(memory_space=pltpu.HBM)] * 5,
        scratch_shapes=[pltpu.VMEM((stored, SPARE), F32)]
        + [pltpu.VMEM(array.shape, array.dtype) for array in operands]
        + [pltpu.SemaphoreType.DMA((5,))],
        compiler_params=PARAMS,
        cost_estimate=cost(2 * size * size * features, 4 * size * features + 8 * tokens * width),
        name="prepare",
    )(*held)


def join_pieces(parts):
    quarter, stored, features = parts.shape
    size = stored * quarter

    def kernel(part_ref, out_ref):
        out_ref[...] = matmul(piece_matrix(stored, quarter), part_ref[...], 0, 0).astype(BF)

    joined = pl.pallas_call(
        kernel,
        out_shape=jax.ShapeDtypeStruct((size, features), BF),
        compiler_params=PARAMS,
        cost_estimate=cost(2 * size * size * features, 4 * size * features),
        name="join_pieces",
    )(parts.reshape(size, features))
    return joined.reshape(stored, quarter, features)


def message_rows(picks, blocks):
    return -(-picks * blocks // 8) * 8


def pick_rows(store, target, lanes, picks, features, before=None):
    rows = store.shape[0]
    size = target.shape[0]
    each = size // lanes
    blocks = features // HD
    length = message_rows(picks, blocks)

    def kernel(target_ref, store_ref, *refs):
        column = lax.broadcasted_iota(I32, (size, rows), 1)
        one_hot = (column == target_ref[...]).astype(F32).astype(BF)
        if before is None:
            refs[0][...] = matmul(one_hot, store_ref[:, :features]).astype(BF)
            return
        before_ref, out_ref, spread = refs
        spread[:, length - 8 :, :] = jnp.zeros((lanes, 8, HD), F32)
        for block in range(blocks):
            cols = slice(block * HD, (block + 1) * HD)
            total = matmul(one_hot, store_ref[:, cols]) + before_ref[:, cols].astype(F32)
            for lane in range(lanes):
                part = total[lane * each : lane * each + picks]
                spread[lane, pl.ds(block, picks, stride=blocks), :] = part
        out_ref[...] = spread[...].astype(BF)

    last = before is not None
    shape = (lanes, length, HD) if last else (size, features)
    return pl.pallas_call(
        kernel,
        out_shape=jax.ShapeDtypeStruct(shape, BF),
        scratch_shapes=[pltpu.VMEM(shape, F32)] if last else [],
        compiler_params=PARAMS,
        cost_estimate=cost(2 * size * rows * features, 2 * (2 * size + rows) * features),
        name="pick_rows",
    )(target, store, *([before] if last else []))


def sum_rows(term, target, picks, rows, features, before=None):
    lanes, length, _ = term.shape
    size = target.shape[1]
    each = size // lanes
    blocks = features // HD
    last = before is not None

    def kernel(target_ref, term_ref, *refs):
        out_ref, spread, flat = refs[-3:]
        row = lax.broadcasted_iota(I32, (rows, size), 0)
        one_hot = (row == target_ref[...]).astype(F32).astype(BF)
        spread[...] = term_ref[...].astype(F32)
        for lane in range(lanes):
            low = lane * each + picks // 8 * 8
            flat[low : (lane + 1) * each, :] = jnp.zeros(((lane + 1) * each - low, HD), F32)
        for block in range(blocks):
            cols = slice(block * HD, (block + 1) * HD)
            for lane in range(lanes):
                part = spread[lane, pl.ds(block, picks, stride=blocks), :]
                flat[lane * each : lane * each + picks, :] = part
            total = matmul(one_hot, flat[...].astype(BF))
            if last:
                total = total + refs[0][:, cols]
            out_ref[:, cols] = total.astype(out_ref.dtype)

    return pl.pallas_call(
        kernel,
        out_shape=jax.ShapeDtypeStruct((rows, features), BF if last else F32),
        scratch_shapes=[pltpu.VMEM((lanes, length, HD), F32), pltpu.VMEM((size, HD), F32)],
        compiler_params=PARAMS,
        cost_estimate=cost(2 * size * rows * features, 2 * (size + 2 * rows) * features),
        name="sum_rows",
    )(target, term, *([before] if last else []))


def move_back(moved):
    tokens, width = moved.shape[-2:]
    spans = tokens // SPAN

    def kernel(moved_ref, *outs):
        order = shift_matrix(1)
        blank = jnp.zeros((SPAN, width), BF)
        for which, out in enumerate(outs):
            for span in range(spans):
                at = span * SPAN
                before = moved_ref[which, at - SPAN : at] if span else blank
                pair = jnp.concatenate([before, moved_ref[which, at : at + SPAN]], 0)
                out[at : at + SPAN] = matmul(order, pair).astype(BF)

    return pl.pallas_call(
        kernel,
        out_shape=[jax.ShapeDtypeStruct((tokens, width), BF)] * 2,
        compiler_params=PARAMS,
        cost_estimate=cost(8 * tokens * SPAN * width, 8 * tokens * width),
        name="move_back",
    )(moved.reshape(2, tokens, width))


def two_heads(pair):
    blank = jnp.zeros((SPAN, HD), pair.dtype)
    upper = jnp.concatenate([pair[:, :HD], blank], 1)
    lower = jnp.concatenate([blank, pair[:, HD:]], 1)
    return jnp.concatenate([upper, lower], 0)


def score_spans(fetched, key_weight, value_weight, moved):
    lanes = fetched.shape[0]
    features, all_width = key_weight.shape
    groups, _, tokens, width = moved.shape
    spans = tokens // SPAN
    keys = lanes * NBRS
    count = keys // 8
    blocks = features // HD
    per_group = width // (2 * HD)
    pairs = all_width // (2 * HD)
    factor = HD ** (-0.5)

    def kernel(
        part_ref,
        wk_ref,
        wv_ref,
        moved_ref,
        k_ref,
        v_ref,
        w_ref,
        gp_ref,
        top_ref,
        stat_ref,
        rows_ref,
        spread,
        flat,
    ):
        @pl.when(pl.program_id(0) == 0)
        def _():
            spread[...] = part_ref[...].astype(F32)
            for block in range(blocks):
                for lane in range(lanes):
                    for nbr in range(NBRS):
                        to = lane * NBRS // 8 * 8 * spans + lane * NBRS % 8 + nbr
                        flat[pl.ds(to, spans, stride=8), :] = spread[
                            lane, pl.ds(nbr * blocks + block, spans, stride=NBRS * blocks), :
                        ]
                rows_ref[:, block * HD : (block + 1) * HD] = flat[...].astype(BF)

        rows = rows_ref[...]

        def project(weight):
            out = matmul(rows, weight).reshape(count, spans, 8, 2 * HD)
            return out.transpose(1, 0, 2, 3).reshape(spans, keys, 2 * HD).astype(BF)

        step = pl.program_id(0)
        k_ref[step] = project(wk_ref[...])
        v_ref[step] = project(wv_ref[...])
        for span in range(spans):
            tok = pl.ds(span * SPAN, SPAN)
            scores = matmul(k_ref[step, span], two_heads(moved_ref[0, 0, tok, :]), 1, 1) * factor
            grad = matmul(v_ref[step, span], two_heads(moved_ref[0, 1, tok, :]), 1, 1)
            top = jnp.max(scores, axis=0, keepdims=True)
            weights = jnp.exp(scores - top)
            w_ref[step, span] = weights
            gp_ref[step, span] = grad
            mass = jnp.sum(weights, axis=0, keepdims=True)
            mean = jnp.sum(weights * grad, axis=0, keepdims=True) / mass
            top_ref[step, pl.ds(span, 1), :] = top
            stat_ref[pl.ds(2 * spans * step + span, 1), :] = top + jnp.log(mass)
            stat_ref[pl.ds(2 * spans * step + spans + span, 1), :] = mean

    whole = pl.BlockSpec(fetched.shape, lambda i: (0, 0, 0))
    weight_spec = pl.BlockSpec((features, 2 * HD), lambda i: (0, i))
    token_spec = pl.BlockSpec(
        (1, 2, tokens, 2 * HD), lambda i: (i // per_group, 0, 0, i % per_group)
    )
    held = pl.BlockSpec(memory_space=pltpu.VMEM)
    size = (2 * spans * pairs, 2 * SPAN)
    return pl.pallas_call(
        kernel,
        grid=(pairs,),
        in_specs=[whole, weight_spec, weight_spec, token_spec],
        out_specs=[held] * 5 + [pl.BlockSpec(size, lambda i: (0, 0))],
        out_shape=[
            pltpu.VMEM((pairs, spans, keys, 2 * HD), BF),
            pltpu.VMEM((pairs, spans, keys, 2 * HD), BF),
            pltpu.VMEM((pairs, spans, keys, 2 * SPAN), F32),
            pltpu.VMEM((pairs, spans, keys, 2 * SPAN), F32),
            pltpu.VMEM((pairs, spans, 2 * SPAN), F32),
            jax.ShapeDtypeStruct(size, F32),
        ],
        scratch_shapes=[
            pltpu.VMEM((spans * keys, features), BF),
            pltpu.VMEM(fetched.shape, F32),
            pltpu.VMEM((spans * keys, HD), F32),
        ],
        compiler_params=SMALL,
        cost_estimate=cost(
            4 * spans * keys * (features + SPAN) * all_width,
            8 * spans * keys * all_width,
            spans * keys * SPAN * 2 * pairs,
        ),
        name="score_spans",
    )(fetched, key_weight, value_weight, moved)


def blend_spans(scored, stats, key_weight, value_weight, moved):
    scored = [pltpu.with_memory_space_constraint(array, pltpu.VMEM) for array in scored]
    features, all_width = key_weight.shape
    groups, _, tokens, width = moved.shape
    _, spans, keys, _ = scored[0].shape
    count = keys // 8
    lanes = keys // NBRS
    blocks = features // HD
    per_group = width // (2 * HD)
    pairs = all_width // (2 * HD)
    factor = HD ** (-0.5)
    devices = len(stats)

    def kernel(k_ref, v_ref, w_ref, gp_ref, top_ref, *refs):
        stat_refs = refs[:devices]
        wk_ref, wv_ref, moved_ref, out_ref, part_ref = refs[devices : devices + 5]
        total, gk_ref, gv_ref, spread = refs[devices + 5 :]
        step = pl.program_id(0)

        first = 2 * spans * step
        logs = [ref[pl.ds(first, spans), :] for ref in stat_refs]
        means = [ref[pl.ds(first + spans, spans), :] for ref in stat_refs]
        most = logs[0]
        for log in logs[1:]:
            most = jnp.maximum(most, log)
        shares = [jnp.exp(log - most) for log in logs]
        whole = shares[0]
        inner = shares[0] * means[0]
        for share, mean in zip(shares[1:], means[1:]):
            whole = whole + share
            inner = inner + share * mean
        inner = inner / whole
        scale = jnp.exp(top_ref[step] - most) / whole

        for span in range(spans):
            tok = pl.ds(span * SPAN, SPAN)
            probs = w_ref[step, span] * scale[span : span + 1]
            probs_b = probs.astype(BF)
            grad_scores = (
                probs * (gp_ref[step, span] - inner[span : span + 1]) * factor
            ).astype(BF)
            k, v = k_ref[step, span], v_ref[step, span]
            blended = matmul(probs_b, v, 0, 0)
            shifted_grad = matmul(grad_scores, k, 0, 0)
            out_ref[0, 0, tok, :HD] = blended[:SPAN, :HD].astype(BF)
            out_ref[0, 0, tok, HD:] = blended[SPAN:, HD:].astype(BF)
            out_ref[0, 1, tok, :HD] = shifted_grad[:SPAN, :HD].astype(BF)
            out_ref[0, 1, tok, HD:] = shifted_grad[SPAN:, HD:].astype(BF)
            gk = matmul(grad_scores, two_heads(moved_ref[0, 0, tok, :]))
            gv = matmul(probs_b, two_heads(moved_ref[0, 1, tok, :]))
            gk_ref[:, span] = gk.reshape(count, 8, 2 * HD)
            gv_ref[:, span] = gv.reshape(count, 8, 2 * HD)

        flat = (spans * keys, 2 * HD)
        term = matmul(gk_ref[...].reshape(flat).astype(BF), wk_ref[...], 1, 1)
        term = term + matmul(gv_ref[...].reshape(flat).astype(BF), wv_ref[...], 1, 1)

        @pl.when(step == 0)
        def _():
            for block in range(blocks):
                total[block] = term[:, block * HD : (block + 1) * HD]

        @pl.when(step > 0)
        def _():
            for block in range(blocks):
                total[block] += term[:, block * HD : (block + 1) * HD]

        @pl.when(step == pairs - 1)
        def _():
            spread[:, length - 8 :, :] = jnp.zeros((lanes, 8, HD), F32)
            for block in range(blocks):
                for lane in range(lanes):
                    for nbr in range(NBRS):
                        at = lane * NBRS // 8 * 8 * spans + lane * NBRS % 8 + nbr
                        to = pl.ds(nbr * blocks + block, spans, stride=NBRS * blocks)
                        spread[lane, to, :] = total[block, pl.ds(at, spans, stride=8), :]
            part_ref[...] = spread[...].astype(BF)

    weight_spec = pl.BlockSpec((features, 2 * HD), lambda i: (0, i))
    token_spec = pl.BlockSpec(
        (1, 2, tokens, 2 * HD), lambda i: (i // per_group, 0, 0, i % per_group)
    )
    held = pl.BlockSpec(memory_space=pltpu.VMEM)
    stat_spec = pl.BlockSpec(stats[0].shape, lambda i: (0, 0))
    length = message_rows(spans * NBRS, blocks)
    result = (lanes, length, HD)
    return pl.pallas_call(
        kernel,
        grid=(pairs,),
        in_specs=[held] * 5
        + [stat_spec] * devices
        + [weight_spec, weight_spec, token_spec],
        out_specs=[token_spec, pl.BlockSpec(result, lambda i: (0, 0, 0))],
        out_shape=[
            jax.ShapeDtypeStruct((groups, 2, tokens, width), BF),
            jax.ShapeDtypeStruct(result, BF),
        ],
        scratch_shapes=[
            pltpu.VMEM((blocks, spans * keys, HD), F32),
            pltpu.VMEM((count, spans, 8, 2 * HD), F32),
            pltpu.VMEM((count, spans, 8, 2 * HD), F32),
            pltpu.VMEM(result, F32),
        ],
        compiler_params=SMALL,
        cost_estimate=cost(
            4 * spans * keys * (features + 2 * SPAN) * all_width, 12 * spans * keys * all_width
        ),
        name="blend_spans",
    )(*scored, *stats, key_weight, value_weight, moved)


def after(value, *others):
    return lax.optimization_barrier((value, *others))[0]


def shards(query, d_attended, encoded, key_weight, value_weight, nbr_shard, nbr_row):
    lanes = lax.axis_size(("z", "y"))
    groups = lax.axis_size("x")
    c = lax.axis_index("c").astype(I32)
    spans, neighbours = nbr_shard.shape
    stored, quarter, features = encoded.shape
    rows = lanes * stored
    picks = spans * neighbours

    pieces, moved = prepare(encoded, nbr_shard, nbr_row, query, d_attended)
    store = lax.all_to_all(pieces, ("z", "y"), 0, 0, tiled=True).reshape(rows, features + SPARE)

    moved = lax.all_gather(moved, "x")

    def places(held):
        named = held.reshape(lanes, stored, -1)[:, : 2 * neighbours, features : features + stored]
        named = named.astype(I32).transpose(0, 2, 1)
        owner, row = named[..., :neighbours], named[..., neighbours:]
        place = owner // 2 * stored + row
        live = (jnp.arange(stored) < spans)[None, :, None]
        here = owner % 2 == c
        return [jnp.where(live & there, place, -1).reshape(-1) for there in (here, ~here)]

    others = send_ring(store, "c", 1)
    own_here, own_there = places(store)
    picked = pick_rows(store, own_here.reshape(-1, 1), lanes, picks, features)
    picked = pick_rows(others, own_there.reshape(-1, 1), lanes, picks, features, picked)
    fetched = lax.all_to_all(picked, ("z", "y"), 0, 0, tiled=True)

    *scored, stat = score_spans(fetched, key_weight, value_weight, moved)
    stats = [send_ring(stat, "x", away) for away in range(groups)]
    output, terms = blend_spans(scored, stats, key_weight, value_weight, moved)
    output = lax.psum_scatter(output, "x", scatter_dimension=0)

    home = lax.all_to_all(terms, ("z", "y"), 0, 0, tiled=True)
    others_here = places(others)[0]
    sums = sum_rows(home, own_here.reshape(1, -1), picks, rows, features)
    home = send_ring(home, "c", 1)
    sums = sum_rows(home, others_here.reshape(1, -1), picks, rows, features, sums)
    returned = sums.reshape(lanes, stored, features)
    returned = lax.all_to_all(returned, ("z", "y"), 0, 0, tiled=True)
    attended, d_query = move_back(output)
    d_encoded = join_pieces(after(returned, attended))
    return (attended, d_query, d_encoded)


def solution(mesh):
    groups = mesh.devices.shape[1]
    fine = Mesh(mesh.devices.reshape(-1, 4, 2, groups), ("z", "y", "c", "x"))
    seq = ("z", "y", "c")
    placed = (
        P(seq, "x"),
        P(seq, "x"),
        P(seq, "x", None),
        P(),
        P(),
        P(seq, None),
        P(seq, None),
    )
    return jax.shard_map(
        shards,
        mesh=fine,
        in_specs=placed,
        out_specs=(P(seq, "x"), P(seq, "x"), P(seq, "x", None)),
        check_vma=False,
    )
```

```python
import jax
import jax.numpy as jnp
from jax import lax
from jax.experimental import pallas as pl
from jax.experimental.pallas import tpu as pltpu
from jax.sharding import Mesh, PartitionSpec as P

HD = 128
SPAN = 64
NBRS = 2
SPARE = 8
TURN = 4
BF = jnp.bfloat16
F32 = jnp.float32
I32 = jnp.int32
PARAMS = pltpu.CompilerParams(vmem_limit_bytes=48 * 1024 * 1024)
SMALL = pltpu.CompilerParams(vmem_limit_bytes=48 * 1024 * 1024)


def matmul(left, right, left_dim=1, right_dim=0):
    return lax.dot_general(
        left, right, (((left_dim,), (right_dim,)), ((), ())), preferred_element_type=F32
    )


def cost(flops, bytes_accessed, transcendentals=0):
    return pl.CostEstimate(
        flops=int(flops), bytes_accessed=int(bytes_accessed), transcendentals=int(transcendentals)
    )


def send_ring(array, axis, step):
    size = lax.axis_size(axis)
    if step % size == 0:
        return array
    return lax.ppermute(array, axis, [(i, (i + step) % size) for i in range(size)])


def piece_matrix(stored, quarter):
    shape = (stored * quarter, stored * quarter)
    to = lax.broadcasted_iota(I32, shape, 0)
    source = lax.broadcasted_iota(I32, shape, 1)
    token = to % stored * quarter + to // stored
    return (source == token).astype(F32).astype(BF)


def shift_matrix(step):
    to = lax.broadcasted_iota(I32, (SPAN, 2 * SPAN), 0)
    source = lax.broadcasted_iota(I32, (SPAN, 2 * SPAN), 1)
    return (source == to + step).astype(F32).astype(BF)


def prepare(encoded, nbr_shard, nbr_row, query, d_attended):
    stored, quarter, features = encoded.shape
    size = stored * quarter
    spans, neighbours = nbr_shard.shape
    tokens, width = query.shape

    operands = [encoded.reshape(size, features), nbr_shard.T, nbr_row.T, query, d_attended]
    held = [pltpu.with_memory_space_constraint(array, pltpu.HBM) for array in operands]

    def kernel(*refs):
        sources = refs[:5]
        out_ref, moved_ref, names = refs[5:8]
        landed, sems = refs[8:13], refs[13]
        copies = [
            pltpu.make_async_copy(source, target, sems.at[i])
            for i, (source, target) in enumerate(zip(sources, landed))
        ]
        for copy in copies:
            copy.start()
        enc_ref, shard_ref, row_ref, q_ref, g_ref = landed
        names[...] = jnp.zeros_like(names)
        source_matrix = piece_matrix(stored, quarter)
        for copy in copies[:3]:
            copy.wait()
        names[:neighbours, :spans] = shard_ref[...].astype(F32)
        names[neighbours : 2 * neighbours, :spans] = row_ref[...].astype(F32)
        named = names[...]
        pieces = matmul(source_matrix, enc_ref[...])
        for token in range(quarter):
            piece = pieces[token * stored : (token + 1) * stored]
            parts = [piece[:, at : at + HD] for at in range(0, features, HD)]
            out_ref[token] = jnp.concatenate([*parts, named], 0).astype(BF)
        order = shift_matrix(SPAN - 1)
        for copy in copies[3:]:
            copy.wait()
        blank = jnp.zeros((SPAN, width), BF)
        for which, ref in enumerate((q_ref, g_ref)):
            for span in range(spans):
                at = span * SPAN
                after = ref[at + SPAN : at + 2 * SPAN] if span < spans - 1 else blank
                pair = jnp.concatenate([ref[at : at + SPAN], after], 0)
                moved_ref[which, at : at + SPAN] = matmul(order, pair).astype(BF)

    return pl.pallas_call(
        kernel,
        out_shape=[
            jax.ShapeDtypeStruct((quarter, features // HD * stored + SPARE, HD), BF),
            jax.ShapeDtypeStruct((2, tokens, width), BF),
        ],
        in_specs=[pl.BlockSpec(memory_space=pltpu.HBM)] * 5,
        scratch_shapes=[pltpu.VMEM((SPARE, HD), F32)]
        + [pltpu.VMEM(array.shape, array.dtype) for array in operands]
        + [pltpu.SemaphoreType.DMA((5,))],
        compiler_params=PARAMS,
        cost_estimate=cost(2 * size * size * features, 4 * size * features + 8 * tokens * width),
        name="prepare",
    )(*held)


def join_pieces(parts):
    quarter, stored, features = parts.shape
    size = stored * quarter

    def kernel(part_ref, out_ref):
        out_ref[...] = matmul(piece_matrix(stored, quarter), part_ref[...], 0, 0).astype(BF)

    joined = pl.pallas_call(
        kernel,
        out_shape=jax.ShapeDtypeStruct((size, features), BF),
        compiler_params=PARAMS,
        cost_estimate=cost(2 * size * size * features, 4 * size * features),
        name="join_pieces",
    )(parts.reshape(size, features))
    return joined.reshape(stored, quarter, features)


def message_rows(picks, blocks):
    return -(-picks * blocks // 8) * 8


def pick_rows(store, target, picks, before=None):
    lanes = store.shape[0]
    size = target.shape[0]
    each = size // lanes
    stored = each // NBRS
    rows = lanes * stored
    blocks = (store.shape[1] - SPARE) // stored
    features = blocks * HD
    length = message_rows(picks, blocks)

    def kernel(target_ref, store_ref, *refs):
        column = lax.broadcasted_iota(I32, (size, rows), 1)
        one_hot = (column == target_ref[...]).astype(F32).astype(BF)

        def part_of(block):
            part = store_ref[:, block * stored : (block + 1) * stored, :].reshape(rows, HD)
            return matmul(one_hot, part)

        if before is None:
            for block in range(blocks):
                refs[0][:, block * HD : (block + 1) * HD] = part_of(block).astype(BF)
            return
        before_ref, out_ref, spread = refs
        spread[:, length - 8 :, :] = jnp.zeros((lanes, 8, HD), F32)
        for block in range(blocks):
            cols = slice(block * HD, (block + 1) * HD)
            total = part_of(block) + before_ref[:, cols].astype(F32)
            for lane in range(lanes):
                part = total[lane * each : lane * each + picks]
                spread[lane, pl.ds(block, picks, stride=blocks), :] = part
        out_ref[...] = spread[...].astype(BF)

    last = before is not None
    shape = (lanes, length, HD) if last else (size, features)
    return pl.pallas_call(
        kernel,
        out_shape=jax.ShapeDtypeStruct(shape, BF),
        scratch_shapes=[pltpu.VMEM(shape, F32)] if last else [],
        compiler_params=PARAMS,
        cost_estimate=cost(2 * size * rows * features, 2 * (2 * size + rows) * features),
        name="pick_rows",
    )(target, store, *([before] if last else []))


def sum_rows(term, target, picks, rows, features, before=None):
    lanes, length, _ = term.shape
    size = target.shape[1]
    each = size // lanes
    blocks = features // HD
    last = before is not None

    def kernel(target_ref, term_ref, *refs):
        out_ref, spread, flat = refs[-3:]
        row = lax.broadcasted_iota(I32, (rows, size), 0)
        one_hot = (row == target_ref[...]).astype(F32).astype(BF)
        spread[...] = term_ref[...].astype(F32)
        for lane in range(lanes):
            low = lane * each + picks // 8 * 8
            flat[low : (lane + 1) * each, :] = jnp.zeros(((lane + 1) * each - low, HD), F32)
        for block in range(blocks):
            cols = slice(block * HD, (block + 1) * HD)
            for lane in range(lanes):
                part = spread[lane, pl.ds(block, picks, stride=blocks), :]
                flat[lane * each : lane * each + picks, :] = part
            total = matmul(one_hot, flat[...].astype(BF))
            if last:
                total = total + refs[0][:, cols]
            out_ref[:, cols] = total.astype(out_ref.dtype)

    return pl.pallas_call(
        kernel,
        out_shape=jax.ShapeDtypeStruct((rows, features), BF if last else F32),
        scratch_shapes=[pltpu.VMEM((lanes, length, HD), F32), pltpu.VMEM((size, HD), F32)],
        compiler_params=PARAMS,
        cost_estimate=cost(2 * size * rows * features, 2 * (size + 2 * rows) * features),
        name="sum_rows",
    )(target, term, *([before] if last else []))


def move_back(moved):
    tokens, width = moved.shape[-2:]
    spans = tokens // SPAN

    def kernel(moved_ref, *outs):
        order = shift_matrix(1)
        blank = jnp.zeros((SPAN, width), BF)
        for which, out in enumerate(outs):
            for span in range(spans):
                at = span * SPAN
                before = moved_ref[which, at - SPAN : at] if span else blank
                pair = jnp.concatenate([before, moved_ref[which, at : at + SPAN]], 0)
                out[at : at + SPAN] = matmul(order, pair).astype(BF)

    return pl.pallas_call(
        kernel,
        out_shape=[jax.ShapeDtypeStruct((tokens, width), BF)] * 2,
        compiler_params=PARAMS,
        cost_estimate=cost(8 * tokens * SPAN * width, 8 * tokens * width),
        name="move_back",
    )(moved.reshape(2, tokens, width))


def two_heads(pair):
    blank = jnp.zeros((SPAN, HD), pair.dtype)
    upper = jnp.concatenate([pair[:, :HD], blank], 1)
    lower = jnp.concatenate([blank, pair[:, HD:]], 1)
    return jnp.concatenate([upper, lower], 0)


def score_spans(fetched, key_weight, value_weight, moved):
    lanes = fetched.shape[0]
    features, all_width = key_weight.shape
    groups, _, tokens, width = moved.shape
    spans = tokens // SPAN
    keys = lanes * NBRS
    count = keys // 8
    blocks = features // HD
    per_group = width // (2 * HD)
    pairs = all_width // (2 * HD)
    factor = HD ** (-0.5)

    def kernel(
        part_ref,
        wk_ref,
        wv_ref,
        moved_ref,
        k_ref,
        v_ref,
        w_ref,
        gp_ref,
        top_ref,
        stat_ref,
        rows_ref,
        spread,
        flat,
    ):
        @pl.when(pl.program_id(0) == 0)
        def _():
            spread[...] = part_ref[...].astype(F32)
            for block in range(blocks):
                for lane in range(lanes):
                    for nbr in range(NBRS):
                        to = lane * NBRS // 8 * 8 * spans + lane * NBRS % 8 + nbr
                        flat[pl.ds(to, spans, stride=8), :] = spread[
                            lane, pl.ds(nbr * blocks + block, spans, stride=NBRS * blocks), :
                        ]
                rows_ref[:, block * HD : (block + 1) * HD] = flat[...].astype(BF)

        rows = rows_ref[...]

        def project(weight):
            out = matmul(rows, weight).reshape(count, spans, 8, 2 * HD)
            return out.transpose(1, 0, 2, 3).reshape(spans, keys, 2 * HD).astype(BF)

        step = pl.program_id(0)
        k_ref[step] = project(wk_ref[...])
        v_ref[step] = project(wv_ref[...])
        for span in range(spans):
            tok = pl.ds(span * SPAN, SPAN)
            scores = matmul(k_ref[step, span], two_heads(moved_ref[0, 0, tok, :]), 1, 1) * factor
            grad = matmul(v_ref[step, span], two_heads(moved_ref[0, 1, tok, :]), 1, 1)
            top = jnp.max(scores, axis=0, keepdims=True)
            weights = jnp.exp(scores - top)
            w_ref[step, span] = weights
            gp_ref[step, span] = grad
            mass = jnp.sum(weights, axis=0, keepdims=True)
            mean = jnp.sum(weights * grad, axis=0, keepdims=True) / mass
            top_ref[step, pl.ds(span, 1), :] = top
            stat_ref[pl.ds(2 * spans * step + span, 1), :] = top + jnp.log(mass)
            stat_ref[pl.ds(2 * spans * step + spans + span, 1), :] = mean

    whole = pl.BlockSpec(fetched.shape, lambda i: (0, 0, 0))
    weight_spec = pl.BlockSpec((features, 2 * HD), lambda i: (0, i))
    token_spec = pl.BlockSpec(
        (1, 2, tokens, 2 * HD), lambda i: (i // per_group, 0, 0, i % per_group)
    )
    held = pl.BlockSpec(memory_space=pltpu.VMEM)
    size = (2 * spans * pairs, 2 * SPAN)
    return pl.pallas_call(
        kernel,
        grid=(pairs,),
        in_specs=[whole, weight_spec, weight_spec, token_spec],
        out_specs=[held] * 5 + [pl.BlockSpec(size, lambda i: (0, 0))],
        out_shape=[
            pltpu.VMEM((pairs, spans, keys, 2 * HD), BF),
            pltpu.VMEM((pairs, spans, keys, 2 * HD), BF),
            pltpu.VMEM((pairs, spans, keys, 2 * SPAN), F32),
            pltpu.VMEM((pairs, spans, keys, 2 * SPAN), F32),
            pltpu.VMEM((pairs, spans, 2 * SPAN), F32),
            jax.ShapeDtypeStruct(size, F32),
        ],
        scratch_shapes=[
            pltpu.VMEM((spans * keys, features), BF),
            pltpu.VMEM(fetched.shape, F32),
            pltpu.VMEM((spans * keys, HD), F32),
        ],
        compiler_params=SMALL,
        cost_estimate=cost(
            4 * spans * keys * (features + SPAN) * all_width,
            8 * spans * keys * all_width,
            spans * keys * SPAN * 2 * pairs,
        ),
        name="score_spans",
    )(fetched, key_weight, value_weight, moved)


def blend_spans(scored, stats, key_weight, value_weight, moved):
    scored = [pltpu.with_memory_space_constraint(array, pltpu.VMEM) for array in scored]
    features, all_width = key_weight.shape
    groups, _, tokens, width = moved.shape
    _, spans, keys, _ = scored[0].shape
    count = keys // 8
    lanes = keys // NBRS
    blocks = features // HD
    per_group = width // (2 * HD)
    pairs = all_width // (2 * HD)
    factor = HD ** (-0.5)
    devices = len(stats)

    def kernel(k_ref, v_ref, w_ref, gp_ref, top_ref, *refs):
        stat_refs = refs[:devices]
        wk_ref, wv_ref, moved_ref, out_ref, part_ref = refs[devices : devices + 5]
        total, keys_ref, values_ref, spread = refs[devices + 5 :]
        step = pl.program_id(0)

        first = 2 * spans * step
        logs = [ref[pl.ds(first, spans), :] for ref in stat_refs]
        means = [ref[pl.ds(first + spans, spans), :] for ref in stat_refs]
        most = logs[0]
        for log in logs[1:]:
            most = jnp.maximum(most, log)
        shares = [jnp.exp(log - most) for log in logs]
        whole = shares[0]
        inner = shares[0] * means[0]
        for share, mean in zip(shares[1:], means[1:]):
            whole = whole + share
            inner = inner + share * mean
        inner = inner / whole
        scale = jnp.exp(top_ref[step] - most) / whole

        for span in range(spans):
            tok = pl.ds(span * SPAN, SPAN)
            probs = w_ref[step, span] * scale[span : span + 1]
            probs_b = probs.astype(BF)
            grad_scores = (
                probs * (gp_ref[step, span] - inner[span : span + 1]) * factor
            ).astype(BF)
            k, v = k_ref[step, span], v_ref[step, span]
            blended = matmul(probs_b, v, 0, 0)
            shifted_grad = matmul(grad_scores, k, 0, 0)
            out_ref[0, 0, tok, :HD] = blended[:SPAN, :HD].astype(BF)
            out_ref[0, 0, tok, HD:] = blended[SPAN:, HD:].astype(BF)
            out_ref[0, 1, tok, :HD] = shifted_grad[:SPAN, :HD].astype(BF)
            out_ref[0, 1, tok, HD:] = shifted_grad[SPAN:, HD:].astype(BF)
            gk = matmul(grad_scores, two_heads(moved_ref[0, 0, tok, :]))
            gv = matmul(probs_b, two_heads(moved_ref[0, 1, tok, :]))
            at = pl.ds(pl.multiple_of(step % TURN * 2 * HD, 2 * HD), 2 * HD)
            gk = gk.reshape(count, 8, 2 * HD)
            gv = gv.reshape(count, 8, 2 * HD)
            keys_ref[:, span, :, at] = gk
            values_ref[:, span, :, at] = gv

        def project():
            left = jnp.concatenate([keys_ref[...], values_ref[...]], 3)
            left = left.reshape(spans * keys, 4 * TURN * HD).astype(BF)
            return matmul(left, jnp.concatenate([wk_ref[...], wv_ref[...]], 1), 1, 1)

        @pl.when(step == TURN - 1)
        def _():
            term = project()
            for block in range(blocks):
                total[block] = term[:, block * HD : (block + 1) * HD]

        @pl.when((step % TURN == TURN - 1) & (step >= TURN))
        def _():
            term = project()
            for block in range(blocks):
                total[block] += term[:, block * HD : (block + 1) * HD]

        @pl.when(step == pairs - 1)
        def _():
            spread[:, length - 8 :, :] = jnp.zeros((lanes, 8, HD), F32)
            for block in range(blocks):
                for lane in range(lanes):
                    for nbr in range(NBRS):
                        at = lane * NBRS // 8 * 8 * spans + lane * NBRS % 8 + nbr
                        to = pl.ds(nbr * blocks + block, spans, stride=NBRS * blocks)
                        spread[lane, to, :] = total[block, pl.ds(at, spans, stride=8), :]
            part_ref[...] = spread[...].astype(BF)

    weight_spec = pl.BlockSpec((features, 2 * TURN * HD), lambda i: (0, i // TURN))
    token_spec = pl.BlockSpec(
        (1, 2, tokens, 2 * HD), lambda i: (i // per_group, 0, 0, i % per_group)
    )
    held = pl.BlockSpec(memory_space=pltpu.VMEM)
    stat_spec = pl.BlockSpec(stats[0].shape, lambda i: (0, 0))
    length = message_rows(spans * NBRS, blocks)
    result = (lanes, length, HD)
    return pl.pallas_call(
        kernel,
        grid=(pairs,),
        in_specs=[held] * 5
        + [stat_spec] * devices
        + [weight_spec, weight_spec, token_spec],
        out_specs=[token_spec, pl.BlockSpec(result, lambda i: (0, 0, 0))],
        out_shape=[
            jax.ShapeDtypeStruct((groups, 2, tokens, width), BF),
            pltpu.HBM(result, BF),
        ],
        scratch_shapes=[
            pltpu.VMEM((blocks, spans * keys, HD), F32),
            pltpu.VMEM((count, spans, 8, 2 * TURN * HD), F32),
            pltpu.VMEM((count, spans, 8, 2 * TURN * HD), F32),
            pltpu.VMEM(result, F32),
        ],
        compiler_params=SMALL,
        cost_estimate=cost(
            4 * spans * keys * (features + 2 * SPAN) * all_width, 12 * spans * keys * all_width
        ),
        name="blend_spans",
    )(*scored, *stats, key_weight, value_weight, moved)


def after(value, *others):
    return lax.optimization_barrier((value, *others))[0]


def shards(query, d_attended, encoded, key_weight, value_weight, nbr_shard, nbr_row):
    lanes = lax.axis_size(("z", "y"))
    groups = lax.axis_size("x")
    c = lax.axis_index("c").astype(I32)
    spans, neighbours = nbr_shard.shape
    stored, quarter, features = encoded.shape
    rows = lanes * stored
    picks = spans * neighbours

    pieces, moved = prepare(encoded, nbr_shard, nbr_row, query, d_attended)
    store = lax.all_to_all(pieces, ("z", "y"), 0, 0, tiled=True)

    moved = lax.all_gather(moved, "x")

    def places(held):
        named = held[:, -SPARE : 2 * neighbours - SPARE, :stored].astype(I32).transpose(0, 2, 1)
        owner, row = named[..., :neighbours], named[..., neighbours:]
        place = owner // 2 * stored + row
        live = (jnp.arange(stored) < spans)[None, :, None]
        here = owner % 2 == c
        return [jnp.where(live & there, place, -1).reshape(-1) for there in (here, ~here)]

    others = send_ring(store, "c", 1)
    own_here, own_there = places(store)
    picked = pick_rows(store, own_here.reshape(-1, 1), picks)
    picked = pick_rows(others, own_there.reshape(-1, 1), picks, picked)
    fetched = lax.all_to_all(picked, ("z", "y"), 0, 0, tiled=True)

    *scored, stat = score_spans(fetched, key_weight, value_weight, moved)
    stats = [send_ring(stat, "x", away) for away in range(groups)]
    output, terms = blend_spans(scored, stats, key_weight, value_weight, moved)
    output = lax.psum_scatter(output, "x", scatter_dimension=0)

    home = lax.all_to_all(terms, ("z", "y"), 0, 0, tiled=True)
    others_here = places(after(others, terms))[0]
    sums = sum_rows(home, own_here.reshape(1, -1), picks, rows, features)
    home = send_ring(home, "c", 1)
    sums = sum_rows(home, others_here.reshape(1, -1), picks, rows, features, sums)
    returned = sums.reshape(lanes, stored, features)
    returned = lax.all_to_all(returned, ("z", "y"), 0, 0, tiled=True)
    attended, d_query = move_back(output)
    d_encoded = join_pieces(after(returned, attended))
    return (attended, d_query, d_encoded)


def solution(mesh):
    groups = mesh.devices.shape[1]
    fine = Mesh(mesh.devices.reshape(-1, 4, 2, groups), ("z", "y", "c", "x"))
    seq = ("z", "y", "c")
    placed = (
        P(seq, "x"),
        P(seq, "x"),
        P(seq, "x", None),
        P(),
        P(),
        P(seq, None),
        P(seq, None),
    )
    return jax.shard_map(
        shards,
        mesh=fine,
        in_specs=placed,
        out_specs=(P(seq, "x"), P(seq, "x"), P(seq, "x", None)),
        check_vma=False,
    )
```

```python
import jax
import jax.numpy as jnp
from jax import lax
from jax.experimental import pallas as pl
from jax.experimental.pallas import tpu as pltpu
from jax.sharding import Mesh, PartitionSpec as P

HD = 128
SPAN = 64
NBRS = 2
SPARE = 8
SIDES = 2
BF = jnp.bfloat16
F32 = jnp.float32
I32 = jnp.int32
PARAMS = pltpu.CompilerParams(vmem_limit_bytes=48 * 1024 * 1024)
SMALL = pltpu.CompilerParams(vmem_limit_bytes=50 * 1024 * 1024)


def matmul(left, right, left_dim=1, right_dim=0):
    return lax.dot_general(
        left, right, (((left_dim,), (right_dim,)), ((), ())), preferred_element_type=F32
    )


def cost(flops, bytes_accessed, transcendentals=0):
    return pl.CostEstimate(
        flops=int(flops), bytes_accessed=int(bytes_accessed), transcendentals=int(transcendentals)
    )


def send_ring(array, axis, step):
    size = lax.axis_size(axis)
    if step % size == 0:
        return array
    return lax.ppermute(array, axis, [(i, (i + step) % size) for i in range(size)])


def piece_matrix(stored, quarter):
    shape = (stored * quarter, stored * quarter)
    to = lax.broadcasted_iota(I32, shape, 0)
    source = lax.broadcasted_iota(I32, shape, 1)
    token = to % stored * quarter + to // stored
    return (source == token).astype(F32).astype(BF)


def shift_matrix(step):
    to = lax.broadcasted_iota(I32, (SPAN, 2 * SPAN), 0)
    source = lax.broadcasted_iota(I32, (SPAN, 2 * SPAN), 1)
    return (source == to + step).astype(F32).astype(BF)


def prepare(encoded, nbr_shard, nbr_row, query, d_attended):
    stored, quarter, features = encoded.shape
    size = stored * quarter
    spans, neighbours = nbr_shard.shape
    tokens, width = query.shape

    operands = [encoded.reshape(size, features), nbr_shard.T, nbr_row.T, query, d_attended]
    held = [pltpu.with_memory_space_constraint(array, pltpu.HBM) for array in operands]

    def kernel(*refs):
        sources = refs[:5]
        out_ref, moved_ref, names = refs[5:8]
        landed, sems = refs[8:13], refs[13]
        copies = [
            pltpu.make_async_copy(source, target, sems.at[i])
            for i, (source, target) in enumerate(zip(sources, landed))
        ]
        for copy in copies:
            copy.start()
        enc_ref, shard_ref, row_ref, q_ref, g_ref = landed
        names[...] = jnp.zeros_like(names)
        source_matrix = piece_matrix(stored, quarter)
        for copy in copies[:3]:
            copy.wait()
        names[:neighbours, :spans] = shard_ref[...].astype(F32)
        names[neighbours : 2 * neighbours, :spans] = row_ref[...].astype(F32)
        named = names[...]
        pieces = matmul(source_matrix, enc_ref[...])
        for token in range(quarter):
            piece = pieces[token * stored : (token + 1) * stored]
            parts = [piece[:, at : at + HD] for at in range(0, features, HD)]
            out_ref[token] = jnp.concatenate([*parts, named], 0).astype(BF)
        order = shift_matrix(SPAN - 1)
        for copy in copies[3:]:
            copy.wait()
        blank = jnp.zeros((SPAN, width), BF)
        for which, ref in enumerate((q_ref, g_ref)):
            for span in range(spans):
                at = span * SPAN
                after = ref[at + SPAN : at + 2 * SPAN] if span < spans - 1 else blank
                pair = jnp.concatenate([ref[at : at + SPAN], after], 0)
                moved_ref[which, at : at + SPAN] = matmul(order, pair).astype(BF)

    return pl.pallas_call(
        kernel,
        out_shape=[
            jax.ShapeDtypeStruct((quarter, features // HD * stored + SPARE, HD), BF),
            jax.ShapeDtypeStruct((2, tokens, width), BF),
        ],
        in_specs=[pl.BlockSpec(memory_space=pltpu.HBM)] * 5,
        scratch_shapes=[pltpu.VMEM((SPARE, HD), F32)]
        + [pltpu.VMEM(array.shape, array.dtype) for array in operands]
        + [pltpu.SemaphoreType.DMA((5,))],
        compiler_params=PARAMS,
        cost_estimate=cost(2 * size * size * features, 4 * size * features + 8 * tokens * width),
        name="prepare",
    )(*held)


def join_pieces(parts):
    quarter, stored, features = parts.shape
    size = stored * quarter

    def kernel(part_ref, out_ref):
        out_ref[...] = matmul(piece_matrix(stored, quarter), part_ref[...], 0, 0).astype(BF)

    joined = pl.pallas_call(
        kernel,
        out_shape=jax.ShapeDtypeStruct((size, features), BF),
        compiler_params=PARAMS,
        cost_estimate=cost(2 * size * size * features, 4 * size * features),
        name="join_pieces",
    )(parts.reshape(size, features))
    return joined.reshape(stored, quarter, features)


def message_rows(picks, blocks):
    return -(-picks * blocks // 8) * 8


def pick_rows(store, target, picks, before=None):
    lanes = store.shape[0]
    size = target.shape[0]
    each = size // lanes
    stored = each // NBRS
    rows = lanes * stored
    blocks = (store.shape[1] - SPARE) // stored
    features = blocks * HD
    length = message_rows(picks, blocks)

    def kernel(target_ref, store_ref, *refs):
        column = lax.broadcasted_iota(I32, (size, rows), 1)
        one_hot = (column == target_ref[...]).astype(F32).astype(BF)

        def part_of(block):
            part = store_ref[:, block * stored : (block + 1) * stored, :].reshape(rows, HD)
            return matmul(one_hot, part)

        if before is None:
            for block in range(blocks):
                refs[0][:, block * HD : (block + 1) * HD] = part_of(block).astype(BF)
            return
        before_ref, out_ref, spread = refs
        spread[:, length - 8 :, :] = jnp.zeros((lanes, 8, HD), F32)
        for block in range(blocks):
            cols = slice(block * HD, (block + 1) * HD)
            total = part_of(block) + before_ref[:, cols].astype(F32)
            for lane in range(lanes):
                part = total[lane * each : lane * each + picks]
                spread[lane, pl.ds(block, picks, stride=blocks), :] = part
        out_ref[...] = spread[...].astype(BF)

    last = before is not None
    shape = (lanes, length, HD) if last else (size, features)
    return pl.pallas_call(
        kernel,
        out_shape=jax.ShapeDtypeStruct(shape, BF),
        scratch_shapes=[pltpu.VMEM(shape, F32)] if last else [],
        compiler_params=PARAMS,
        cost_estimate=cost(2 * size * rows * features, 2 * (2 * size + rows) * features),
        name="pick_rows",
    )(target, store, *([before] if last else []))


def sum_rows(term, target, picks, rows, features, before=None):
    lanes, length, _ = term.shape
    size = target.shape[1]
    each = size // lanes
    blocks = features // HD
    last = before is not None

    def kernel(target_ref, term_ref, *refs):
        out_ref, spread, flat = refs[-3:]
        row = lax.broadcasted_iota(I32, (rows, size), 0)
        one_hot = (row == target_ref[...]).astype(F32).astype(BF)
        spread[...] = term_ref[...].astype(F32)
        for lane in range(lanes):
            low = lane * each + picks // 8 * 8
            flat[low : (lane + 1) * each, :] = jnp.zeros(((lane + 1) * each - low, HD), F32)
        for block in range(blocks):
            cols = slice(block * HD, (block + 1) * HD)
            for lane in range(lanes):
                part = spread[lane, pl.ds(block, picks, stride=blocks), :]
                flat[lane * each : lane * each + picks, :] = part
            total = matmul(one_hot, flat[...].astype(BF))
            if last:
                total = total + refs[0][:, cols]
            out_ref[:, cols] = total.astype(out_ref.dtype)

    return pl.pallas_call(
        kernel,
        out_shape=jax.ShapeDtypeStruct((rows, features), BF if last else F32),
        scratch_shapes=[pltpu.VMEM((lanes, length, HD), F32), pltpu.VMEM((size, HD), F32)],
        compiler_params=PARAMS,
        cost_estimate=cost(2 * size * rows * features, 2 * (size + 2 * rows) * features),
        name="sum_rows",
    )(target, term, *([before] if last else []))


def move_back(moved):
    tokens, width = moved.shape[-2:]
    spans = tokens // SPAN

    def kernel(moved_ref, *outs):
        order = shift_matrix(1)
        blank = jnp.zeros((SPAN, width), BF)
        for which, out in enumerate(outs):
            for span in range(spans):
                at = span * SPAN
                before = moved_ref[which, at - SPAN : at] if span else blank
                pair = jnp.concatenate([before, moved_ref[which, at : at + SPAN]], 0)
                out[at : at + SPAN] = matmul(order, pair).astype(BF)

    return pl.pallas_call(
        kernel,
        out_shape=[jax.ShapeDtypeStruct((tokens, width), BF)] * 2,
        compiler_params=PARAMS,
        cost_estimate=cost(8 * tokens * SPAN * width, 8 * tokens * width),
        name="move_back",
    )(moved.reshape(2, tokens, width))


def two_heads(pair):
    blank = jnp.zeros((SPAN, HD), pair.dtype)
    upper = jnp.concatenate([pair[:, :HD], blank], 1)
    lower = jnp.concatenate([blank, pair[:, HD:]], 1)
    return jnp.concatenate([upper, lower], 0)


def score_spans(fetched, key_weight, value_weight, moved):
    lanes = fetched.shape[0]
    features, all_width = key_weight.shape
    groups, _, tokens, width = moved.shape
    spans = tokens // SPAN
    keys = lanes * NBRS
    count = keys // 8
    blocks = features // HD
    per_group = width // (2 * HD)
    pairs = all_width // (2 * HD)
    factor = HD ** (-0.5)

    def kernel(
        part_ref,
        wk_ref,
        wv_ref,
        moved_ref,
        k_ref,
        v_ref,
        w_ref,
        gp_ref,
        top_ref,
        stat_ref,
        rows_ref,
        spread,
        flat,
    ):
        @pl.when(pl.program_id(0) == 0)
        def _():
            spread[...] = part_ref[...].astype(F32)
            for block in range(blocks):
                for lane in range(lanes):
                    for nbr in range(NBRS):
                        to = lane * NBRS // 8 * 8 * spans + lane * NBRS % 8 + nbr
                        flat[pl.ds(to, spans, stride=8), :] = spread[
                            lane, pl.ds(nbr * blocks + block, spans, stride=NBRS * blocks), :
                        ]
                rows_ref[:, block * HD : (block + 1) * HD] = flat[...].astype(BF)

        rows = rows_ref[...]

        def project(weight):
            out = matmul(rows, weight).reshape(count, spans, 8, 2 * HD)
            return out.transpose(1, 0, 2, 3).reshape(spans, keys, 2 * HD).astype(BF)

        step = pl.program_id(0)
        scores, grads = [], []
        for side in range(SIDES):
            pair = SIDES * step + side
            cols = slice(side * 2 * HD, (side + 1) * 2 * HD)
            k_all = project(wk_ref[:, cols])
            v_all = project(wv_ref[:, cols])
            k_ref[pair] = k_all
            v_ref[pair] = v_all
            for span in range(spans):
                tok = slice(span * SPAN, (span + 1) * SPAN)
                queries = two_heads(moved_ref[0, 0, tok, cols])
                scores.append(matmul(k_all[span], queries, 1, 1) * factor)
                grads.append(matmul(v_all[span], two_heads(moved_ref[0, 1, tok, cols]), 1, 1))
        for side in range(SIDES):
            pair = SIDES * step + side
            for span in range(spans):
                score, grad = scores[side * spans + span], grads[side * spans + span]
                top = jnp.max(score, axis=0, keepdims=True)
                weights = jnp.exp(score - top)
                w_ref[pair, span] = weights
                gp_ref[pair, span] = grad
                mass = jnp.sum(weights, axis=0, keepdims=True)
                mean = jnp.sum(weights * grad, axis=0, keepdims=True) / mass
                top_ref[pair, pl.ds(span, 1), :] = top
                stat_ref[pl.ds(2 * spans * pair + span, 1), :] = top + jnp.log(mass)
                stat_ref[pl.ds(2 * spans * pair + spans + span, 1), :] = mean

    whole = pl.BlockSpec(fetched.shape, lambda i: (0, 0, 0))
    weight_spec = pl.BlockSpec((features, SIDES * 2 * HD), lambda i: (0, i))
    turns = per_group // SIDES
    token_spec = pl.BlockSpec(
        (1, 2, tokens, SIDES * 2 * HD), lambda i: (i // turns, 0, 0, i % turns)
    )
    held = pl.BlockSpec(memory_space=pltpu.VMEM)
    size = (2 * spans * pairs, 2 * SPAN)
    return pl.pallas_call(
        kernel,
        grid=(pairs // SIDES,),
        in_specs=[whole, weight_spec, weight_spec, token_spec],
        out_specs=[held] * 5 + [pl.BlockSpec(size, lambda i: (0, 0))],
        out_shape=[
            pltpu.VMEM((pairs, spans, keys, 2 * HD), BF),
            pltpu.VMEM((pairs, spans, keys, 2 * HD), BF),
            pltpu.VMEM((pairs, spans, keys, 2 * SPAN), F32),
            pltpu.VMEM((pairs, spans, keys, 2 * SPAN), F32),
            pltpu.VMEM((pairs, spans, 2 * SPAN), F32),
            jax.ShapeDtypeStruct(size, F32),
        ],
        scratch_shapes=[
            pltpu.VMEM((spans * keys, features), BF),
            pltpu.VMEM(fetched.shape, F32),
            pltpu.VMEM((spans * keys, HD), F32),
        ],
        compiler_params=SMALL,
        cost_estimate=cost(
            4 * spans * keys * (features + SPAN) * all_width,
            8 * spans * keys * all_width,
            spans * keys * SPAN * 2 * pairs,
        ),
        name="score_spans",
    )(fetched, key_weight, value_weight, moved)


def blend_spans(scored, stats, key_weight, value_weight, moved):
    scored = [pltpu.with_memory_space_constraint(array, pltpu.VMEM) for array in scored]
    features, all_width = key_weight.shape
    groups, _, tokens, width = moved.shape
    _, spans, keys, _ = scored[0].shape
    count = keys // 8
    lanes = keys // NBRS
    blocks = features // HD
    per_group = width // (2 * HD)
    pairs = all_width // (2 * HD)
    factor = HD ** (-0.5)
    devices = len(stats)

    def kernel(k_ref, v_ref, w_ref, gp_ref, top_ref, *refs):
        stat_refs = refs[:devices]
        wk_ref, wv_ref, moved_ref, out_ref, part_ref = refs[devices : devices + 5]
        total, spread = refs[devices + 5 :]
        step = pl.program_id(0)

        @pl.when(step == 0)
        def _():
            total[...] = jnp.zeros_like(total)

        def merge(pair):
            first = 2 * spans * pair
            logs = [ref[pl.ds(first, spans), :] for ref in stat_refs]
            means = [ref[pl.ds(first + spans, spans), :] for ref in stat_refs]
            most = logs[0]
            for log in logs[1:]:
                most = jnp.maximum(most, log)
            shares = [jnp.exp(log - most) for log in logs]
            whole = shares[0]
            inner = shares[0] * means[0]
            for share, mean in zip(shares[1:], means[1:]):
                whole = whole + share
                inner = inner + share * mean
            return jnp.exp(top_ref[pair] - most) / whole, inner / whole

        flat = (spans * keys, 2 * HD)
        terms = []
        for side in range(SIDES):
            pair = SIDES * step + side
            cols = slice(side * 2 * HD, (side + 1) * 2 * HD)
            scale, inner = merge(pair)
            gks, gvs = [], []
            for span in range(spans):
                tok = slice(span * SPAN, (span + 1) * SPAN)
                probs = w_ref[pair, span] * scale[span : span + 1]
                probs_b = probs.astype(BF)
                grad_scores = (
                    probs * (gp_ref[pair, span] - inner[span : span + 1]) * factor
                ).astype(BF)
                for which, out in enumerate(
                    (
                        matmul(probs_b, v_ref[pair, span], 0, 0),
                        matmul(grad_scores, k_ref[pair, span], 0, 0),
                    )
                ):
                    both = jnp.concatenate([out[:SPAN, :HD], out[SPAN:, HD:]], 1)
                    out_ref[0, which, tok, cols] = both.astype(BF)
                gk = matmul(grad_scores, two_heads(moved_ref[0, 0, tok, cols]))
                gv = matmul(probs_b, two_heads(moved_ref[0, 1, tok, cols]))
                gks.append(gk.reshape(count, 1, 8, 2 * HD))
                gvs.append(gv.reshape(count, 1, 8, 2 * HD))
            left = [
                jnp.concatenate(parts, 1).reshape(flat).astype(BF) for parts in (gks, gvs)
            ]
            right = [wk_ref[:, cols], wv_ref[:, cols]]
            terms.append(matmul(jnp.concatenate(left, 1), jnp.concatenate(right, 1), 1, 1))
        for block in range(blocks):
            at = slice(block * HD, (block + 1) * HD)
            term = terms[0][:, at]
            for other in terms[1:]:
                term = term + other[:, at]
            total[block] += term

        @pl.when(step == pairs // SIDES - 1)
        def _():
            spread[:, length - 8 :, :] = jnp.zeros((lanes, 8, HD), F32)
            for block in range(blocks):
                for lane in range(lanes):
                    for nbr in range(NBRS):
                        at = lane * NBRS // 8 * 8 * spans + lane * NBRS % 8 + nbr
                        to = pl.ds(nbr * blocks + block, spans, stride=NBRS * blocks)
                        spread[lane, to, :] = total[block, pl.ds(at, spans, stride=8), :]
            part_ref[...] = spread[...].astype(BF)

    weight_spec = pl.BlockSpec((features, SIDES * 2 * HD), lambda i: (0, i))
    turns = per_group // SIDES
    token_spec = pl.BlockSpec(
        (1, 2, tokens, SIDES * 2 * HD), lambda i: (i // turns, 0, 0, i % turns)
    )
    held = pl.BlockSpec(memory_space=pltpu.VMEM)
    stat_spec = pl.BlockSpec(stats[0].shape, lambda i: (0, 0))
    length = message_rows(spans * NBRS, blocks)
    result = (lanes, length, HD)
    return pl.pallas_call(
        kernel,
        grid=(pairs // SIDES,),
        in_specs=[held] * 5
        + [stat_spec] * devices
        + [weight_spec, weight_spec, token_spec],
        out_specs=[token_spec, pl.BlockSpec(result, lambda i: (0, 0, 0))],
        out_shape=[
            jax.ShapeDtypeStruct((groups, 2, tokens, width), BF),
            jax.ShapeDtypeStruct(result, BF),
        ],
        scratch_shapes=[
            pltpu.VMEM((blocks, spans * keys, HD), F32),
            pltpu.VMEM(result, F32),
        ],
        compiler_params=SMALL,
        cost_estimate=cost(
            4 * spans * keys * (features + 2 * SPAN) * all_width, 12 * spans * keys * all_width
        ),
        name="blend_spans",
    )(*scored, *stats, key_weight, value_weight, moved)


def after(value, *others):
    return lax.optimization_barrier((value, *others))[0]


def shards(query, d_attended, encoded, key_weight, value_weight, nbr_shard, nbr_row):
    lanes = lax.axis_size(("z", "y"))
    groups = lax.axis_size("x")
    c = lax.axis_index("c").astype(I32)
    spans, neighbours = nbr_shard.shape
    stored, quarter, features = encoded.shape
    rows = lanes * stored
    picks = spans * neighbours

    pieces, moved = prepare(encoded, nbr_shard, nbr_row, query, d_attended)
    store = lax.all_to_all(pieces, ("z", "y"), 0, 0, tiled=True)

    moved = lax.all_gather(moved, "x")

    def places(held):
        named = held[:, -SPARE : 2 * neighbours - SPARE, :stored].astype(I32).transpose(0, 2, 1)
        owner, row = named[..., :neighbours], named[..., neighbours:]
        place = owner // 2 * stored + row
        live = (jnp.arange(stored) < spans)[None, :, None]
        here = owner % 2 == c
        return [jnp.where(live & there, place, -1).reshape(-1) for there in (here, ~here)]

    others = send_ring(store, "c", 1)
    own_here, own_there = places(store)
    picked = pick_rows(store, own_here.reshape(-1, 1), picks)
    picked = pick_rows(others, own_there.reshape(-1, 1), picks, picked)
    fetched = lax.all_to_all(picked, ("z", "y"), 0, 0, tiled=True)

    *scored, stat = score_spans(fetched, key_weight, value_weight, moved)
    own_target = after(own_here, stat).reshape(1, -1)
    others_target = places(after(others, stat))[0].reshape(1, -1)
    stats = [send_ring(stat, "x", away) for away in range(groups)]
    stats[0] = after(stats[0], own_target, others_target)
    output, terms = blend_spans(scored, stats, key_weight, value_weight, moved)
    output = lax.psum_scatter(output, "x", scatter_dimension=0)

    home = lax.all_to_all(terms, ("z", "y"), 0, 0, tiled=True)
    sums = sum_rows(home, own_target, picks, rows, features)
    home = send_ring(home, "c", 1)
    sums = sum_rows(home, others_target, picks, rows, features, sums)
    returned = sums.reshape(lanes, stored, features)
    returned = lax.all_to_all(returned, ("z", "y"), 0, 0, tiled=True)
    attended, d_query = move_back(output)
    d_encoded = join_pieces(after(returned, attended))
    return (attended, d_query, d_encoded)


def solution(mesh):
    groups = mesh.devices.shape[1]
    fine = Mesh(mesh.devices.reshape(-1, 4, 2, groups), ("z", "y", "c", "x"))
    seq = ("z", "y", "c")
    placed = (
        P(seq, "x"),
        P(seq, "x"),
        P(seq, "x", None),
        P(),
        P(),
        P(seq, None),
        P(seq, None),
    )
    return jax.shard_map(
        shards,
        mesh=fine,
        in_specs=placed,
        out_specs=(P(seq, "x"), P(seq, "x"), P(seq, "x", None)),
        check_vma=False,
    )
```

```python
import jax
import jax.numpy as jnp
from jax import lax
from jax.experimental import pallas as pl
from jax.experimental.pallas import tpu as pltpu
from jax.sharding import Mesh, PartitionSpec as P

HD = 128
SPAN = 64
NBRS = 2
SPARE = 8
SIDES = 2
BF = jnp.bfloat16
F32 = jnp.float32
I32 = jnp.int32
PARAMS = pltpu.CompilerParams(vmem_limit_bytes=48 * 1024 * 1024)
SMALL = pltpu.CompilerParams(vmem_limit_bytes=48 * 1024 * 1024)


def matmul(left, right, left_dim=1, right_dim=0):
    return lax.dot_general(
        left, right, (((left_dim,), (right_dim,)), ((), ())), preferred_element_type=F32
    )


def cost(flops, bytes_accessed, transcendentals=0):
    return pl.CostEstimate(
        flops=int(flops), bytes_accessed=int(bytes_accessed), transcendentals=int(transcendentals)
    )


def send_ring(array, axis, step):
    size = lax.axis_size(axis)
    if step % size == 0:
        return array
    return lax.ppermute(array, axis, [(i, (i + step) % size) for i in range(size)])


def piece_matrix(stored, quarter):
    shape = (stored * quarter, stored * quarter)
    to = lax.broadcasted_iota(I32, shape, 0)
    source = lax.broadcasted_iota(I32, shape, 1)
    token = to % stored * quarter + to // stored
    return (source == token).astype(F32).astype(BF)


def shift_matrix(step):
    to = lax.broadcasted_iota(I32, (SPAN, 2 * SPAN), 0)
    source = lax.broadcasted_iota(I32, (SPAN, 2 * SPAN), 1)
    return (source == to + step).astype(F32).astype(BF)


def prepare(encoded, nbr_shard, nbr_row, query, d_attended):
    stored, quarter, features = encoded.shape
    size = stored * quarter
    spans, neighbours = nbr_shard.shape
    tokens, width = query.shape

    operands = [encoded.reshape(size, features), nbr_shard.T, nbr_row.T, query, d_attended]
    held = [pltpu.with_memory_space_constraint(array, pltpu.HBM) for array in operands]

    def kernel(*refs):
        sources = refs[:5]
        out_ref, moved_ref, names = refs[5:8]
        landed, sems = refs[8:13], refs[13]
        copies = [
            pltpu.make_async_copy(source, target, sems.at[i])
            for i, (source, target) in enumerate(zip(sources, landed))
        ]
        for copy in copies:
            copy.start()
        enc_ref, shard_ref, row_ref, q_ref, g_ref = landed
        names[...] = jnp.zeros_like(names)
        source_matrix = piece_matrix(stored, quarter)
        for copy in copies[:3]:
            copy.wait()
        names[:neighbours, :spans] = shard_ref[...].astype(F32)
        names[neighbours : 2 * neighbours, :spans] = row_ref[...].astype(F32)
        named = names[...]
        pieces = matmul(source_matrix, enc_ref[...])
        for token in range(quarter):
            piece = pieces[token * stored : (token + 1) * stored]
            parts = [piece[:, at : at + HD] for at in range(0, features, HD)]
            out_ref[token] = jnp.concatenate([*parts, named], 0).astype(BF)
        order = shift_matrix(SPAN - 1)
        for copy in copies[3:]:
            copy.wait()
        blank = jnp.zeros((SPAN, width), BF)
        for which, ref in enumerate((q_ref, g_ref)):
            for span in range(spans):
                at = span * SPAN
                after = ref[at + SPAN : at + 2 * SPAN] if span < spans - 1 else blank
                pair = jnp.concatenate([ref[at : at + SPAN], after], 0)
                moved_ref[which, at : at + SPAN] = matmul(order, pair).astype(BF)

    return pl.pallas_call(
        kernel,
        out_shape=[
            jax.ShapeDtypeStruct((quarter, features // HD * stored + SPARE, HD), BF),
            jax.ShapeDtypeStruct((2, tokens, width), BF),
        ],
        in_specs=[pl.BlockSpec(memory_space=pltpu.HBM)] * 5,
        scratch_shapes=[pltpu.VMEM((SPARE, HD), F32)]
        + [pltpu.VMEM(array.shape, array.dtype) for array in operands]
        + [pltpu.SemaphoreType.DMA((5,))],
        compiler_params=PARAMS,
        cost_estimate=cost(2 * size * size * features, 4 * size * features + 8 * tokens * width),
        name="prepare",
    )(*held)


def join_pieces(parts):
    quarter, stored, features = parts.shape
    size = stored * quarter

    def kernel(part_ref, out_ref):
        out_ref[...] = matmul(piece_matrix(stored, quarter), part_ref[...], 0, 0).astype(BF)

    joined = pl.pallas_call(
        kernel,
        out_shape=jax.ShapeDtypeStruct((size, features), BF),
        compiler_params=PARAMS,
        cost_estimate=cost(2 * size * size * features, 4 * size * features),
        name="join_pieces",
    )(parts.reshape(size, features))
    return joined.reshape(stored, quarter, features)


def message_rows(picks, blocks):
    return -(-picks * blocks // 8) * 8


def pick_rows(store, target, picks, before=None):
    lanes = store.shape[0]
    size = target.shape[0]
    each = size // lanes
    stored = each // NBRS
    rows = lanes * stored
    blocks = (store.shape[1] - SPARE) // stored
    features = blocks * HD
    length = message_rows(picks, blocks)

    def kernel(target_ref, store_ref, *refs):
        column = lax.broadcasted_iota(I32, (size, rows), 1)
        one_hot = (column == target_ref[...]).astype(F32).astype(BF)

        def part_of(block):
            part = store_ref[:, block * stored : (block + 1) * stored, :].reshape(rows, HD)
            return matmul(one_hot, part)

        if before is None:
            for block in range(blocks):
                refs[0][:, block * HD : (block + 1) * HD] = part_of(block).astype(BF)
            return
        before_ref, out_ref, spread = refs
        spread[:, length - 8 :, :] = jnp.zeros((lanes, 8, HD), F32)
        for block in range(blocks):
            cols = slice(block * HD, (block + 1) * HD)
            total = part_of(block) + before_ref[:, cols].astype(F32)
            for lane in range(lanes):
                part = total[lane * each : lane * each + picks]
                spread[lane, pl.ds(block, picks, stride=blocks), :] = part
        out_ref[...] = spread[...].astype(BF)

    last = before is not None
    shape = (lanes, length, HD) if last else (size, features)
    return pl.pallas_call(
        kernel,
        out_shape=jax.ShapeDtypeStruct(shape, BF),
        scratch_shapes=[pltpu.VMEM(shape, F32)] if last else [],
        compiler_params=PARAMS,
        cost_estimate=cost(2 * size * rows * features, 2 * (2 * size + rows) * features),
        name="pick_rows",
    )(target, store, *([before] if last else []))


def sum_rows(term, target, picks, rows, features, before=None):
    lanes, length, _ = term.shape
    size = target.shape[1]
    each = size // lanes
    blocks = features // HD
    last = before is not None

    def kernel(target_ref, term_ref, *refs):
        out_ref, spread, flat = refs[-3:]
        row = lax.broadcasted_iota(I32, (rows, size), 0)
        one_hot = (row == target_ref[...]).astype(F32).astype(BF)
        spread[...] = term_ref[...].astype(F32)
        for lane in range(lanes):
            low = lane * each + picks // 8 * 8
            flat[low : (lane + 1) * each, :] = jnp.zeros(((lane + 1) * each - low, HD), F32)
        for block in range(blocks):
            cols = slice(block * HD, (block + 1) * HD)
            for lane in range(lanes):
                part = spread[lane, pl.ds(block, picks, stride=blocks), :]
                flat[lane * each : lane * each + picks, :] = part
            total = matmul(one_hot, flat[...].astype(BF))
            if last:
                total = total + refs[0][:, cols]
            out_ref[:, cols] = total.astype(out_ref.dtype)

    return pl.pallas_call(
        kernel,
        out_shape=jax.ShapeDtypeStruct((rows, features), BF if last else F32),
        scratch_shapes=[pltpu.VMEM((lanes, length, HD), F32), pltpu.VMEM((size, HD), F32)],
        compiler_params=PARAMS,
        cost_estimate=cost(2 * size * rows * features, 2 * (size + 2 * rows) * features),
        name="sum_rows",
    )(target, term, *([before] if last else []))


def move_back(moved):
    tokens, width = moved.shape[-2:]
    spans = tokens // SPAN

    def kernel(moved_ref, *outs):
        order = shift_matrix(1)
        blank = jnp.zeros((SPAN, width), BF)
        for which, out in enumerate(outs):
            for span in range(spans):
                at = span * SPAN
                before = moved_ref[which, at - SPAN : at] if span else blank
                pair = jnp.concatenate([before, moved_ref[which, at : at + SPAN]], 0)
                out[at : at + SPAN] = matmul(order, pair).astype(BF)

    return pl.pallas_call(
        kernel,
        out_shape=[jax.ShapeDtypeStruct((tokens, width), BF)] * 2,
        compiler_params=PARAMS,
        cost_estimate=cost(8 * tokens * SPAN * width, 8 * tokens * width),
        name="move_back",
    )(moved.reshape(2, tokens, width))


def two_heads(pair):
    blank = jnp.zeros((SPAN, HD), pair.dtype)
    upper = jnp.concatenate([pair[:, :HD], blank], 1)
    lower = jnp.concatenate([blank, pair[:, HD:]], 1)
    return jnp.concatenate([upper, lower], 0)


def score_spans(fetched, key_weight, value_weight, moved):
    lanes = fetched.shape[0]
    features, all_width = key_weight.shape
    groups, _, tokens, width = moved.shape
    spans = tokens // SPAN
    keys = lanes * NBRS
    count = keys // 8
    blocks = features // HD
    per_group = width // (2 * HD)
    pairs = all_width // (2 * HD)
    factor = HD ** (-0.5)

    def kernel(
        part_ref,
        wk_ref,
        wv_ref,
        moved_ref,
        k_ref,
        v_ref,
        w_ref,
        gp_ref,
        top_ref,
        stat_ref,
        rows_ref,
        spread,
        flat,
    ):
        @pl.when(pl.program_id(0) == 0)
        def _():
            spread[...] = part_ref[...].astype(F32)
            for block in range(blocks):
                for lane in range(lanes):
                    for nbr in range(NBRS):
                        to = lane * NBRS // 8 * 8 * spans + lane * NBRS % 8 + nbr
                        flat[pl.ds(to, spans, stride=8), :] = spread[
                            lane, pl.ds(nbr * blocks + block, spans, stride=NBRS * blocks), :
                        ]
                rows_ref[:, block * HD : (block + 1) * HD] = flat[...].astype(BF)

        rows = rows_ref[...]

        def project(weight):
            out = matmul(rows, weight).reshape(count, spans, 8, 2 * HD)
            return out.transpose(1, 0, 2, 3).reshape(spans, keys, 2 * HD).astype(BF)

        step = pl.program_id(0)
        scores, grads = [], []
        for side in range(SIDES):
            pair = SIDES * step + side
            cols = slice(side * 2 * HD, (side + 1) * 2 * HD)
            k_all = project(wk_ref[:, cols])
            v_all = project(wv_ref[:, cols])
            k_ref[pair] = k_all
            v_ref[pair] = v_all
            for span in range(spans):
                tok = slice(span * SPAN, (span + 1) * SPAN)
                queries = two_heads(moved_ref[0, 0, tok, cols])
                scores.append(matmul(k_all[span], queries, 1, 1) * factor)
                grads.append(matmul(v_all[span], two_heads(moved_ref[0, 1, tok, cols]), 1, 1))
        for side in range(SIDES):
            pair = SIDES * step + side
            for span in range(spans):
                score, grad = scores[side * spans + span], grads[side * spans + span]
                top = jnp.max(score, axis=0, keepdims=True)
                weights = jnp.exp(score - top)
                w_ref[pair, span] = weights
                gp_ref[pair, span] = grad
                mass = jnp.sum(weights, axis=0, keepdims=True)
                mean = jnp.sum(weights * grad, axis=0, keepdims=True) / mass
                top_ref[pair, pl.ds(span, 1), :] = top
                stat_ref[pl.ds(2 * spans * pair + span, 1), :] = top + jnp.log(mass)
                stat_ref[pl.ds(2 * spans * pair + spans + span, 1), :] = mean

    whole = pl.BlockSpec(fetched.shape, lambda i: (0, 0, 0))
    weight_spec = pl.BlockSpec((features, SIDES * 2 * HD), lambda i: (0, i))
    turns = per_group // SIDES
    token_spec = pl.BlockSpec(
        (1, 2, tokens, SIDES * 2 * HD), lambda i: (i // turns, 0, 0, i % turns)
    )
    held = pl.BlockSpec(memory_space=pltpu.VMEM)
    size = (2 * spans * pairs, 2 * SPAN)
    return pl.pallas_call(
        kernel,
        grid=(pairs // SIDES,),
        in_specs=[whole, weight_spec, weight_spec, token_spec],
        out_specs=[held] * 5 + [pl.BlockSpec(size, lambda i: (0, 0))],
        out_shape=[
            pltpu.VMEM((pairs, spans, keys, 2 * HD), BF),
            pltpu.VMEM((pairs, spans, keys, 2 * HD), BF),
            pltpu.VMEM((pairs, spans, keys, 2 * SPAN), F32),
            pltpu.VMEM((pairs, spans, keys, 2 * SPAN), F32),
            pltpu.VMEM((pairs, spans, 2 * SPAN), F32),
            jax.ShapeDtypeStruct(size, F32),
        ],
        scratch_shapes=[
            pltpu.VMEM((spans * keys, features), BF),
            pltpu.VMEM(fetched.shape, F32),
            pltpu.VMEM((spans * keys, HD), F32),
        ],
        compiler_params=SMALL,
        cost_estimate=cost(
            4 * spans * keys * (features + SPAN) * all_width,
            8 * spans * keys * all_width,
            spans * keys * SPAN * 2 * pairs,
        ),
        name="score_spans",
    )(fetched, key_weight, value_weight, moved)


def blend_spans(scored, stats, key_weight, value_weight, moved):
    scored = [pltpu.with_memory_space_constraint(array, pltpu.VMEM) for array in scored]
    features, all_width = key_weight.shape
    groups, _, tokens, width = moved.shape
    _, spans, keys, _ = scored[0].shape
    count = keys // 8
    lanes = keys // NBRS
    blocks = features // HD
    per_group = width // (2 * HD)
    pairs = all_width // (2 * HD)
    factor = HD ** (-0.5)
    devices = len(stats)

    def kernel(k_ref, v_ref, w_ref, gp_ref, top_ref, *refs):
        stat_refs = refs[:devices]
        wk_ref, wv_ref, moved_ref, out_ref, part_ref = refs[devices : devices + 5]
        total, spread = refs[devices + 5 :]
        step = pl.program_id(0)

        @pl.when(step == 0)
        def _():
            total[...] = jnp.zeros_like(total)

        def merge(pair):
            first = 2 * spans * pair
            logs = [ref[pl.ds(first, spans), :] for ref in stat_refs]
            means = [ref[pl.ds(first + spans, spans), :] for ref in stat_refs]
            most = logs[0]
            for log in logs[1:]:
                most = jnp.maximum(most, log)
            shares = [jnp.exp(log - most) for log in logs]
            whole = shares[0]
            inner = shares[0] * means[0]
            for share, mean in zip(shares[1:], means[1:]):
                whole = whole + share
                inner = inner + share * mean
            return jnp.exp(top_ref[pair] - most) / whole, inner / whole

        flat = (spans * keys, 2 * HD)
        terms = []
        for side in range(SIDES):
            pair = SIDES * step + side
            cols = slice(side * 2 * HD, (side + 1) * 2 * HD)
            scale, inner = merge(pair)
            gks, gvs = [], []
            for span in range(spans):
                tok = slice(span * SPAN, (span + 1) * SPAN)
                probs = w_ref[pair, span] * scale[span : span + 1]
                probs_b = probs.astype(BF)
                grad_scores = (
                    probs * (gp_ref[pair, span] - inner[span : span + 1]) * factor
                ).astype(BF)
                for which, out in enumerate(
                    (
                        matmul(probs_b, v_ref[pair, span], 0, 0),
                        matmul(grad_scores, k_ref[pair, span], 0, 0),
                    )
                ):
                    both = jnp.concatenate([out[:SPAN, :HD], out[SPAN:, HD:]], 1)
                    out_ref[0, which, tok, cols] = both.astype(BF)
                gk = matmul(grad_scores, two_heads(moved_ref[0, 0, tok, cols]))
                gv = matmul(probs_b, two_heads(moved_ref[0, 1, tok, cols]))
                gks.append(gk.reshape(count, 1, 8, 2 * HD))
                gvs.append(gv.reshape(count, 1, 8, 2 * HD))
            left = [
                jnp.concatenate(parts, 1).reshape(flat).astype(BF) for parts in (gks, gvs)
            ]
            right = [wk_ref[:, cols], wv_ref[:, cols]]
            terms.append(matmul(jnp.concatenate(left, 1), jnp.concatenate(right, 1), 1, 1))
        for block in range(blocks):
            at = slice(block * HD, (block + 1) * HD)
            term = terms[0][:, at]
            for other in terms[1:]:
                term = term + other[:, at]
            total[block] += term

        @pl.when(step == pairs // SIDES - 1)
        def _():
            spread[:, length - 8 :, :] = jnp.zeros((lanes, 8, HD), F32)
            for block in range(blocks):
                for lane in range(lanes):
                    for nbr in range(NBRS):
                        at = lane * NBRS // 8 * 8 * spans + lane * NBRS % 8 + nbr
                        to = pl.ds(nbr * blocks + block, spans, stride=NBRS * blocks)
                        spread[lane, to, :] = total[block, pl.ds(at, spans, stride=8), :]
            part_ref[...] = spread[...].astype(BF)

    weight_spec = pl.BlockSpec((features, SIDES * 2 * HD), lambda i: (0, i))
    turns = per_group // SIDES
    token_spec = pl.BlockSpec(
        (1, 2, tokens, SIDES * 2 * HD), lambda i: (i // turns, 0, 0, i % turns)
    )
    held = pl.BlockSpec(memory_space=pltpu.VMEM)
    stat_spec = pl.BlockSpec(stats[0].shape, lambda i: (0, 0))
    length = message_rows(spans * NBRS, blocks)
    result = (lanes, length, HD)
    return pl.pallas_call(
        kernel,
        grid=(pairs // SIDES,),
        in_specs=[held] * 5
        + [stat_spec] * devices
        + [weight_spec, weight_spec, token_spec],
        out_specs=[token_spec, pl.BlockSpec(result, lambda i: (0, 0, 0))],
        out_shape=[
            jax.ShapeDtypeStruct((groups, 2, tokens, width), BF),
            jax.ShapeDtypeStruct(result, BF),
        ],
        scratch_shapes=[
            pltpu.VMEM((blocks, spans * keys, HD), F32),
            pltpu.VMEM(result, F32),
        ],
        compiler_params=SMALL,
        cost_estimate=cost(
            4 * spans * keys * (features + 2 * SPAN) * all_width, 12 * spans * keys * all_width
        ),
        name="blend_spans",
    )(*scored, *stats, key_weight, value_weight, moved)


def after(value, *others):
    return lax.optimization_barrier((value, *others))[0]


def shards(query, d_attended, encoded, key_weight, value_weight, nbr_shard, nbr_row):
    lanes = lax.axis_size(("z", "y"))
    groups = lax.axis_size("x")
    c = lax.axis_index("c").astype(I32)
    spans, neighbours = nbr_shard.shape
    stored, quarter, features = encoded.shape
    rows = lanes * stored
    picks = spans * neighbours

    pieces, moved = prepare(encoded, nbr_shard, nbr_row, query, d_attended)
    store = lax.all_to_all(pieces, ("z", "y"), 0, 0, tiled=True)

    moved = lax.all_gather(moved, "x")

    def places(held):
        named = held[:, -SPARE : 2 * neighbours - SPARE, :stored].astype(I32).transpose(0, 2, 1)
        owner, row = named[..., :neighbours], named[..., neighbours:]
        place = owner // 2 * stored + row
        live = (jnp.arange(stored) < spans)[None, :, None]
        here = owner % 2 == c
        return [jnp.where(live & there, place, -1).reshape(-1) for there in (here, ~here)]

    others = send_ring(store, "c", 1)
    own_here, own_there = places(store)
    picked = pick_rows(store, own_here.reshape(-1, 1), picks)
    picked = pick_rows(others, own_there.reshape(-1, 1), picks, picked)
    fetched = lax.all_to_all(picked, ("z", "y"), 0, 0, tiled=True)

    *scored, stat = score_spans(fetched, key_weight, value_weight, moved)
    own_target = after(own_here, stat).reshape(1, -1)
    others_target = places(after(others, stat))[0].reshape(1, -1)
    stats = [send_ring(stat, "x", away) for away in range(groups)]
    stats[0] = after(stats[0], own_target, others_target)
    output, terms = blend_spans(scored, stats, key_weight, value_weight, moved)
    output = lax.psum_scatter(output, "x", scatter_dimension=0)

    home = lax.all_to_all(terms, ("z", "y"), 0, 0, tiled=True)
    sums = sum_rows(home, own_target, picks, rows, features)
    home = send_ring(home, "c", 1)
    sums = sum_rows(home, others_target, picks, rows, features, sums)
    returned = sums.reshape(lanes, stored, features)
    returned = lax.all_to_all(returned, ("z", "y"), 0, 0, tiled=True)
    attended, d_query = move_back(output)
    d_encoded = join_pieces(after(returned, attended))
    return (attended, d_query, d_encoded)


def solution(mesh):
    groups = mesh.devices.shape[1]
    fine = Mesh(mesh.devices.reshape(-1, 4, 2, groups), ("z", "y", "c", "x"))
    seq = ("z", "y", "c")
    placed = (
        P(seq, "x"),
        P(seq, "x"),
        P(seq, "x", None),
        P(),
        P(),
        P(seq, None),
        P(seq, None),
    )
    return jax.shard_map(
        shards,
        mesh=fine,
        in_specs=placed,
        out_specs=(P(seq, "x"), P(seq, "x"), P(seq, "x", None)),
        check_vma=False,
    )
```

```python
import jax
import jax.numpy as jnp
from jax import lax
from jax.experimental import pallas as pl
from jax.experimental.pallas import tpu as pltpu
from jax.sharding import Mesh, PartitionSpec as P

HD = 128
SPAN = 64
NBRS = 2
SPARE = 8
SIDES = 2
BF = jnp.bfloat16
F32 = jnp.float32
I32 = jnp.int32
PARAMS = pltpu.CompilerParams(vmem_limit_bytes=48 * 1024 * 1024)
SMALL = pltpu.CompilerParams(vmem_limit_bytes=48 * 1024 * 1024)


def matmul(left, right, left_dim=1, right_dim=0):
    return lax.dot_general(
        left, right, (((left_dim,), (right_dim,)), ((), ())), preferred_element_type=F32
    )


def cost(flops, bytes_accessed, transcendentals=0):
    return pl.CostEstimate(
        flops=int(flops), bytes_accessed=int(bytes_accessed), transcendentals=int(transcendentals)
    )


def send_ring(array, axis, step):
    size = lax.axis_size(axis)
    if step % size == 0:
        return array
    return lax.ppermute(array, axis, [(i, (i + step) % size) for i in range(size)])


def piece_matrix(stored, quarter):
    shape = (stored * quarter, stored * quarter)
    to = lax.broadcasted_iota(I32, shape, 0)
    source = lax.broadcasted_iota(I32, shape, 1)
    token = to % stored * quarter + to // stored
    return (source == token).astype(F32).astype(BF)


def shift_matrix(step):
    to = lax.broadcasted_iota(I32, (SPAN, 2 * SPAN), 0)
    source = lax.broadcasted_iota(I32, (SPAN, 2 * SPAN), 1)
    return (source == to + step).astype(F32).astype(BF)


def prepare(encoded, nbr_shard, nbr_row, query, d_attended):
    stored, quarter, features = encoded.shape
    size = stored * quarter
    spans, neighbours = nbr_shard.shape
    tokens, width = query.shape

    operands = [encoded.reshape(size, features), nbr_shard.T, nbr_row.T, query, d_attended]
    held = [pltpu.with_memory_space_constraint(array, pltpu.HBM) for array in operands]

    def kernel(*refs):
        sources = refs[:5]
        out_ref, moved_ref, names = refs[5:8]
        landed, sems = refs[8:13], refs[13]
        copies = [
            pltpu.make_async_copy(source, target, sems.at[i])
            for i, (source, target) in enumerate(zip(sources, landed))
        ]
        for copy in copies:
            copy.start()
        enc_ref, shard_ref, row_ref, q_ref, g_ref = landed
        names[...] = jnp.zeros_like(names)
        source_matrix = piece_matrix(stored, quarter)
        for copy in copies[:3]:
            copy.wait()
        names[:neighbours, :spans] = shard_ref[...].astype(F32)
        names[neighbours : 2 * neighbours, :spans] = row_ref[...].astype(F32)
        named = names[...]
        pieces = matmul(source_matrix, enc_ref[...])
        for token in range(quarter):
            piece = pieces[token * stored : (token + 1) * stored]
            parts = [piece[:, at : at + HD] for at in range(0, features, HD)]
            out_ref[token] = jnp.concatenate([*parts, named], 0).astype(BF)
        order = shift_matrix(SPAN - 1)
        for copy in copies[3:]:
            copy.wait()
        blank = jnp.zeros((SPAN, width), BF)
        for which, ref in enumerate((q_ref, g_ref)):
            for span in range(spans):
                at = span * SPAN
                after = ref[at + SPAN : at + 2 * SPAN] if span < spans - 1 else blank
                pair = jnp.concatenate([ref[at : at + SPAN], after], 0)
                moved_ref[which, at : at + SPAN] = matmul(order, pair).astype(BF)

    return pl.pallas_call(
        kernel,
        out_shape=[
            jax.ShapeDtypeStruct((quarter, features // HD * stored + SPARE, HD), BF),
            jax.ShapeDtypeStruct((2, tokens, width), BF),
        ],
        in_specs=[pl.BlockSpec(memory_space=pltpu.HBM)] * 5,
        scratch_shapes=[pltpu.VMEM((SPARE, HD), F32)]
        + [pltpu.VMEM(array.shape, array.dtype) for array in operands]
        + [pltpu.SemaphoreType.DMA((5,))],
        compiler_params=PARAMS,
        cost_estimate=cost(2 * size * size * features, 4 * size * features + 8 * tokens * width),
        name="prepare",
    )(*held)


def join_pieces(parts):
    quarter, stored, features = parts.shape
    size = stored * quarter

    def kernel(part_ref, out_ref):
        out_ref[...] = matmul(piece_matrix(stored, quarter), part_ref[...], 0, 0).astype(BF)

    joined = pl.pallas_call(
        kernel,
        out_shape=jax.ShapeDtypeStruct((size, features), BF),
        compiler_params=PARAMS,
        cost_estimate=cost(2 * size * size * features, 4 * size * features),
        name="join_pieces",
    )(parts.reshape(size, features))
    return joined.reshape(stored, quarter, features)


def message_rows(picks, blocks):
    return -(-picks * blocks // 8) * 8


def pick_rows(store, target, picks, before=None):
    lanes = store.shape[0]
    size = target.shape[0]
    each = size // lanes
    stored = each // NBRS
    rows = lanes * stored
    blocks = (store.shape[1] - SPARE) // stored
    features = blocks * HD
    length = message_rows(picks, blocks)

    def kernel(target_ref, store_ref, *refs):
        column = lax.broadcasted_iota(I32, (size, rows), 1)
        one_hot = (column == target_ref[...]).astype(F32).astype(BF)

        def part_of(block):
            part = store_ref[:, block * stored : (block + 1) * stored, :].reshape(rows, HD)
            return matmul(one_hot, part)

        if before is None:
            for block in range(blocks):
                refs[0][:, block * HD : (block + 1) * HD] = part_of(block).astype(BF)
            return
        before_ref, out_ref, spread = refs
        spread[:, length - 8 :, :] = jnp.zeros((lanes, 8, HD), F32)
        for block in range(blocks):
            cols = slice(block * HD, (block + 1) * HD)
            total = part_of(block) + before_ref[:, cols].astype(F32)
            for lane in range(lanes):
                part = total[lane * each : lane * each + picks]
                spread[lane, pl.ds(block, picks, stride=blocks), :] = part
        out_ref[...] = spread[...].astype(BF)

    last = before is not None
    shape = (lanes, length, HD) if last else (size, features)
    return pl.pallas_call(
        kernel,
        out_shape=jax.ShapeDtypeStruct(shape, BF),
        scratch_shapes=[pltpu.VMEM(shape, F32)] if last else [],
        compiler_params=PARAMS,
        cost_estimate=cost(2 * size * rows * features, 2 * (2 * size + rows) * features),
        name="pick_rows",
    )(target, store, *([before] if last else []))


def sum_rows(term, target, picks, rows, features, before=None):
    lanes, length, _ = term.shape
    size = target.shape[1]
    each = size // lanes
    blocks = features // HD
    last = before is not None

    def kernel(target_ref, term_ref, *refs):
        out_ref, spread, flat = refs[-3:]
        row = lax.broadcasted_iota(I32, (rows, size), 0)
        one_hot = (row == target_ref[...]).astype(F32).astype(BF)
        spread[...] = term_ref[...].astype(F32)
        for lane in range(lanes):
            low = lane * each + picks // 8 * 8
            flat[low : (lane + 1) * each, :] = jnp.zeros(((lane + 1) * each - low, HD), F32)
        for block in range(blocks):
            cols = slice(block * HD, (block + 1) * HD)
            for lane in range(lanes):
                part = spread[lane, pl.ds(block, picks, stride=blocks), :]
                flat[lane * each : lane * each + picks, :] = part
            total = matmul(one_hot, flat[...].astype(BF))
            if last:
                total = total + refs[0][:, cols]
            out_ref[:, cols] = total.astype(out_ref.dtype)

    return pl.pallas_call(
        kernel,
        out_shape=jax.ShapeDtypeStruct((rows, features), BF if last else F32),
        scratch_shapes=[pltpu.VMEM((lanes, length, HD), F32), pltpu.VMEM((size, HD), F32)],
        compiler_params=PARAMS,
        cost_estimate=cost(2 * size * rows * features, 2 * (size + 2 * rows) * features),
        name="sum_rows",
    )(target, term, *([before] if last else []))


def move_back(moved):
    tokens, width = moved.shape[-2:]
    spans = tokens // SPAN

    def kernel(moved_ref, *outs):
        order = shift_matrix(1)
        blank = jnp.zeros((SPAN, width), BF)
        for which, out in enumerate(outs):
            for span in range(spans):
                at = span * SPAN
                before = moved_ref[which, at - SPAN : at] if span else blank
                pair = jnp.concatenate([before, moved_ref[which, at : at + SPAN]], 0)
                out[at : at + SPAN] = matmul(order, pair).astype(BF)

    return pl.pallas_call(
        kernel,
        out_shape=[jax.ShapeDtypeStruct((tokens, width), BF)] * 2,
        compiler_params=PARAMS,
        cost_estimate=cost(8 * tokens * SPAN * width, 8 * tokens * width),
        name="move_back",
    )(moved.reshape(2, tokens, width))


def two_heads(pair):
    blank = jnp.zeros((SPAN, HD), pair.dtype)
    upper = jnp.concatenate([pair[:, :HD], blank], 1)
    lower = jnp.concatenate([blank, pair[:, HD:]], 1)
    return jnp.concatenate([upper, lower], 0)


def score_spans(fetched, key_weight, value_weight, moved):
    lanes = fetched.shape[0]
    features, all_width = key_weight.shape
    groups, _, tokens, width = moved.shape
    spans = tokens // SPAN
    keys = lanes * NBRS
    count = keys // 8
    blocks = features // HD
    per_group = width // (2 * HD)
    pairs = all_width // (2 * HD)
    factor = HD ** (-0.5)

    def kernel(
        part_ref,
        wk_ref,
        wv_ref,
        moved_ref,
        k_ref,
        v_ref,
        w_ref,
        gp_ref,
        top_ref,
        stat_ref,
        rows_ref,
        spread,
        flat,
    ):
        @pl.when(pl.program_id(0) == 0)
        def _():
            spread[...] = part_ref[...].astype(F32)
            for block in range(blocks):
                for lane in range(lanes):
                    for nbr in range(NBRS):
                        to = lane * NBRS // 8 * 8 * spans + lane * NBRS % 8 + nbr
                        flat[pl.ds(to, spans, stride=8), :] = spread[
                            lane, pl.ds(nbr * blocks + block, spans, stride=NBRS * blocks), :
                        ]
                rows_ref[:, block * HD : (block + 1) * HD] = flat[...].astype(BF)

        rows = rows_ref[...]

        def project(weight):
            out = matmul(rows, weight).reshape(count, spans, 8, 2 * HD)
            return out.transpose(1, 0, 2, 3).reshape(spans, keys, 2 * HD).astype(BF)

        step = pl.program_id(0)
        scores, grads = [], []
        for side in range(SIDES):
            pair = SIDES * step + side
            cols = slice(side * 2 * HD, (side + 1) * 2 * HD)
            k_all = project(wk_ref[:, cols])
            v_all = project(wv_ref[:, cols])
            k_ref[pair] = k_all
            v_ref[pair] = v_all
            for span in range(spans):
                tok = slice(span * SPAN, (span + 1) * SPAN)
                queries = two_heads(moved_ref[0, 0, tok, cols])
                scores.append(matmul(k_all[span], queries, 1, 1) * factor)
                grads.append(matmul(v_all[span], two_heads(moved_ref[0, 1, tok, cols]), 1, 1))
        for side in range(SIDES):
            pair = SIDES * step + side
            for span in range(spans):
                score, grad = scores[side * spans + span], grads[side * spans + span]
                top = jnp.max(score, axis=0, keepdims=True)
                weights = jnp.exp(score - top)
                w_ref[pair, span] = weights
                gp_ref[pair, span] = grad
                mass = jnp.sum(weights, axis=0, keepdims=True)
                mean = jnp.sum(weights * grad, axis=0, keepdims=True) / mass
                top_ref[pair, pl.ds(span, 1), :] = top
                stat_ref[pl.ds(2 * spans * pair + span, 1), :] = top + jnp.log(mass)
                stat_ref[pl.ds(2 * spans * pair + spans + span, 1), :] = mean

    whole = pl.BlockSpec(fetched.shape, lambda i: (0, 0, 0))
    weight_spec = pl.BlockSpec((features, SIDES * 2 * HD), lambda i: (0, i))
    turns = per_group // SIDES
    token_spec = pl.BlockSpec(
        (1, 2, tokens, SIDES * 2 * HD), lambda i: (i // turns, 0, 0, i % turns)
    )
    held = pl.BlockSpec(memory_space=pltpu.VMEM)
    size = (2 * spans * pairs, 2 * SPAN)
    return pl.pallas_call(
        kernel,
        grid=(pairs // SIDES,),
        in_specs=[whole, weight_spec, weight_spec, token_spec],
        out_specs=[held] * 5 + [pl.BlockSpec(size, lambda i: (0, 0))],
        out_shape=[
            pltpu.VMEM((pairs, spans, keys, 2 * HD), BF),
            pltpu.VMEM((pairs, spans, keys, 2 * HD), BF),
            pltpu.VMEM((pairs, spans, keys, 2 * SPAN), F32),
            pltpu.VMEM((pairs, spans, keys, 2 * SPAN), F32),
            pltpu.VMEM((pairs, spans, 2 * SPAN), F32),
            jax.ShapeDtypeStruct(size, F32),
        ],
        scratch_shapes=[
            pltpu.VMEM((spans * keys, features), BF),
            pltpu.VMEM(fetched.shape, F32),
            pltpu.VMEM((spans * keys, HD), F32),
        ],
        compiler_params=SMALL,
        cost_estimate=cost(
            4 * spans * keys * (features + SPAN) * all_width,
            8 * spans * keys * all_width,
            spans * keys * SPAN * 2 * pairs,
        ),
        name="score_spans",
    )(fetched, key_weight, value_weight, moved)


def blend_spans(scored, stats, key_weight, value_weight, moved):
    scored = [pltpu.with_memory_space_constraint(array, pltpu.VMEM) for array in scored]
    features, all_width = key_weight.shape
    groups, _, tokens, width = moved.shape
    _, spans, keys, _ = scored[0].shape
    count = keys // 8
    lanes = keys // NBRS
    blocks = features // HD
    per_group = width // (2 * HD)
    pairs = all_width // (2 * HD)
    factor = HD ** (-0.5)
    devices = len(stats)

    def kernel(k_ref, v_ref, w_ref, gp_ref, top_ref, *refs):
        stat_refs = refs[:devices]
        wk_ref, wv_ref, moved_ref, out_ref, part_ref = refs[devices : devices + 5]
        total, spread = refs[devices + 5 :]
        step = pl.program_id(0)

        @pl.when(step == 0)
        def _():
            total[...] = jnp.zeros_like(total)

        def merge(pair):
            first = 2 * spans * pair
            logs = [ref[pl.ds(first, spans), :] for ref in stat_refs]
            means = [ref[pl.ds(first + spans, spans), :] for ref in stat_refs]
            most = logs[0]
            for log in logs[1:]:
                most = jnp.maximum(most, log)
            shares = [jnp.exp(log - most) for log in logs]
            whole = shares[0]
            inner = shares[0] * means[0]
            for share, mean in zip(shares[1:], means[1:]):
                whole = whole + share
                inner = inner + share * mean
            return jnp.exp(top_ref[pair] - most) / whole, inner / whole

        flat = (spans * keys, 2 * HD)
        terms = []
        for side in range(SIDES):
            pair = SIDES * step + side
            cols = slice(side * 2 * HD, (side + 1) * 2 * HD)
            scale, inner = merge(pair)
            gks, gvs = [], []
            for span in range(spans):
                tok = slice(span * SPAN, (span + 1) * SPAN)
                probs = w_ref[pair, span] * scale[span : span + 1]
                probs_b = probs.astype(BF)
                grad_scores = (
                    probs * (gp_ref[pair, span] - inner[span : span + 1]) * factor
                ).astype(BF)
                for which, out in enumerate(
                    (
                        matmul(probs_b, v_ref[pair, span], 0, 0),
                        matmul(grad_scores, k_ref[pair, span], 0, 0),
                    )
                ):
                    both = jnp.concatenate([out[:SPAN, :HD], out[SPAN:, HD:]], 1)
                    out_ref[0, which, tok, cols] = both.astype(BF)
                gk = matmul(grad_scores, two_heads(moved_ref[0, 0, tok, cols]))
                gv = matmul(probs_b, two_heads(moved_ref[0, 1, tok, cols]))
                gks.append(gk.reshape(count, 1, 8, 2 * HD))
                gvs.append(gv.reshape(count, 1, 8, 2 * HD))
            left = [
                jnp.concatenate(parts, 1).reshape(flat).astype(BF) for parts in (gks, gvs)
            ]
            right = [wk_ref[:, cols], wv_ref[:, cols]]
            terms.append(matmul(jnp.concatenate(left, 1), jnp.concatenate(right, 1), 1, 1))
        for block in range(blocks):
            at = slice(block * HD, (block + 1) * HD)
            term = terms[0][:, at]
            for other in terms[1:]:
                term = term + other[:, at]
            total[block] += term

        @pl.when(step == pairs // SIDES - 1)
        def _():
            spread[:, length - 8 :, :] = jnp.zeros((lanes, 8, HD), F32)
            for block in range(blocks):
                for lane in range(lanes):
                    for nbr in range(NBRS):
                        at = lane * NBRS // 8 * 8 * spans + lane * NBRS % 8 + nbr
                        to = pl.ds(nbr * blocks + block, spans, stride=NBRS * blocks)
                        spread[lane, to, :] = total[block, pl.ds(at, spans, stride=8), :]
            part_ref[...] = spread[...].astype(BF)

    weight_spec = pl.BlockSpec((features, SIDES * 2 * HD), lambda i: (0, i))
    turns = per_group // SIDES
    token_spec = pl.BlockSpec(
        (1, 2, tokens, SIDES * 2 * HD), lambda i: (i // turns, 0, 0, i % turns)
    )
    held = pl.BlockSpec(memory_space=pltpu.VMEM)
    stat_spec = pl.BlockSpec(stats[0].shape, lambda i: (0, 0))
    length = message_rows(spans * NBRS, blocks)
    result = (lanes, length, HD)
    return pl.pallas_call(
        kernel,
        grid=(pairs // SIDES,),
        in_specs=[held] * 5
        + [stat_spec] * devices
        + [weight_spec, weight_spec, token_spec],
        out_specs=[token_spec, pl.BlockSpec(result, lambda i: (0, 0, 0))],
        out_shape=[
            jax.ShapeDtypeStruct((groups, 2, tokens, width), BF),
            jax.ShapeDtypeStruct(result, BF),
        ],
        scratch_shapes=[
            pltpu.VMEM((blocks, spans * keys, HD), F32),
            pltpu.VMEM(result, F32),
        ],
        compiler_params=SMALL,
        cost_estimate=cost(
            4 * spans * keys * (features + 2 * SPAN) * all_width, 12 * spans * keys * all_width
        ),
        name="blend_spans",
    )(*scored, *stats, key_weight, value_weight, moved)


def after(value, *others):
    return lax.optimization_barrier((value, *others))[0]


def shards(query, d_attended, encoded, key_weight, value_weight, nbr_shard, nbr_row):
    lanes = lax.axis_size(("z", "y"))
    groups = lax.axis_size("x")
    c = lax.axis_index("c").astype(I32)
    spans, neighbours = nbr_shard.shape
    stored, quarter, features = encoded.shape
    rows = lanes * stored
    picks = spans * neighbours

    pieces, moved = prepare(encoded, nbr_shard, nbr_row, query, d_attended)
    store = lax.all_to_all(pieces, ("z", "y"), 0, 0, tiled=True)

    moved = lax.all_gather(moved, "x")

    def places(held):
        named = held[:, -SPARE : 2 * neighbours - SPARE, :stored].astype(I32).transpose(0, 2, 1)
        owner, row = named[..., :neighbours], named[..., neighbours:]
        place = owner // 2 * stored + row
        live = (jnp.arange(stored) < spans)[None, :, None]
        here = owner % 2 == c
        return [jnp.where(live & there, place, -1).reshape(-1) for there in (here, ~here)]

    others = send_ring(store, "c", 1)
    own_here, own_there = places(store)
    picked = pick_rows(store, own_here.reshape(-1, 1), picks)
    picked = pick_rows(others, own_there.reshape(-1, 1), picks, picked)
    fetched = lax.all_to_all(picked, ("z", "y"), 0, 0, tiled=True)

    *scored, stat = score_spans(fetched, key_weight, value_weight, moved)
    stats = [send_ring(stat, "x", away) for away in range(groups)]
    output, terms = blend_spans(scored, stats, key_weight, value_weight, moved)
    output = lax.psum_scatter(output, "x", scatter_dimension=0)

    home = lax.all_to_all(terms, ("z", "y"), 0, 0, tiled=True)
    others_here = places(after(others, terms))[0]
    sums = sum_rows(home, own_here.reshape(1, -1), picks, rows, features)
    home = send_ring(home, "c", 1)
    sums = sum_rows(home, others_here.reshape(1, -1), picks, rows, features, sums)
    returned = sums.reshape(lanes, stored, features)
    returned = lax.all_to_all(returned, ("z", "y"), 0, 0, tiled=True)
    attended, d_query = move_back(output)
    d_encoded = join_pieces(after(returned, attended))
    return (attended, d_query, d_encoded)


def solution(mesh):
    groups = mesh.devices.shape[1]
    fine = Mesh(mesh.devices.reshape(-1, 4, 2, groups), ("z", "y", "c", "x"))
    seq = ("z", "y", "c")
    placed = (
        P(seq, "x"),
        P(seq, "x"),
        P(seq, "x", None),
        P(),
        P(),
        P(seq, None),
        P(seq, None),
    )
    return jax.shard_map(
        shards,
        mesh=fine,
        in_specs=placed,
        out_specs=(P(seq, "x"), P(seq, "x"), P(seq, "x", None)),
        check_vma=False,
    )
```
